32 devices in a mesh: seq: 4 (over y, x), batch: 8 (over z, core).
Axes of the slice: x: 2, y: 2, z: 4, core: 2. Of those that a mesh axis runs over, the one named last changes fastest.
Arguments:
- tokens: bfloat16 [2, 32, 1024, 1280], P(None, 'batch', 'seq'), may hold values from -8 to 8
- lengths: int32 [2, 32], P(None, 'batch'), may hold values from 30 to 1024, as said below
- first_gain: bfloat16 [1280], P('batch'), may hold values from 0.5 to 1.5
- first_shift: bfloat16 [1280], P('batch'), may hold values from -1.25 to 1.25
- down_weight: bfloat16 [1280, 640], P('seq', 'batch'), may hold values from -0.15625 to 0.15625
- down_bias: bfloat16 [640], P('batch'), may hold values from -1.25 to 1.25
- middle_gain: bfloat16 [640], P('batch'), may hold values from 0.5 to 1.5
- middle_shift: bfloat16 [640], P('batch'), may hold values from -1.25 to 1.25
- conv_weight: bfloat16 [5, 640, 640], P(None, 'seq', 'batch'), may hold values from -0.109375 to 0.109375
- conv_bias: bfloat16 [640], P('batch'), may hold values from -1.25 to 1.25
- final_gain: bfloat16 [640], P('batch'), may hold values from 0.5 to 1.5
- final_shift: bfloat16 [640], P('batch'), may hold values from -1.25 to 1.25
- up_weight: bfloat16 [640, 1280], P('seq', 'batch'), may hold values from -0.25 to 0.25
- up_bias: bfloat16 [1280], P('batch'), may hold values from -1.25 to 1.25
- cotangent: bfloat16 [2, 32, 1024, 1280], P(None, 'batch', 'seq'), may hold values from -8 to 8
Outputs:
- block_output: bfloat16 [2, 32, 1024, 1280], P(None, 'batch', 'seq')
- tokens_grad: bfloat16 [2, 32, 1024, 1280], P(None, 'batch', 'seq')
- first_gain_grad: float32 [1280], P('batch')
- first_shift_grad: float32 [1280], P('batch')
- down_weight_grad: float32 [1280, 640], P('seq', 'batch')
- down_bias_grad: float32 [640], P('batch')
- middle_gain_grad: float32 [640], P('batch')
- middle_shift_grad: float32 [640], P('batch')
- conv_weight_grad: float32 [5, 640, 640], P(None, 'seq', 'batch')
- conv_bias_grad: float32 [640], P('batch')
- final_gain_grad: float32 [640], P('batch')
- final_shift_grad: float32 [640], P('batch')
- up_weight_grad: float32 [640, 1280], P('seq', 'batch')
- up_bias_grad: float32 [1280], P('batch')
The draws below stay inside these ranges and needn't reach their ends.
Inputs may be any that keep to these rules, and one draw needn't show every extreme that they name: `lengths`: short proteins are more common than long ones. In every micro-batch, among proteins 4 * i to 4 * (i + 1) - 1 for each i, exactly one, at a place drawn from the seed, has length 1024.
All inputs are finite; a program needn't handle non-finite values.
Results may differ from the reference program's by a relative error of at most 0.0072.
Values may be sent and summed in bfloat16 or wider, within the bound.
No kernel may reach another device: no remote copies, remote signals or barrier semaphores. Data moves between devices by JAX's collectives and lax.ppermute only.
A program may use at most 192 MiB of HBM per device.

```python
import math
import jax
import jax.numpy as jnp
from jax import lax

D = 1280
H = 640
KERNEL = 5
DILATION = 16
LENGTH = 1024
MB = 2
PROT_DEV = 4
PROTEINS = 32


def draw_lengths(key, part):
    key = jax.random.fold_in(key, 7)
    key_first, key_second, key_place = jax.random.split(key, 3)
    first_draw = jax.random.randint(key_first, (MB, PROTEINS), 30, LENGTH + 1)
    second_draw = jax.random.randint(key_second, (MB, PROTEINS), 30, LENGTH + 1)
    shorter = jnp.minimum(first_draw, second_draw)
    chosen = jax.random.randint(key_place, (MB, PROTEINS // PROT_DEV), 0, PROT_DEV)
    repeated = jnp.repeat(chosen, PROT_DEV, axis=1)
    within = jnp.arange(PROTEINS, dtype=jnp.int32) % PROT_DEV
    full_length = within[None, :] == repeated
    return jnp.where(full_length, LENGTH, shorter).astype(jnp.int32)


def strengthened(entries, key, source, target, parts, factor):
    def block_of(dim):
        return (jnp.arange(entries.shape[dim]) // (entries.shape[dim] // parts)).reshape((-1,) + (1,) * (entries.ndim - 1 - dim))

    first = jax.random.permutation(key, parts)[block_of(target)]
    other_side = (block_of(target) + parts // 2) % parts
    return jnp.where((block_of(source) == first) | (block_of(source) == other_side), factor * entries, entries)


def levels(key, shape, cuts, least, largest):
    loudness = 1.0
    for dim, shards_of in cuts:
        heights = jax.random.uniform(jax.random.fold_in(jax.random.fold_in(key, 6), dim), (shards_of,), jnp.float32, least / len(cuts), largest / len(cuts))
        loudness = loudness * jnp.repeat(jnp.exp(heights), shape[dim] // shards_of).reshape((-1,) + (1,) * (len(shape) - 1 - dim))
    return loudness


def gaussian(own_key, extent, scale, limit, pieces=(), kind=jnp.bfloat16):
    entries = scale * jax.random.normal(own_key, extent, jnp.float32)
    if pieces:
        entries = entries * levels(own_key, extent, pieces, -0.22, 0.18)
    return jnp.clip(entries, -limit, limit).astype(kind)


def gaussian_with(rng, shape, scale, reach, cuts, heavy, kind=jnp.bfloat16):
    array = scale * jax.random.normal(rng, shape, jnp.float32)
    if cuts:
        array = array * levels(rng, shape, cuts, -0.22, 0.18)
    return jnp.clip(strengthened(array, jax.random.fold_in(rng, 3), *heavy), -reach, reach).astype(kind)


def setup_inputs(seed: int = 0) -> dict:
    streams_of = jax.random.split(jax.random.key(seed), 16)
    tokens = gaussian_with(streams_of[0], (MB, PROTEINS, LENGTH, D), 1.0, 8.0, ((1, 8), (2, 4)), (2, 3, 4, 2.0))
    lengths = draw_lengths(jax.random.fold_in(streams_of[15], 71), 0)
    first_gain = jnp.clip(1.0 + 0.1 * jax.random.normal(streams_of[2], (D,), jnp.float32), 0.5, 1.5).astype(jnp.bfloat16)
    first_shift = gaussian(streams_of[3], (D,), 0.2, 1.25, ((0, 8),))
    down_weight = gaussian(streams_of[4], (D, H), D ** -0.5, 0.15625, ((0, 4), (1, 8)))
    down_bias = gaussian(streams_of[5], (H,), 0.2, 1.25, ((0, 8),))
    middle_gain = jnp.clip(1.0 + 0.1 * jax.random.normal(streams_of[6], (H,), jnp.float32), 0.5, 1.5).astype(jnp.bfloat16)
    middle_shift = gaussian(streams_of[7], (H,), 0.2, 1.25, ((0, 8),))
    conv_weight = gaussian(streams_of[8], (KERNEL, H, H), (KERNEL * H) ** -0.5, 0.109375, ((1, 4), (2, 8)))
    conv_bias = gaussian(streams_of[9], (H,), 0.2, 1.25, ((0, 8),))
    final_gain = jnp.clip(1.0 + 0.1 * jax.random.normal(streams_of[10], (H,), jnp.float32), 0.5, 1.5).astype(jnp.bfloat16)
    final_shift = gaussian(streams_of[11], (H,), 0.2, 1.25, ((0, 8),))
    up_weight = gaussian(streams_of[12], (H, D), H ** -0.5, 0.25, ((0, 4), (1, 8)))
    up_bias = gaussian(streams_of[13], (D,), 0.2, 1.25, ((0, 8),))
    cotangent = gaussian_with(streams_of[14], (MB, PROTEINS, LENGTH, D), 1.0, 8.0, ((1, 8), (2, 4)), (1, 3, 8, 2.0))
    return dict(tokens=tokens, lengths=lengths, first_gain=first_gain, first_shift=first_shift, down_weight=down_weight, down_bias=down_bias, middle_gain=middle_gain, middle_shift=middle_shift, conv_weight=conv_weight, conv_bias=conv_bias, final_gain=final_gain, final_shift=final_shift, up_weight=up_weight, up_bias=up_bias, cotangent=cotangent)


EPSILON = 1e-05
HIGHEST = lax.Precision.HIGHEST

@jax.custom_vjp
def low(v):
    return lax.optimization_barrier(v.astype(jnp.bfloat16)).astype(jnp.float32)

@jax.custom_vjp
def low_back(v):
    return v

def low_keep(v):
    return (low(v), None)

def low_pass(kept, grad):
    return (grad,)

def back_keep(v):
    return (v, None)

def back_low(kept, grad):
    return (low(grad),)
low.defvjp(low_keep, low_pass)
low_back.defvjp(back_keep, back_low)

def layer_norm(values, norm_gain, norm_shift):
    center = values - lax.optimization_barrier(jnp.mean(values, axis=-1, keepdims=True))
    spread = lax.optimization_barrier(jnp.mean(center * center, axis=-1, keepdims=True))
    return center * lax.rsqrt(spread + EPSILON) * norm_gain + norm_shift

def norm_gelu(values, norm_gain, norm_shift):
    return jax.nn.gelu(layer_norm(values, norm_gain, norm_shift), approximate=False)

def forward(inputs, lengths_group, params):
    first_gain, first_shift, down_weight, down_bias, middle_gain, middle_shift, conv_weight, conv_bias, final_gain, final_shift, up_weight, up_bias = params
    positions = inputs.shape[1]
    hidden_one = low(norm_gelu(inputs, first_gain, first_shift))
    narrow = low_back(jnp.einsum('gld,dh->glh', hidden_one, down_weight, precision=HIGHEST) + down_bias)
    valid_rows = (jnp.arange(positions, dtype=jnp.int32)[None, :] < lengths_group[:, None]).astype(jnp.float32)
    conv_input = low(norm_gelu(narrow, middle_gain, middle_shift) * valid_rows[:, :, None])
    reach_rows = (KERNEL - 1) // 2 * DILATION
    padded = jnp.pad(conv_input, ((0, 0), (reach_rows, reach_rows), (0, 0)))
    conv_out = jnp.zeros(conv_input.shape, jnp.float32) + conv_bias
    for tap_index in range(KERNEL):
        window = padded[:, tap_index * DILATION:tap_index * DILATION + positions]
        conv_out = conv_out + jnp.einsum('glh,hj->glj', window, conv_weight[tap_index], precision=HIGHEST)
    conv_out = low_back(conv_out)
    hidden_three = low(norm_gelu(conv_out, final_gain, final_shift))
    return inputs + jnp.einsum('glh,hd->gld', hidden_three, up_weight, precision=HIGHEST) + up_bias

def reference(tokens, lengths, first_gain, first_shift, down_weight, down_bias, middle_gain, middle_shift, conv_weight, conv_bias, final_gain, final_shift, up_weight, up_bias, cotangent):
    params = tuple((member.astype(jnp.float32) for member in (first_gain, first_shift, down_weight, down_bias, middle_gain, middle_shift, conv_weight, conv_bias, final_gain, final_shift, up_weight, up_bias)))
    group_size = math.gcd(PROTEINS, max(1, 4096 // LENGTH))
    group_count = MB * PROTEINS // group_size
    token_groups = tokens.reshape(group_count, group_size, LENGTH, D)
    length_groups = lengths.reshape(group_count, group_size)
    cotangent_groups = cotangent.reshape(group_count, group_size, LENGTH, D)

    def advance(totals, record):
        token_part, length_part, cotangent_part = record
        output_value, pullback = jax.vjp(lambda input_value, param_values: forward(input_value, length_part, param_values), token_part.astype(jnp.float32), params)
        input_grad, param_grads = pullback(cotangent_part.astype(jnp.float32))
        totals = tuple((first_term + second_term for first_term, second_term in zip(totals, param_grads)))
        return (totals, (output_value.astype(jnp.bfloat16), input_grad.astype(jnp.bfloat16)))
    zero_grads = tuple((jnp.zeros(member.shape, jnp.float32) for member in params))
    totals, (outputs, input_grads) = lax.scan(advance, zero_grads, (token_groups, length_groups, cotangent_groups))
    return (outputs.reshape(MB, PROTEINS, LENGTH, D), input_grads.reshape(MB, PROTEINS, LENGTH, D), totals[0], totals[1], totals[2], totals[3], totals[4], totals[5], totals[6], totals[7], totals[8], totals[9], totals[10], totals[11])
```

```python
import functools
import math

import jax
import jax.numpy as jnp
from jax import lax
from jax.experimental import pallas as pl
from jax.experimental.pallas import tpu as pltpu
from jax.sharding import PartitionSpec as P

DILATION = 16
EPSILON = 1e-05
BF = jnp.bfloat16
F32 = jnp.float32
ROOT_HALF = 0.7071067811865476
PHI_SCALE = 0.3989422804014327
MIB = 1 << 20

WIDE = ("first_gain", "first_shift", "up_bias")
NARROW = ("down_bias", "middle_gain", "middle_shift", "conv_bias", "final_gain", "final_shift")
ROW = {name: row for row, name in enumerate(WIDE + NARROW)}
TABLE_ROWS = 16


class Grid:
    def __init__(self, seq, batch):
        self.seq, self.batch = seq, batch
        self.side = math.isqrt(seq)
        assert self.side * self.side == seq
        self.depth = batch // 2

    def here(self):
        s, b = lax.axis_index("seq"), lax.axis_index("batch")
        return s // self.side, s % self.side, b // 2, b % 2

    def send(self, value, move):
        pairs = []
        for s in range(self.seq):
            for b in range(self.batch):
                h, l, z, c = move(s // self.side, s % self.side, b // 2, b % 2)
                pairs.append((s * self.batch + b, (h * self.side + l) * self.batch + z * 2 + c))
        return lax.ppermute(value, ("seq", "batch"), pairs)

    def high(self, value, k):
        return self.send(value, lambda h, l, z, c: ((h + k) % self.side, l, z, c))

    def low(self, value, k):
        return self.send(value, lambda h, l, z, c: (h, (l + k) % self.side, z, c))

    def deep(self, value, k):
        return self.send(value, lambda h, l, z, c: (h, l, (z + k) % self.depth, c))

    def core(self, value):
        return self.send(value, lambda h, l, z, c: (h, l, z, 1 - c))

    def gather(self, piece):
        side, half = self.side, self.depth // 2
        column = jnp.stack([piece] + [self.deep(piece, k) for k in range(1, self.depth)])
        one, two = column[:half], column[half:]
        one = jnp.stack([one] + [self.low(one, k) for k in range(1, side)])
        two = jnp.stack([two] + [self.high(two, k) for k in range(1, side)])
        one = jnp.stack([one] + [self.high(one, k) for k in range(1, side)])
        two = jnp.stack([two] + [self.low(two, k) for k in range(1, side)], axis=1)
        mine = jnp.concatenate([one, two], axis=2)
        other = self.core(mine)
        return jnp.stack([mine, other])

    def scatter(self, pieces):
        side, half = self.side, self.depth // 2

        def add(terms, kind):
            total = terms[0].astype(F32)
            for term in terms[1:]:
                total = total + term.astype(F32)
            return total.astype(kind)

        total = add([pieces[0], self.core(pieces[1])], BF)
        one, two = total[:, :, :half], total[:, :, half:]
        one = add([one[0]] + [self.high(one[k], -k) for k in range(1, side)], BF)
        two = add([two[:, 0]] + [self.low(two[:, k], -k) for k in range(1, side)], BF)
        one = add([one[0]] + [self.low(one[k], -k) for k in range(1, side)], BF)
        two = add([two[0]] + [self.high(two[k], -k) for k in range(1, side)], BF)
        column = jnp.concatenate([one, two], axis=0)
        return add([column[0]] + [self.deep(column[k], -k) for k in range(1, self.depth)], F32)


def distance(grid, place, s, b):
    side, depth = grid.side, grid.depth
    h, l, z, c = place[0], place[1], place[2], place[3]
    rh = lax.rem(h - s // side + side, side)
    rl = lax.rem(l - s % side + side, side)
    rz = lax.rem(z - b // 2 + depth, depth)
    core = b - (b // 2) * 2
    rc = jnp.where(core == c, 0, 1)
    return ((rc * side + rh) * side + rl) * depth + rz


def normed(values):
    center = values - jnp.mean(values, axis=-1, keepdims=True)
    spread = jnp.mean(center * center, axis=-1, keepdims=True)
    inverse = lax.rsqrt(spread + EPSILON)
    return center * inverse, inverse


def cumulative(s):
    return 0.5 + 0.5 * lax.erf(s * ROOT_HALF)


def gelu(s):
    return s * cumulative(s)


def gelu_slope(s):
    return cumulative(s) + s * (PHI_SCALE * jnp.exp(-0.5 * s * s))


def back_rows(q, gain, unit, inverse):
    weighted = q * gain
    first = jnp.mean(weighted, axis=-1, keepdims=True)
    second = jnp.mean(weighted * unit, axis=-1, keepdims=True)
    return (weighted - first - unit * second) * inverse


def row_sum(values):
    return jnp.sum(values, axis=0, keepdims=True)


def dot_nn(left, right):
    return lax.dot_general(left, right, (((1,), (0,)), ((), ())), preferred_element_type=F32)


def dot_nt(left, right):
    return lax.dot_general(left, right, (((1,), (1,)), ((), ())), preferred_element_type=F32)


def dot_tn(left, right):
    return lax.dot_general(left, right, (((0,), (0,)), ((), ())), preferred_element_type=F32)


def params(limit):
    return pltpu.CompilerParams(
        dimension_semantics=("arbitrary",), vmem_limit_bytes=limit * MIB
    )


def cost(flops, bytes_accessed, transcendentals=0):
    return pl.CostEstimate(
        flops=flops, bytes_accessed=bytes_accessed, transcendentals=transcendentals
    )


def whole(shape):
    return pl.BlockSpec(shape, lambda i, *_: (0,) * len(shape))


def rows_of(block):
    return pl.BlockSpec(block, lambda i, *_: (i,) + (0,) * (len(block) - 1))


def sds(shape, kind):
    return jax.ShapeDtypeStruct(shape, kind)


def assemble_down_kernel(grid, hb, dl, place, pieces, down_ref, table_ref):
    wide = down_ref.shape[2] // grid.batch
    hidden = hb * grid.batch
    table_ref[...] = jnp.zeros_like(table_ref)
    for b in range(grid.batch):
        for s in range(grid.seq):
            down_ref[b, :, s * dl : (s + 1) * dl] = pieces[distance(grid, place, s, b), 0:hb, :]
        vec = pieces[distance(grid, place, 0, b), hb : hb + 16, :].astype(F32)
        at = 0
        for name in WIDE + NARROW:
            width = wide if name in WIDE else hidden // grid.batch
            done = 0
            while done < width:
                line, col = at // dl, at % dl
                take = min(width - done, dl - col)
                start = b * width + done
                table_ref[ROW[name] : ROW[name] + 1, start : start + take] = vec[
                    line : line + 1, col : col + take
                ]
                at += take
                done += take


def assemble_down(grid, hb, model, pieces, place):
    dl = model // grid.seq
    count = grid.seq * grid.batch
    return pl.pallas_call(
        functools.partial(assemble_down_kernel, grid, hb, dl),
        out_shape=(sds((grid.batch, hb, model), BF), sds((TABLE_ROWS, model), F32)),
        grid_spec=pltpu.PrefetchScalarGridSpec(
            num_scalar_prefetch=1,
            grid=(1,),
            in_specs=[whole(pieces.shape)],
            out_specs=[whole((grid.batch, hb, model)), whole((TABLE_ROWS, model))],
        ),
        compiler_params=params(32),
        cost_estimate=cost(0, 4 * count * hb * dl),
        name="assemble_down",
    )(place, pieces)


def assemble_rest_kernel(grid, hb, hl, taps, fold, place, pieces, conv_ref, up_ref):
    def block(b, _):
        for s in range(grid.seq):
            at = distance(grid, place, s, b)
            piece = pieces[at]
            for k in range(taps):
                conv_ref[k, b, :, s * hl : (s + 1) * hl] = piece[:, k * hl : (k + 1) * hl]
            for f in range(fold):
                col = (taps + f) * hl
                up_ref[b, f, :, s * hl : (s + 1) * hl] = piece[:, col : col + hl]
        return 0

    lax.fori_loop(0, grid.batch, block, 0)


def assemble_rest(grid, hb, hidden, taps, fold, pieces, place):
    hl = hidden // grid.seq
    return pl.pallas_call(
        functools.partial(assemble_rest_kernel, grid, hb, hl, taps, fold),
        out_shape=(
            sds((taps, grid.batch, hb, hidden), BF),
            sds((grid.batch, fold, hb, hidden), BF),
        ),
        grid_spec=pltpu.PrefetchScalarGridSpec(
            num_scalar_prefetch=1,
            grid=(1,),
            in_specs=[whole(pieces.shape)],
            out_specs=[
                whole((taps, grid.batch, hb, hidden)),
                whole((grid.batch, fold, hb, hidden)),
            ],
        ),
        compiler_params=params(48),
        cost_estimate=cost(0, 4 * (taps + fold) * hidden * hidden),
        name="assemble_rest",
    )(place, pieces)


def stage_one_kernel(
    start_ref, length_ref, tokens, table, down_t, hidden_one, narrow, conv_input
):
    model = tokens.shape[2]
    hidden = narrow.shape[2]

    def vec(name, width):
        return table[ROW[name] : ROW[name] + 1, 0:width]

    unit, _ = normed(tokens[0].astype(F32))
    one = gelu(unit * vec("first_gain", model) + vec("first_shift", model)).astype(BF)
    hidden_one[0] = one
    values = dot_nt(one, down_t[...]) + vec("down_bias", hidden)
    narrow[0] = values
    unit, _ = normed(values)
    active = gelu(unit * vec("middle_gain", hidden) + vec("middle_shift", hidden))
    rows = values.shape[0]
    position = start_ref[0] + lax.broadcasted_iota(jnp.int32, (rows, 1), 0)
    valid = (position < length_ref[pl.program_id(0)]).astype(F32)
    conv_input[0] = (active * valid).astype(BF)


def stage_one(tokens, table, down_t, start, lengths):
    count, span, model = tokens.shape
    hidden = down_t.shape[0]
    return pl.pallas_call(
        stage_one_kernel,
        out_shape=(
            sds((count, span, model), BF),
            sds((count, span, hidden), F32),
            sds((count, span, hidden), BF),
        ),
        grid_spec=pltpu.PrefetchScalarGridSpec(
            num_scalar_prefetch=2,
            grid=(count,),
            in_specs=[rows_of((1, span, model)), whole(table.shape), whole(down_t.shape)],
            out_specs=[
                rows_of((1, span, model)),
                rows_of((1, span, hidden)),
                rows_of((1, span, hidden)),
            ],
        ),
        compiler_params=params(32),
        cost_estimate=cost(
            2 * count * span * model * hidden, count * span * (4 * model + 6 * hidden)
        ),
        name="stage_one",
    )(start, lengths, tokens, table, down_t)


def fill_padded(padded, left, body, right):
    reach = left.shape[0]
    span = body.shape[0]
    padded[0:reach] = left
    padded[reach : reach + span] = body
    padded[reach + span : 2 * reach + span] = right


def stage_two_kernel(
    place,
    tokens,
    cotangent,
    conv_input,
    left,
    right,
    table,
    conv_t,
    up_t,
    output,
    conv_out_grad,
    sums,
    padded,
):
    span, model = tokens.shape[1], tokens.shape[2]
    hidden = conv_input.shape[2]
    taps = conv_t.shape[0]

    def vec(name, width):
        return table[ROW[name] : ROW[name] + 1, 0:width]

    @pl.when(pl.program_id(0) == 0)
    def _():
        sums[...] = jnp.zeros_like(sums)

    fill_padded(padded, left[0], conv_input[0], right[0])
    total = dot_nt(padded[0:span], conv_t[0])
    for k in range(1, taps):
        total = total + dot_nt(padded[k * DILATION : k * DILATION + span], conv_t[k])
    total = total + vec("conv_bias", hidden)
    unit, inverse = normed(total)
    gain = vec("final_gain", hidden)
    s = unit * gain + vec("final_shift", hidden)
    phi = cumulative(s)
    three = (s * phi).astype(BF)
    slope = phi + s * (PHI_SCALE * jnp.exp(-0.5 * s * s))
    incoming = cotangent[0]
    result = tokens[0].astype(F32) + dot_nt(three, up_t[...]) + vec("up_bias", model)
    output[0] = result.astype(BF)
    q = dot_nn(incoming, up_t[...]) * slope
    grad = back_rows(q, gain, unit, inverse).astype(BF)
    conv_out_grad[0] = grad

    def add(name, values):
        width = values.shape[1]
        sums[ROW[name] : ROW[name] + 1, 0:width] += row_sum(values)

    add("final_gain", q * unit)
    add("final_shift", q)
    add("conv_bias", grad.astype(F32))
    add("up_bias", incoming.astype(F32))
    return three, incoming


def stage_two_body(grid, hb, fold, place, *refs):
    refs, (three_grad, total) = refs[:-2], refs[-2:]
    three, incoming = stage_two_kernel(place, *refs)

    @pl.when(pl.program_id(0) == 0)
    def _():
        total[...] = jnp.zeros_like(total)

    total[...] += dot_tn(incoming, three)

    @pl.when(pl.program_id(0) == pl.num_programs(0) - 1)
    def _():
        write_pieces(grid, fold * hb, place, total, three_grad)


def write_pieces(grid, rows, place, total, pieces):
    lanes = pieces.shape[2]
    for b in range(grid.batch):
        block = total[b * rows : (b + 1) * rows, :].astype(BF)
        for s in range(grid.seq):
            pieces[distance(grid, place, s, b), :, :] = block[:, s * lanes : (s + 1) * lanes]


def stage_two(grid, place, tokens, cotangent, conv_input, left, right, table, conv_t, up_t):
    count, span, model = tokens.shape
    hidden = conv_input.shape[2]
    taps = conv_t.shape[0]
    reach = left.shape[1]
    hb = hidden // grid.batch
    fold = model // hidden
    hl = hidden // grid.seq
    devices = grid.seq * grid.batch
    pieces = (devices, fold * hb, hl)

    def kernel(
        place, tokens, cotangent, conv_input, left, right, table, conv_t, up_t,
        output, conv_out_grad, sums, up_grad, padded, total,
    ):
        stage_two_body(
            grid, hb, fold, place, tokens, cotangent, conv_input, left, right, table, conv_t,
            up_t, output, conv_out_grad, sums, padded, up_grad, total,
        )

    return pl.pallas_call(
        kernel,
        out_shape=(
            sds((count, span, model), BF),
            sds((count, span, hidden), BF),
            sds((TABLE_ROWS, model), F32),
            sds(pieces, BF),
        ),
        grid_spec=pltpu.PrefetchScalarGridSpec(
            num_scalar_prefetch=1,
            grid=(count,),
            in_specs=[
                rows_of((1, span, model)),
                rows_of((1, span, model)),
                rows_of((1, span, hidden)),
                rows_of((1, reach, hidden)),
                rows_of((1, reach, hidden)),
                whole(table.shape),
                whole(conv_t.shape),
                whole(up_t.shape),
            ],
            out_specs=[
                rows_of((1, span, model)),
                rows_of((1, span, hidden)),
                whole((TABLE_ROWS, model)),
                whole(pieces),
            ],
            scratch_shapes=[
                pltpu.VMEM((span + 2 * reach, hidden), BF),
                pltpu.VMEM((model, hidden), F32),
            ],
        ),
        compiler_params=params(56),
        cost_estimate=cost(
            2 * count * span * hidden * (taps * hidden + 3 * model),
            count * span * (6 * model + 4 * hidden),
        ),
        name="stage_two",
    )(place, tokens, cotangent, conv_input, left, right, table, conv_t, up_t)


def stage_three_kernel(
    grid, taps, place, conv_input, left, right, conv_out_grad, pieces, padded, total
):
    group, span, hidden = conv_input.shape
    reach = left.shape[1]

    @pl.when(pl.program_id(0) == 0)
    def _():
        total[...] = jnp.zeros_like(total)

    for g in range(group):
        padded[g, 0:reach] = left[g]
        padded[g, reach : reach + span] = conv_input[g]
        padded[g, reach + span : 2 * reach + span] = right[g]
    flipped = conv_out_grad[...].reshape(group * span, hidden).T
    for k in range(taps):
        window = padded[:, k * DILATION : k * DILATION + span, :].reshape(group * span, hidden)
        total[k] += dot_nn(flipped, window)

    @pl.when(pl.program_id(0) == pl.num_programs(0) - 1)
    def _():
        rows = hidden // grid.batch
        lanes = hidden // grid.seq
        for b in range(grid.batch):
            for k in range(taps):
                block = total[k, b * rows : (b + 1) * rows, :].astype(BF)
                for s in range(grid.seq):
                    pieces[distance(grid, place, s, b), :, k * lanes : (k + 1) * lanes] = block[
                        :, s * lanes : (s + 1) * lanes
                    ]


def stage_three(grid, place, conv_input, left, right, conv_out_grad, taps):
    count, span, hidden = conv_input.shape
    reach = left.shape[1]
    group = 2 if count % 2 == 0 else 1
    pieces = (grid.seq * grid.batch, hidden // grid.batch, taps * (hidden // grid.seq))
    return pl.pallas_call(
        functools.partial(stage_three_kernel, grid, taps),
        out_shape=sds(pieces, BF),
        grid_spec=pltpu.PrefetchScalarGridSpec(
            num_scalar_prefetch=1,
            grid=(count // group,),
            in_specs=[
                rows_of((group, span, hidden)),
                rows_of((group, reach, hidden)),
                rows_of((group, reach, hidden)),
                rows_of((group, span, hidden)),
            ],
            out_specs=whole(pieces),
            scratch_shapes=[
                pltpu.VMEM((group, span + 2 * reach, hidden), BF),
                pltpu.VMEM((taps, hidden, hidden), F32),
            ],
        ),
        compiler_params=params(48),
        cost_estimate=cost(
            2 * count * span * hidden * taps * hidden, count * span * 4 * hidden
        ),
        name="stage_three",
    )(place, conv_input, left, right, conv_out_grad)


def stage_four_kernel(
    grid,
    place,
    start_ref,
    length_ref,
    tokens,
    cotangent,
    hidden_one,
    narrow,
    conv_out_grad,
    left,
    right,
    table,
    sums_in,
    conv_t,
    down_t,
    tokens_grad,
    pieces,
    padded,
    sums,
    total,
):
    span, model = tokens.shape[1], tokens.shape[2]
    hidden = narrow.shape[2]
    taps = conv_t.shape[0]

    def vec(name, width):
        return table[ROW[name] : ROW[name] + 1, 0:width]

    def add(name, values):
        width = values.shape[1]
        sums[ROW[name] : ROW[name] + 1, 0:width] += row_sum(values)

    @pl.when(pl.program_id(0) == 0)
    def _():
        sums[...] = sums_in[...]
        total[...] = jnp.zeros_like(total)

    fill_padded(padded, left[0], conv_out_grad[0], right[0])
    back = None
    for k in range(taps):
        at = (taps - 1 - k) * DILATION
        term = dot_nn(padded[at : at + span], conv_t[k])
        back = term if back is None else back + term
    position = start_ref[0] + lax.broadcasted_iota(jnp.int32, (span, 1), 0)
    valid = (position < length_ref[pl.program_id(0)]).astype(F32)
    back = back * valid
    unit, inverse = normed(narrow[0])
    gain = vec("middle_gain", hidden)
    q = back * gelu_slope(unit * gain + vec("middle_shift", hidden))
    low = back_rows(q, gain, unit, inverse).astype(BF)
    add("middle_gain", q * unit)
    add("middle_shift", q)
    add("down_bias", low.astype(F32))
    total[...] += dot_tn(low, hidden_one[0])
    deep = dot_nn(low, down_t[...])
    unit, inverse = normed(tokens[0].astype(F32))
    gain = vec("first_gain", model)
    q = deep * gelu_slope(unit * gain + vec("first_shift", model))
    add("first_gain", q * unit)
    add("first_shift", q)
    grad = back_rows(q, gain, unit, inverse) + cotangent[0].astype(F32)
    tokens_grad[0] = grad.astype(BF)

    @pl.when(pl.program_id(0) == pl.num_programs(0) - 1)
    def _():
        hb = hidden // grid.batch
        dl = model // grid.seq
        wide = model // grid.batch
        sub = lax.broadcasted_iota(jnp.int32, (16, dl), 0)
        for b in range(grid.batch):
            block = total[b * hb : (b + 1) * hb, :].astype(BF)
            tail = jnp.zeros((16, dl), F32)
            at = 0
            for name in WIDE + NARROW:
                width = wide if name in WIDE else hb
                done = 0
                while done < width:
                    line, col = at // dl, at % dl
                    take = min(width - done, dl - col)
                    first = b * width + done
                    value = sums[ROW[name] : ROW[name] + 1, first : first + take]
                    parts = []
                    if col:
                        parts.append(jnp.zeros((1, col), F32))
                    parts.append(value)
                    if col + take < dl:
                        parts.append(jnp.zeros((1, dl - col - take), F32))
                    spread = jnp.concatenate(parts, axis=1) if len(parts) > 1 else value
                    tail = tail + jnp.where(sub == line, spread, 0.0)
                    at += take
                    done += take
            tail = tail.astype(BF)
            for s in range(grid.seq):
                to = distance(grid, place, s, b)
                pieces[to, 0:hb, :] = block[:, s * dl : (s + 1) * dl]
                pieces[to, hb : hb + 16, :] = tail


def stage_four(
    grid,
    place,
    start,
    lengths,
    tokens,
    cotangent,
    hidden_one,
    narrow,
    conv_out_grad,
    left,
    right,
    table,
    sums,
    conv_t,
    down_t,
):
    count, span, model = tokens.shape
    hidden = narrow.shape[2]
    taps = conv_t.shape[0]
    reach = left.shape[1]
    hb = hidden // grid.batch
    pieces = (grid.seq * grid.batch, hb + 16, model // grid.seq)
    return pl.pallas_call(
        functools.partial(stage_four_kernel, grid),
        out_shape=(sds((count, span, model), BF), sds(pieces, BF)),
        grid_spec=pltpu.PrefetchScalarGridSpec(
            num_scalar_prefetch=3,
            grid=(count,),
            in_specs=[
                rows_of((1, span, model)),
                rows_of((1, span, model)),
                rows_of((1, span, model)),
                rows_of((1, span, hidden)),
                rows_of((1, span, hidden)),
                rows_of((1, reach, hidden)),
                rows_of((1, reach, hidden)),
                whole(table.shape),
                whole(table.shape),
                whole(conv_t.shape),
                whole(down_t.shape),
            ],
            out_specs=[rows_of((1, span, model)), whole(pieces)],
            scratch_shapes=[
                pltpu.VMEM((span + 2 * reach, hidden), BF),
                pltpu.VMEM((TABLE_ROWS, model), F32),
                pltpu.VMEM((hidden, model), F32),
            ],
        ),
        compiler_params=params(56),
        cost_estimate=cost(
            2 * count * span * hidden * (taps * hidden + 2 * model),
            count * span * (8 * model + 6 * hidden),
        ),
        name="stage_four",
    )(
        place, start, lengths, tokens, cotangent, hidden_one, narrow, conv_out_grad, left, right,
        table, sums, conv_t, down_t,
    )


def halos(cells, reach):
    count = lax.axis_size("seq")
    left = lax.ppermute(
        cells[:, cells.shape[1] - reach :], "seq", [(i, i + 1) for i in range(count - 1)]
    )
    right = lax.ppermute(cells[:, :reach], "seq", [(i + 1, i) for i in range(count - 1)])
    return left, right


def body(
    grid,
    tokens,
    lengths,
    first_gain,
    first_shift,
    down_weight,
    down_bias,
    middle_gain,
    middle_shift,
    conv_weight,
    conv_bias,
    final_gain,
    final_shift,
    up_weight,
    up_bias,
    cotangent,
):
    shape = tokens.shape
    span, model = shape[2], shape[3]
    count = shape[0] * shape[1]
    taps = conv_weight.shape[0]
    hb = down_weight.shape[1]
    hidden = hb * grid.batch
    dl, hl = down_weight.shape[0], conv_weight.shape[1]
    fold = model // hidden
    reach = (taps - 1) // 2 * DILATION

    tokens = tokens.reshape(count, span, model)
    cotangent = cotangent.reshape(count, span, model)
    lengths = lengths.reshape(count)
    here = grid.here()
    place = jnp.stack(here).astype(jnp.int32)
    start = (lax.axis_index("seq") * span).astype(jnp.int32).reshape(1)

    vectors = {
        "first_gain": first_gain,
        "first_shift": first_shift,
        "up_bias": up_bias,
        "down_bias": down_bias,
        "middle_gain": middle_gain,
        "middle_shift": middle_shift,
        "conv_bias": conv_bias,
        "final_gain": final_gain,
        "final_shift": final_shift,
    }
    flat = jnp.concatenate([vectors[name] for name in WIDE + NARROW])
    flat = jnp.pad(flat, (0, 16 * dl - flat.shape[0])).reshape(16, dl)
    first_piece = jnp.concatenate([down_weight.T, flat], axis=0)
    second_piece = jnp.concatenate(
        [
            conv_weight.transpose(2, 0, 1).reshape(hb, taps * hl),
            up_weight.T.reshape(fold, hb, hl).transpose(1, 0, 2).reshape(hb, fold * hl),
        ],
        axis=1,
    )
    devices = grid.seq * grid.batch
    gathered = grid.gather(first_piece).reshape((devices,) + first_piece.shape)
    down_t, table = assemble_down(grid, hb, model, gathered, place)
    down_t = down_t.reshape(hidden, model)
    gathered = grid.gather(second_piece).reshape((devices,) + second_piece.shape)
    conv_t, up_t = assemble_rest(grid, hb, hidden, taps, fold, gathered, place)
    conv_t = conv_t.reshape(taps, hidden, hidden)
    up_t = up_t.reshape(model, hidden)

    hidden_one, narrow, conv_input = stage_one(tokens, table, down_t, start, lengths)
    left, right = halos(conv_input, reach)
    block_output, conv_out_grad, sums, up_pieces = stage_two(
        grid, place, tokens, cotangent, conv_input, left, right, table, conv_t, up_t
    )
    grad_left, grad_right = halos(conv_out_grad, reach)
    conv_pieces = stage_three(grid, place, conv_input, left, right, conv_out_grad, taps)
    tokens_grad, down_pieces = stage_four(
        grid, place, start, lengths, tokens, cotangent, hidden_one, narrow, conv_out_grad,
        grad_left, grad_right, table, sums, conv_t, down_t,
    )

    spread = (2, grid.side, grid.side, grid.depth)
    up_piece = grid.scatter(up_pieces.reshape(spread + up_pieces.shape[1:]))
    conv_piece = grid.scatter(conv_pieces.reshape(spread + conv_pieces.shape[1:]))
    down_piece = grid.scatter(down_pieces.reshape(spread + down_pieces.shape[1:]))

    up_grad = up_piece.T
    conv_grad = conv_piece.reshape(hb, taps, hl).transpose(1, 2, 0)
    down_grad = down_piece[:hb].T
    tail = down_piece[hb:].reshape(-1)
    grads = {}
    at = 0
    for name in WIDE + NARROW:
        width = vectors[name].shape[0]
        grads[name] = tail[at : at + width]
        at += width
    return (
        block_output.reshape(shape),
        tokens_grad.reshape(shape),
        grads["first_gain"],
        grads["first_shift"],
        down_grad,
        grads["down_bias"],
        grads["middle_gain"],
        grads["middle_shift"],
        conv_grad,
        grads["conv_bias"],
        grads["final_gain"],
        grads["final_shift"],
        up_grad,
        grads["up_bias"],
    )


def solution(mesh):
    grid = Grid(mesh.shape["seq"], mesh.shape["batch"])
    return jax.shard_map(
        functools.partial(body, grid),
        mesh=mesh,
        in_specs=(
            P(None, "batch", "seq", None),
            P(None, "batch"),
            P("batch"),
            P("batch"),
            P("seq", "batch"),
            P("batch"),
            P("batch"),
            P("batch"),
            P(None, "seq", "batch"),
            P("batch"),
            P("batch"),
            P("batch"),
            P("seq", "batch"),
            P("batch"),
            P(None, "batch", "seq", None),
        ),
        out_specs=(
            P(None, "batch", "seq", None),
            P(None, "batch", "seq", None),
            P("batch"),
            P("batch"),
            P("seq", "batch"),
            P("batch"),
            P("batch"),
            P("batch"),
            P(None, "seq", "batch"),
            P("batch"),
            P("batch"),
            P("batch"),
            P("seq", "batch"),
            P("batch"),
        ),
        check_vma=False,
    )
```

```python
import functools
import math

import jax
import jax.numpy as jnp
from jax import lax
from jax.experimental import pallas as pl
from jax.experimental.pallas import tpu as pltpu
from jax.sharding import PartitionSpec as P

DILATION = 16
EPSILON = 1e-05
BF = jnp.bfloat16
F32 = jnp.float32
ROOT_HALF = 0.7071067811865476
PHI_SCALE = 0.3989422804014327
MIB = 1 << 20

WIDE = ("first_gain", "first_shift", "up_bias")
NARROW = ("down_bias", "middle_gain", "middle_shift", "conv_bias", "final_gain", "final_shift")
ROW = {name: row for row, name in enumerate(WIDE + NARROW)}
TABLE_ROWS = 16


def add_up(terms, kind):
    total = terms[0].astype(F32)
    for term in terms[1:]:
        total = total + term.astype(F32)
    return total.astype(kind)


class Grid:
    def __init__(self, seq, batch):
        self.seq, self.batch = seq, batch
        self.side = math.isqrt(seq)
        assert self.side * self.side == seq
        self.depth = batch // 2
        self.half = self.depth // 2

    def here(self):
        s, b = lax.axis_index("seq"), lax.axis_index("batch")
        return s // self.side, s % self.side, b // 2, b % 2

    def send(self, value, move):
        pairs = []
        for s in range(self.seq):
            for b in range(self.batch):
                h, l, z, c = move(s // self.side, s % self.side, b // 2, b % 2)
                pairs.append((s * self.batch + b, (h * self.side + l) * self.batch + z * 2 + c))
        return lax.ppermute(value, ("seq", "batch"), pairs)

    def high(self, value, k):
        return self.send(value, lambda h, l, z, c: ((h + k) % self.side, l, z, c))

    def low(self, value, k):
        return self.send(value, lambda h, l, z, c: (h, (l + k) % self.side, z, c))

    def deep(self, value, k):
        return self.send(value, lambda h, l, z, c: (h, l, (z + k) % self.depth, c))

    def core(self, value):
        return self.send(value, lambda h, l, z, c: (h, l, z, 1 - c))

    def gather_deep(self, piece):
        far = [piece] + [self.deep(piece, k) for k in range(1, self.depth)]
        return jnp.stack(far[: self.half]), jnp.stack(far[self.half :])

    def gather_near(self, one, two):
        one = jnp.stack([one] + [self.low(one, k) for k in range(1, self.side)])
        two = jnp.stack([two] + [self.high(two, k) for k in range(1, self.side)])
        return one, two

    def gather_far(self, one, two):
        one = jnp.stack([one] + [self.high(one, k) for k in range(1, self.side)])
        two = jnp.stack([two] + [self.low(two, k) for k in range(1, self.side)])
        return one, two

    def gather_core(self, one, two):
        return one, two, self.core(one), self.core(two)

    def reduce_core(self, keep_one, keep_two, give_one, give_two):
        return (
            add_up([keep_one, self.core(give_one)], BF),
            add_up([keep_two, self.core(give_two)], BF),
        )

    def reduce_far(self, one, two):
        one = add_up([one[0]] + [self.high(one[k], -k) for k in range(1, self.side)], BF)
        two = add_up([two[0]] + [self.low(two[k], -k) for k in range(1, self.side)], BF)
        return one, two

    def reduce_near(self, one, two):
        one = add_up([one[0]] + [self.low(one[k], -k) for k in range(1, self.side)], BF)
        two = add_up([two[0]] + [self.high(two[k], -k) for k in range(1, self.side)], BF)
        return one, two

    def reduce_deep(self, one, two):
        column = [one[k] for k in range(self.half)] + [two[k] for k in range(self.half)]
        return (column[0],) + tuple(self.deep(column[k], -k) for k in range(1, self.depth))


def near_distance(grid, place, s):
    side = grid.side
    return (
        lax.rem(place[0] - s // side + side, side),
        lax.rem(place[1] - s % side + side, side),
    )


def deep_distance(grid, place, b):
    return lax.rem(place[2] - b // 2 + grid.depth, grid.depth)


def spot_of(grid, place, s, b):
    rh, rl = near_distance(grid, place, s)
    rz = deep_distance(grid, place, b)
    second = rz >= grid.half
    return (
        jnp.where(second, 1, 0),
        jnp.where(second, rl, rh),
        jnp.where(second, rh, rl),
        jnp.where(second, rz - grid.half, rz),
    )


def distance(grid, place, s, b):
    return (jnp.where(place[3] == b % 2, 0, 1),) + spot_of(grid, place, s, b)


class Order:
    def __init__(self, grid, hidden):
        self.grid, self.hidden = grid, hidden
        self.hl, self.hb = hidden // grid.seq, hidden // grid.batch
        self.main = self.hl // 128 * 128
        self.rest = self.hl - self.main

    def runs(self, first, count):
        found = []
        at = first
        while at < first + count:
            block, r = at // self.hl, at % self.hl
            if r < self.main:
                length = min(self.main - r, first + count - at)
                place = block * self.main + r
            else:
                length = min(self.hl - r, first + count - at)
                place = self.grid.seq * self.main + block * self.rest + r - self.main
            if found and found[-1][1] + found[-1][2] == place:
                found[-1] = (found[-1][0], found[-1][1], found[-1][2] + length)
            else:
                found.append((at - first, place, length))
            at += length
        return found


def join(parts):
    return parts[0] if len(parts) == 1 else jnp.concatenate(parts, axis=1)


def wire_from_rows(order, row_blocks):
    main, rest, seq = order.main, order.rest, order.grid.seq
    pieces = []
    for s in range(seq):
        parts = [block[:, s * main : (s + 1) * main] for block in row_blocks if main]
        if rest:
            at = seq * main + s * rest
            parts += [block[:, at : at + rest] for block in row_blocks]
        pieces.append(join(parts))
    return pieces


def rows_from_wire(order, pieces, count, j):
    main, rest = order.main, order.rest
    parts = [piece[:, j * main : (j + 1) * main] for piece in pieces if main]
    if rest:
        at = count * main + j * rest
        parts += [piece[:, at : at + rest] for piece in pieces]
    return join(parts)


def stage_copies(place, parts, stage, sems):
    copies = []
    for index, part in enumerate(parts):
        core = jnp.where(place[3] == 0, index // 2, 1 - index // 2)
        copies.append(
            pltpu.make_async_copy(part, stage.at[core, index % 2], sems.at[index])
        )
    for copy in copies:
        copy.start()
    return copies


def staged(grid, place, stage, s, b):
    return stage[(b % 2,) + spot_of(grid, place, s, b)]


def hand_out(pieces, parts, sems):
    copies = [
        pltpu.make_async_copy(pieces.at[index // 2, index % 2], part, sems.at[index])
        for index, part in enumerate(parts)
    ]
    for copy in copies:
        copy.start()
    for copy in copies:
        copy.wait()


def piece_shape(grid, rows, lanes):
    return (grid.side, grid.side, grid.half, rows, lanes)


def vector_slots(grid, order, model, lanes):
    slots = []
    for b in range(grid.batch):
        at = 0
        for name in WIDE + NARROW:
            if name in WIDE:
                width = model // grid.batch
                runs = [(0, b * width, width)]
            else:
                width = order.hb
                runs = order.runs(b * width, width)
            for offset, spot, length in runs:
                done = 0
                while done < length:
                    flat = at + offset + done
                    take = min(length - done, lanes - flat % lanes)
                    slots.append((ROW[name], flat // lanes, flat % lanes, spot + done, take, b))
                    done += take
            at += width
    return slots


def normed(values):
    center = values - jnp.mean(values, axis=-1, keepdims=True)
    spread = jnp.mean(center * center, axis=-1, keepdims=True)
    inverse = lax.rsqrt(spread + EPSILON)
    return center * inverse, inverse


def cumulative(s):
    return 0.5 + 0.5 * lax.erf(s * ROOT_HALF)


def gelu(s):
    return s * cumulative(s)


def gelu_slope(s):
    return cumulative(s) + s * (PHI_SCALE * jnp.exp(-0.5 * s * s))


def back_rows(q, gain, unit, inverse):
    weighted = q * gain
    first = jnp.mean(weighted, axis=-1, keepdims=True)
    second = jnp.mean(weighted * unit, axis=-1, keepdims=True)
    return (weighted - first - unit * second) * inverse


def row_sum(values):
    return jnp.sum(values, axis=0, keepdims=True)


def dot_nn(left, right):
    return lax.dot_general(left, right, (((1,), (0,)), ((), ())), preferred_element_type=F32)


def dot_nt(left, right):
    return lax.dot_general(left, right, (((1,), (1,)), ((), ())), preferred_element_type=F32)


def dot_tn(left, right):
    return lax.dot_general(left, right, (((0,), (0,)), ((), ())), preferred_element_type=F32)


def params(limit):
    return pltpu.CompilerParams(
        dimension_semantics=("arbitrary",), vmem_limit_bytes=limit * MIB
    )


def cost(flops, bytes_accessed, transcendentals=0):
    return pl.CostEstimate(
        flops=flops, bytes_accessed=bytes_accessed, transcendentals=transcendentals
    )


def whole(shape):
    return pl.BlockSpec(shape, lambda i, *_: (0,) * len(shape))


def rows_of(block):
    return pl.BlockSpec(block, lambda i, *_: (i,) + (0,) * (len(block) - 1))


def sds(shape, kind):
    return jax.ShapeDtypeStruct(shape, kind)


def pack_first_kernel(grid, order, model, down, *refs):
    values, first = refs[:-1], refs[-1]
    hb, dl = order.hb, down.shape[0]
    first[0:hb] = down[...].astype(F32).T.astype(BF)
    sub = lax.broadcasted_iota(jnp.int32, (16, dl), 0)
    tail = jnp.zeros((16, dl), F32)
    at = 0
    for value in values:
        width = value.shape[1]
        done = 0
        while done < width:
            line, column = (at + done) // dl, (at + done) % dl
            take = min(width - done, dl - column)
            tail = tail + jnp.where(
                sub == line, place_in_row(value[:, done : done + take].astype(F32), column, dl), 0.0
            )
            done += take
        at += width
    first[hb : hb + 16] = tail.astype(BF)


def place_in_row(value, column, lanes):
    parts = [value]
    if column:
        parts.insert(0, jnp.zeros((1, column), F32))
    if column + value.shape[1] < lanes:
        parts.append(jnp.zeros((1, lanes - column - value.shape[1]), F32))
    return join(parts)


def pack_first(grid, order, model, down, values):
    hb, dl = order.hb, down.shape[0]
    return pl.pallas_call(
        functools.partial(pack_first_kernel, grid, order, model),
        out_shape=sds((hb + 16, dl), BF),
        compiler_params=pltpu.CompilerParams(vmem_limit_bytes=16 * MIB),
        cost_estimate=cost(0, 4 * hb * dl),
        name="pack_first",
    )(down, *[value.reshape(1, -1) for value in values])


def pack_second_kernel(order, conv, up, second):
    hb, taps = order.hb, conv.shape[0]
    fold = up.shape[1] // hb
    blocks = [conv[k].astype(F32).T.astype(BF) for k in range(taps)]
    turned = up[...].astype(F32).T.astype(BF)
    blocks += [turned[f * hb : (f + 1) * hb] for f in range(fold)]
    parts = [block[:, : order.main] for block in blocks if order.main]
    if order.rest:
        parts += [block[:, order.main :] for block in blocks]
    second[...] = join(parts)


def pack_second(order, conv, up):
    hb = order.hb
    blocks = conv.shape[0] + up.shape[1] // hb
    return pl.pallas_call(
        functools.partial(pack_second_kernel, order),
        out_shape=sds((hb, blocks * order.hl), BF),
        compiler_params=pltpu.CompilerParams(vmem_limit_bytes=16 * MIB),
        cost_estimate=cost(0, 4 * hb * blocks * order.hl),
        name="pack_second",
    )(conv, up)


def unpack_rest_kernel(order, taps, *refs):
    terms, (conv, up) = refs[:-2], refs[-2:]
    hb = order.hb
    fold = up.shape[1] // hb
    total = add_up([term[...] for term in terms], F32)
    for j in range(taps + fold):
        block = rows_from_wire(order, [total], taps + fold, j).T
        if j < taps:
            conv[j] = block
        else:
            up[:, (j - taps) * hb : (j - taps + 1) * hb] = block


def unpack_rest(order, taps, fold, terms):
    return pl.pallas_call(
        functools.partial(unpack_rest_kernel, order, taps),
        out_shape=(
            sds((taps, order.hl, order.hb), F32),
            sds((order.hl, fold * order.hb), F32),
        ),
        compiler_params=pltpu.CompilerParams(vmem_limit_bytes=16 * MIB),
        cost_estimate=cost(0, 8 * (taps + fold) * order.hl * order.hb),
        name="unpack_rest",
    )(*terms)


def unpack_first_kernel(order, *refs):
    terms, (down, tail) = refs[:-2], refs[-2:]
    hb = order.hb
    total = add_up([term[...] for term in terms], F32)
    down[...] = total[0:hb].T
    tail[...] = total[hb : hb + 16]


def unpack_first(order, terms):
    dl = terms[0].shape[1]
    return pl.pallas_call(
        functools.partial(unpack_first_kernel, order),
        out_shape=(sds((dl, order.hb), F32), sds((16, dl), F32)),
        compiler_params=pltpu.CompilerParams(vmem_limit_bytes=16 * MIB),
        cost_estimate=cost(0, 8 * dl * order.hb),
        name="unpack_first",
    )(*terms)


def stage_one_kernel(
    grid, order, place, start_ref, length_ref, tokens, one_m, two_m, one_o, two_o,
    hidden_one, narrow, conv_input, down_t, table, stage, sems,
):
    model = tokens.shape[2]
    hidden = narrow.shape[2]
    hb, dl = order.hb, model // grid.seq

    @pl.when(pl.program_id(0) == 0)
    def _():
        copies = stage_copies(place, (one_m, two_m, one_o, two_o), stage, sems)
        for copy in copies:
            copy.wait()
        table[...] = jnp.zeros_like(table)
        for b in range(grid.batch):
            pieces = [staged(grid, place, stage, s, b) for s in range(grid.seq)]
            block = join([piece[0:hb] for piece in pieces])
            for offset, spot, length in order.runs(b * hb, hb):
                down_t[spot : spot + length] = block[offset : offset + length]
            tail = pieces[0][hb : hb + 16].astype(F32)
            for row, line, column, spot, length, owner in vector_slots(grid, order, model, dl):
                if owner == b:
                    table[row : row + 1, spot : spot + length] = tail[
                        line : line + 1, column : column + length
                    ]

    def vec(name, width):
        return table[ROW[name] : ROW[name] + 1, 0:width]

    unit, _ = normed(tokens[0].astype(F32))
    one = gelu(unit * vec("first_gain", model) + vec("first_shift", model)).astype(BF)
    hidden_one[0] = one
    values = dot_nt(one, down_t[...]) + vec("down_bias", hidden)
    narrow[0] = values
    unit, _ = normed(values)
    active = gelu(unit * vec("middle_gain", hidden) + vec("middle_shift", hidden))
    position = start_ref[0] + lax.broadcasted_iota(jnp.int32, (values.shape[0], 1), 0)
    valid = (position < length_ref[pl.program_id(0)]).astype(F32)
    conv_input[0] = (active * valid).astype(BF)


def stage_one(grid, order, place, start, lengths, tokens, parts):
    count, span, model = tokens.shape
    hidden = order.hidden
    rows, lanes = parts[0].shape[-2:]
    return pl.pallas_call(
        functools.partial(stage_one_kernel, grid, order),
        out_shape=(
            sds((count, span, model), BF),
            sds((count, span, hidden), F32),
            sds((count, span, hidden), BF),
            sds((hidden, model), BF),
            sds((TABLE_ROWS, model), F32),
        ),
        grid_spec=pltpu.PrefetchScalarGridSpec(
            num_scalar_prefetch=3,
            grid=(count,),
            in_specs=[rows_of((1, span, model))]
            + [pl.BlockSpec(memory_space=pl.ANY)] * 4,
            out_specs=[
                rows_of((1, span, model)),
                rows_of((1, span, hidden)),
                rows_of((1, span, hidden)),
                whole((hidden, model)),
                whole((TABLE_ROWS, model)),
            ],
            scratch_shapes=[
                pltpu.VMEM((2, 2) + piece_shape(grid, rows, lanes), BF),
                pltpu.SemaphoreType.DMA((4,)),
            ],
        ),
        compiler_params=params(60),
        cost_estimate=cost(
            2 * count * span * model * hidden, count * span * (4 * model + 6 * hidden)
        ),
        name="stage_one",
    )(place, start, lengths, tokens, *parts)


def fill_padded(padded, left, body, right):
    reach = left.shape[0]
    span = body.shape[0]
    padded[0:reach] = left
    padded[reach : reach + span] = body
    padded[reach + span : 2 * reach + span] = right


def stage_two_kernel(
    grid, order, taps, place, tokens, cotangent, conv_input, left, right, table,
    one_m, two_m, one_o, two_o,
    output, conv_out_grad, sums, part_a, part_b, part_c, part_d, conv_t,
    padded, up_t, total, conv_total, stage, pieces, sems, out_sems,
):
    span, model = tokens.shape[1], tokens.shape[2]
    hidden = conv_input.shape[2]
    hb = order.hb
    fold = model // hidden
    blocks = taps + fold

    def vec(name, width):
        return table[ROW[name] : ROW[name] + 1, 0:width]

    @pl.when(pl.program_id(0) == 0)
    def _():
        copies = stage_copies(place, (one_m, two_m, one_o, two_o), stage, sems)
        sums[...] = jnp.zeros_like(sums)
        total[...] = jnp.zeros_like(total)
        conv_total[...] = jnp.zeros_like(conv_total)
        for copy in copies:
            copy.wait()
        for b in range(grid.batch):
            wires = [staged(grid, place, stage, s, b) for s in range(grid.seq)]
            for k in range(taps):
                block = rows_from_wire(order, wires, blocks, k)
                for offset, spot, length in order.runs(b * hb, hb):
                    conv_t[k, spot : spot + length] = block[offset : offset + length]
            for f in range(fold):
                row = (b * fold + f) * hb
                up_t[row : row + hb] = rows_from_wire(order, wires, blocks, taps + f)

    fill_padded(padded, left[0], conv_input[0], right[0])
    values = dot_nt(padded[0:span], conv_t[0])
    for k in range(1, taps):
        values = values + dot_nt(padded[k * DILATION : k * DILATION + span], conv_t[k])
    values = values + vec("conv_bias", hidden)
    unit, inverse = normed(values)
    gain = vec("final_gain", hidden)
    s = unit * gain + vec("final_shift", hidden)
    phi = cumulative(s)
    three = (s * phi).astype(BF)
    slope = phi + s * (PHI_SCALE * jnp.exp(-0.5 * s * s))
    incoming = cotangent[0]
    result = tokens[0].astype(F32) + dot_nt(three, up_t[...]) + vec("up_bias", model)
    output[0] = result.astype(BF)
    q = dot_nn(incoming, up_t[...]) * slope
    grad = back_rows(q, gain, unit, inverse).astype(BF)
    conv_out_grad[0] = grad

    def add(name, values):
        width = values.shape[1]
        sums[ROW[name] : ROW[name] + 1, 0:width] += row_sum(values)

    add("final_gain", q * unit)
    add("final_shift", q)
    add("conv_bias", grad.astype(F32))
    add("up_bias", incoming.astype(F32))
    total[...] += dot_tn(incoming, three)
    flipped = grad.T
    for k in range(taps):
        conv_total[k] += dot_nn(flipped, padded[k * DILATION : k * DILATION + span])

    @pl.when(pl.program_id(0) == pl.num_programs(0) - 1)
    def _():
        for b in range(grid.batch):
            for offset, spot, length in order.runs(b * hb, hb):
                rows = [conv_total[k, spot : spot + length].astype(BF) for k in range(taps)]
                for f in range(fold):
                    at = (b * fold + f) * hb + offset
                    rows.append(total[at : at + length].astype(BF))
                for s, piece in enumerate(wire_from_rows(order, rows)):
                    pieces[distance(grid, place, s, b) + (pl.ds(offset, length),)] = piece
        hand_out(pieces, (part_a, part_b, part_c, part_d), out_sems)


def stage_two(grid, order, taps, place, tokens, cotangent, conv_input, left, right, table, parts):
    count, span, model = tokens.shape
    hidden = conv_input.shape[2]
    reach = left.shape[1]
    rows, lanes = parts[0].shape[-2:]
    fold = model // hidden
    pieces = piece_shape(grid, order.hb, (taps + fold) * order.hl)
    return pl.pallas_call(
        functools.partial(stage_two_kernel, grid, order, taps),
        out_shape=(
            sds((count, span, model), BF),
            sds((count, span, hidden), BF),
            sds((TABLE_ROWS, model), F32),
            *[sds(pieces, BF)] * 4,
            sds((taps, hidden, hidden), BF),
        ),
        grid_spec=pltpu.PrefetchScalarGridSpec(
            num_scalar_prefetch=1,
            grid=(count,),
            in_specs=[
                rows_of((1, span, model)),
                rows_of((1, span, model)),
                rows_of((1, span, hidden)),
                rows_of((1, reach, hidden)),
                rows_of((1, reach, hidden)),
                whole(table.shape),
            ]
            + [pl.BlockSpec(memory_space=pl.ANY)] * 4,
            out_specs=[
                rows_of((1, span, model)),
                rows_of((1, span, hidden)),
                whole((TABLE_ROWS, model)),
                *[pl.BlockSpec(memory_space=pl.ANY)] * 4,
                whole((taps, hidden, hidden)),
            ],
            scratch_shapes=[
                pltpu.VMEM((span + 2 * reach, hidden), BF),
                pltpu.VMEM((model, hidden), BF),
                pltpu.VMEM((model, hidden), F32),
                pltpu.VMEM((taps, hidden, hidden), F32),
                pltpu.VMEM((2, 2) + piece_shape(grid, rows, lanes), BF),
                pltpu.VMEM((2, 2) + pieces, BF),
                pltpu.SemaphoreType.DMA((4,)),
                pltpu.SemaphoreType.DMA((4,)),
            ],
        ),
        compiler_params=params(60),
        cost_estimate=cost(
            2 * count * span * hidden * (2 * taps * hidden + 3 * model),
            count * span * (6 * model + 4 * hidden),
        ),
        name="stage_two",
    )(place, tokens, cotangent, conv_input, left, right, table, *parts)


def stage_three_kernel(
    start_ref, length_ref, narrow, conv_out_grad, left, right, table, sums_in, conv_t,
    narrow_grad, sums, padded,
):
    span, hidden = narrow.shape[1], narrow.shape[2]
    taps = conv_t.shape[0]

    def vec(name, width):
        return table[ROW[name] : ROW[name] + 1, 0:width]

    def add(name, values):
        width = values.shape[1]
        sums[ROW[name] : ROW[name] + 1, 0:width] += row_sum(values)

    @pl.when(pl.program_id(0) == 0)
    def _():
        sums[...] = sums_in[...]

    fill_padded(padded, left[0], conv_out_grad[0], right[0])
    back = None
    for k in range(taps):
        at = (taps - 1 - k) * DILATION
        term = dot_nn(padded[at : at + span], conv_t[k])
        back = term if back is None else back + term
    position = start_ref[0] + lax.broadcasted_iota(jnp.int32, (span, 1), 0)
    valid = (position < length_ref[pl.program_id(0)]).astype(F32)
    back = back * valid
    unit, inverse = normed(narrow[0])
    gain = vec("middle_gain", hidden)
    q = back * gelu_slope(unit * gain + vec("middle_shift", hidden))
    low = back_rows(q, gain, unit, inverse).astype(BF)
    narrow_grad[0] = low
    add("middle_gain", q * unit)
    add("middle_shift", q)
    add("down_bias", low.astype(F32))


def stage_three(start, lengths, narrow, conv_out_grad, left, right, table, sums, conv_t):
    count, span, hidden = narrow.shape
    taps = conv_t.shape[0]
    reach = left.shape[1]

    return pl.pallas_call(
        stage_three_kernel,
        out_shape=(sds((count, span, hidden), BF), sds(sums.shape, F32)),
        grid_spec=pltpu.PrefetchScalarGridSpec(
            num_scalar_prefetch=2,
            grid=(count,),
            in_specs=[
                rows_of((1, span, hidden)),
                rows_of((1, span, hidden)),
                rows_of((1, reach, hidden)),
                rows_of((1, reach, hidden)),
                whole(table.shape),
                whole(table.shape),
                whole(conv_t.shape),
            ],
            out_specs=[rows_of((1, span, hidden)), whole(sums.shape)],
            scratch_shapes=[pltpu.VMEM((span + 2 * reach, hidden), BF)],
        ),
        compiler_params=params(40),
        cost_estimate=cost(
            2 * count * span * hidden * taps * hidden, count * span * 8 * hidden
        ),
        name="stage_three",
    )(start, lengths, narrow, conv_out_grad, left, right, table, sums, conv_t)


def stage_four_kernel(
    grid, order, last, begin, place, tokens, cotangent, hidden_one, narrow_grad, table, sums_in,
    down_t, *refs,
):
    if begin:
        grad_in, total_in = None, None
    else:
        grad_in, total_in, refs = refs[0], refs[1], refs[2:]
    tokens_grad, sums, total = refs[:3]
    model = tokens.shape[2]
    hidden = narrow_grad.shape[2]
    hb, dl = order.hb, model // grid.seq

    def vec(name, width):
        return table[ROW[name] : ROW[name] + 1, 0:width]

    def add(name, values):
        width = values.shape[1]
        sums[ROW[name] : ROW[name] + 1, 0:width] += row_sum(values)

    @pl.when(pl.program_id(0) == 0)
    def _():
        sums[...] = sums_in[...]
        total[...] = jnp.zeros_like(total) if begin else total_in[...]

    low = narrow_grad[0]
    total[...] += dot_tn(low, hidden_one[0])
    deep = dot_nn(low, down_t[...])
    unit, inverse = normed(tokens[0].astype(F32))
    gain = vec("first_gain", model)
    q = deep * gelu_slope(unit * gain + vec("first_shift", model))
    add("first_gain", q * unit)
    add("first_shift", q)
    grad = back_rows(q, gain, unit, inverse) + cotangent[0].astype(F32)
    tokens_grad[0] = grad.astype(BF)

    if last:
        part_a, part_b, part_c, part_d, pieces, out_sems = refs[3:]

        @pl.when(pl.program_id(0) == pl.num_programs(0) - 1)
        def _():
            sub = lax.broadcasted_iota(jnp.int32, (16, dl), 0)
            for b in range(grid.batch):
                tail = jnp.zeros((16, dl), F32)
                for row, line, column, spot, length, owner in vector_slots(grid, order, model, dl):
                    if owner != b:
                        continue
                    parts = [sums[row : row + 1, spot : spot + length]]
                    if column:
                        parts.insert(0, jnp.zeros((1, column), F32))
                    if column + length < dl:
                        parts.append(jnp.zeros((1, dl - column - length), F32))
                    tail = tail + jnp.where(sub == line, join(parts), 0.0)
                tail = tail.astype(BF)
                for s in range(grid.seq):
                    to = distance(grid, place, s, b)
                    for offset, spot, length in order.runs(b * hb, hb):
                        pieces[to + (pl.ds(offset, length),)] = total[
                            spot : spot + length, s * dl : (s + 1) * dl
                        ].astype(BF)
                    pieces[to + (pl.ds(hb, 16),)] = tail
            hand_out(pieces, (part_a, part_b, part_c, part_d), out_sems)


def stage_four(
    grid, order, first, part, begin, last, place, tokens, cotangent, hidden_one, narrow_grad,
    table, sums, down_t, grad_in, total_in,
):
    count, span, model = tokens.shape
    hidden = narrow_grad.shape[2]
    pieces = piece_shape(grid, order.hb + 16, model // grid.seq)

    def part_of(block):
        return pl.BlockSpec(block, lambda i, *_: (first + i,) + (0,) * (len(block) - 1))

    in_specs = [
        part_of((1, span, model)),
        part_of((1, span, model)),
        part_of((1, span, model)),
        part_of((1, span, hidden)),
        whole(table.shape),
        whole(table.shape),
        whole(down_t.shape),
    ]
    inputs = [tokens, cotangent, hidden_one, narrow_grad, table, sums, down_t]
    aliases = {}
    if not begin:
        in_specs += [pl.BlockSpec(memory_space=pl.ANY), whole((hidden, model))]
        inputs += [grad_in, total_in]
        aliases = {8: 0}
    out_shape = [
        sds((count, span, model), BF),
        sds(table.shape, F32),
        sds((hidden, model), F32),
    ]
    out_specs = [part_of((1, span, model)), whole(table.shape), whole((hidden, model))]
    scratch = []
    if last:
        out_shape += [sds(pieces, BF)] * 4
        out_specs += [pl.BlockSpec(memory_space=pl.ANY)] * 4
        scratch = [pltpu.VMEM((2, 2) + pieces, BF), pltpu.SemaphoreType.DMA((4,))]
    return pl.pallas_call(
        functools.partial(stage_four_kernel, grid, order, last, begin),
        out_shape=tuple(out_shape),
        grid_spec=pltpu.PrefetchScalarGridSpec(
            num_scalar_prefetch=1,
            grid=(part,),
            in_specs=in_specs,
            out_specs=out_specs,
            scratch_shapes=scratch,
        ),
        input_output_aliases=aliases,
        compiler_params=params(48),
        cost_estimate=cost(
            4 * part * span * hidden * model, part * span * (8 * model + 2 * hidden)
        ),
        name="stage_four",
    )(place, *inputs)


def halos(cells, reach):
    count = lax.axis_size("seq")
    left = lax.ppermute(
        cells[:, cells.shape[1] - reach :], "seq", [(i, i + 1) for i in range(count - 1)]
    )
    right = lax.ppermute(cells[:, :reach], "seq", [(i + 1, i) for i in range(count - 1)])
    return left, right


def after(value, *others):
    return lax.optimization_barrier((value,) + others)[0]


def body(
    grid,
    tokens,
    lengths,
    first_gain,
    first_shift,
    down_weight,
    down_bias,
    middle_gain,
    middle_shift,
    conv_weight,
    conv_bias,
    final_gain,
    final_shift,
    up_weight,
    up_bias,
    cotangent,
):
    shape = tokens.shape
    span, model = shape[2], shape[3]
    count = shape[0] * shape[1]
    taps = conv_weight.shape[0]
    hidden = down_weight.shape[1] * grid.batch
    order = Order(grid, hidden)
    hb, hl, dl = order.hb, order.hl, down_weight.shape[0]
    fold = model // hidden
    reach = (taps - 1) // 2 * DILATION

    tokens = tokens.reshape(count, span, model)
    cotangent = cotangent.reshape(count, span, model)
    lengths = lengths.reshape(count)
    place = jnp.stack(grid.here()).astype(jnp.int32)
    start = (lax.axis_index("seq") * span).astype(jnp.int32).reshape(1)

    vectors = {
        "first_gain": first_gain,
        "first_shift": first_shift,
        "up_bias": up_bias,
        "down_bias": down_bias,
        "middle_gain": middle_gain,
        "middle_shift": middle_shift,
        "conv_bias": conv_bias,
        "final_gain": final_gain,
        "final_shift": final_shift,
    }
    first_piece = pack_first(
        grid, order, model, down_weight, [vectors[name] for name in WIDE + NARROW]
    )
    second_piece = pack_second(order, after(conv_weight, first_piece), up_weight)

    def meet(*groups):
        flat = lax.optimization_barrier(tuple(value for group in groups for value in group))
        found, at = [], 0
        for group in groups:
            found.append(flat[at : at + len(group)])
            at += len(group)
        return found

    first = grid.gather_deep(first_piece)
    first = grid.gather_near(*first)
    first, (second_piece,) = meet(first, (second_piece,))
    second = grid.gather_deep(second_piece)
    first = grid.gather_far(*first)
    second, first = meet(second, first)
    second = grid.gather_near(*second)
    first = grid.gather_core(*first)
    second, first = meet(second, first)
    second = grid.gather_far(*second)
    hidden_one, narrow, conv_input, down_t, table = stage_one(
        grid, order, place, start, lengths, tokens, first
    )
    second, (conv_input,) = meet(second, (conv_input,))
    left, right = halos(conv_input, reach)
    second = grid.gather_core(*second)
    block_output, conv_out_grad, sums, *rest, conv_t = stage_two(
        grid, order, taps, place, tokens, cotangent, conv_input, left, right, table, second
    )
    half = count // 2

    left, right = halos(conv_out_grad, reach)
    rest = grid.reduce_core(*rest)
    rest, (sums, left, right) = meet(rest, (sums, left, right))

    rest = grid.reduce_far(*rest)
    narrow_grad, sums = stage_three(
        start, lengths, narrow, conv_out_grad, left, right, table, sums, conv_t
    )
    rest, (sums,) = meet(rest, (sums,))

    rest = grid.reduce_near(*rest)
    tokens_grad, sums, total = stage_four(
        grid, order, 0, half, True, False, place, tokens, cotangent, hidden_one, narrow_grad,
        table, sums, down_t, None, None,
    )
    rest, (sums,) = meet(rest, (sums,))

    rest = grid.reduce_deep(*rest)
    tokens_grad, sums, total, *down = stage_four(
        grid, order, half, half, False, True, place, tokens, cotangent, hidden_one, narrow_grad,
        table, sums, down_t, tokens_grad, total,
    )
    rest, down = meet(rest, down)

    down = grid.reduce_near(*grid.reduce_far(*grid.reduce_core(*down)))
    down = grid.reduce_deep(*down)
    conv_grad, up_grad = unpack_rest(order, taps, fold, rest)
    down_grad, tail = unpack_first(order, down)
    tail = tail.reshape(-1)
    grads = {}
    at = 0
    for name in WIDE + NARROW:
        width = vectors[name].shape[0]
        grads[name] = tail[at : at + width]
        at += width
    return (
        block_output.reshape(shape),
        tokens_grad.reshape(shape),
        grads["first_gain"],
        grads["first_shift"],
        down_grad,
        grads["down_bias"],
        grads["middle_gain"],
        grads["middle_shift"],
        conv_grad,
        grads["conv_bias"],
        grads["final_gain"],
        grads["final_shift"],
        up_grad,
        grads["up_bias"],
    )


def solution(mesh):
    grid = Grid(mesh.shape["seq"], mesh.shape["batch"])
    return jax.shard_map(
        functools.partial(body, grid),
        mesh=mesh,
        in_specs=(
            P(None, "batch", "seq", None),
            P(None, "batch"),
            P("batch"),
            P("batch"),
            P("seq", "batch"),
            P("batch"),
            P("batch"),
            P("batch"),
            P(None, "seq", "batch"),
            P("batch"),
            P("batch"),
            P("batch"),
            P("seq", "batch"),
            P("batch"),
            P(None, "batch", "seq", None),
        ),
        out_specs=(
            P(None, "batch", "seq", None),
            P(None, "batch", "seq", None),
            P("batch"),
            P("batch"),
            P("seq", "batch"),
            P("batch"),
            P("batch"),
            P("batch"),
            P(None, "seq", "batch"),
            P("batch"),
            P("batch"),
            P("batch"),
            P("seq", "batch"),
            P("batch"),
        ),
        check_vma=False,
    )
```

```python
import functools
import math

import jax
import jax.numpy as jnp
from jax import lax
from jax.experimental import pallas as pl
from jax.experimental.pallas import tpu as pltpu
from jax.sharding import PartitionSpec as P

DILATION = 16
EPSILON = 1e-05
BF = jnp.bfloat16
F32 = jnp.float32
ROOT_HALF = math.sqrt(0.5)
SLOPE = 2.0 / math.sqrt(math.pi)
LOG = -math.log2(math.e)
MIB = 1 << 20
GROUP = 2
LIM2P = 60
LIM2 = 60
LIM3P = 40
LIM3 = 40
LIM4 = 48

WIDE = ("first_gain", "first_shift", "up_bias")
NARROW = ("down_bias", "middle_gain", "middle_shift", "conv_bias", "final_gain", "final_shift")
WIDE_ROWS = 3
ROW = {name: row for row, name in enumerate(WIDE + NARROW)}
TABLE_ROWS = 16


def add_up(terms, kind):
    total = terms[0].astype(F32)
    for term in terms[1:]:
        total = total + term.astype(F32)
    return total.astype(kind)


class Grid:
    def __init__(self, seq, batch):
        self.seq, self.batch = seq, batch
        self.side = math.isqrt(seq)
        assert self.side * self.side == seq
        self.depth = batch // 2
        self.half = self.depth // 2

    def here(self):
        s, b = lax.axis_index("seq"), lax.axis_index("batch")
        return s // self.side, s % self.side, b // 2, b % 2

    def send(self, value, move):
        pairs = []
        for s in range(self.seq):
            for b in range(self.batch):
                h, l, z, c = move(s // self.side, s % self.side, b // 2, b % 2)
                pairs.append((s * self.batch + b, (h * self.side + l) * self.batch + z * 2 + c))
        return lax.ppermute(value, ("seq", "batch"), pairs)

    def high(self, value, k):
        return self.send(value, lambda h, l, z, c: ((h + k) % self.side, l, z, c))

    def low(self, value, k):
        return self.send(value, lambda h, l, z, c: (h, (l + k) % self.side, z, c))

    def deep(self, value, k):
        return self.send(value, lambda h, l, z, c: (h, l, (z + k) % self.depth, c))

    def core(self, value):
        return self.send(value, lambda h, l, z, c: (h, l, z, 1 - c))

    def gather_deep(self, piece):
        return [piece] + [self.deep(piece, k) for k in range(1, self.depth)]

    def halves(self, column):
        return jnp.stack(column[: self.half]), jnp.stack(column[self.half :])

    def gather_near(self, one, two):
        one = jnp.stack([one] + [self.low(one, k) for k in range(1, self.side)])
        two = jnp.stack([two] + [self.high(two, k) for k in range(1, self.side)])
        return one, two

    def gather_far(self, one, two):
        return (
            [self.high(one, k) for k in range(1, self.side)],
            [self.low(two, k) for k in range(1, self.side)],
        )

    def gather_core(self, values):
        return [self.core(value) for value in values]

    def reduce_core(self, keep_one, keep_two, give_one, give_two):
        return (
            add_up([keep_one, self.core(give_one)], BF),
            add_up([keep_two, self.core(give_two)], BF),
        )

    def reduce_far(self, one, two):
        one = add_up([one[0]] + [self.high(one[k], -k) for k in range(1, self.side)], BF)
        two = add_up([two[0]] + [self.low(two[k], -k) for k in range(1, self.side)], BF)
        return one, two

    def reduce_near(self, one, two):
        one = add_up([one[0]] + [self.low(one[k], -k) for k in range(1, self.side)], BF)
        two = add_up([two[0]] + [self.high(two[k], -k) for k in range(1, self.side)], BF)
        return one, two

    def reduce_deep(self, one, two):
        column = [one[k] for k in range(self.half)] + [two[k] for k in range(self.half)]
        return (column[0],) + tuple(self.deep(column[k], -k) for k in range(1, self.depth))


def near_distance(grid, place, s):
    side = grid.side
    return (
        lax.rem(place[0] - s // side + side, side),
        lax.rem(place[1] - s % side + side, side),
    )


def deep_distance(grid, place, b):
    return lax.rem(place[2] - b // 2 + grid.depth, grid.depth)


def spot_of(grid, place, s, b):
    rh, rl = near_distance(grid, place, s)
    rz = deep_distance(grid, place, b)
    second = rz >= grid.half
    return (
        jnp.where(second, 1, 0),
        jnp.where(second, rl, rh),
        jnp.where(second, rh, rl),
        jnp.where(second, rz - grid.half, rz),
    )


def distance(grid, place, s, b):
    return (jnp.where(place[3] == b % 2, 0, 1),) + spot_of(grid, place, s, b)


class Order:
    def __init__(self, grid, hidden):
        self.grid, self.hidden = grid, hidden
        self.hl, self.hb = hidden // grid.seq, hidden // grid.batch
        self.main = self.hl // 128 * 128
        self.rest = self.hl - self.main

    def runs(self, first, count):
        found = []
        at = first
        while at < first + count:
            block, r = at // self.hl, at % self.hl
            if r < self.main:
                length = min(self.main - r, first + count - at)
                place = block * self.main + r
            else:
                length = min(self.hl - r, first + count - at)
                place = self.grid.seq * self.main + block * self.rest + r - self.main
            if found and found[-1][1] + found[-1][2] == place:
                found[-1] = (found[-1][0], found[-1][1], found[-1][2] + length)
            else:
                found.append((at - first, place, length))
            at += length
        return found


def join(parts):
    return parts[0] if len(parts) == 1 else jnp.concatenate(parts, axis=1)


def wire_from_rows(order, row_blocks):
    main, rest, seq = order.main, order.rest, order.grid.seq
    pieces = []
    for s in range(seq):
        parts = [block[:, s * main : (s + 1) * main] for block in row_blocks if main]
        if rest:
            at = seq * main + s * rest
            parts += [block[:, at : at + rest] for block in row_blocks]
        pieces.append(join(parts))
    return pieces


def rows_from_wire(order, pieces, count, j):
    main, rest = order.main, order.rest
    parts = [piece[:, j * main : (j + 1) * main] for piece in pieces if main]
    if rest:
        at = count * main + j * rest
        parts += [piece[:, at : at + rest] for piece in pieces]
    return join(parts)


def stage_copies(place, side, parts, stage, sems):
    copies = []
    for index, part in enumerate(parts):
        mine = index < 2 * side
        core = place[3] if mine else 1 - place[3]
        half, far = index // side % 2, index % side
        copies.append(pltpu.make_async_copy(part, stage.at[core, half, far], sems.at[index]))
    for copy in copies:
        copy.start()
    return copies


def staged(grid, place, stage, s, b):
    return stage[(b % 2,) + spot_of(grid, place, s, b)]


def hand_out(pieces, parts, sems):
    copies = [
        pltpu.make_async_copy(pieces.at[index // 2, index % 2], part, sems.at[index])
        for index, part in enumerate(parts)
    ]
    for copy in copies:
        copy.start()
    for copy in copies:
        copy.wait()


def piece_shape(grid, rows, lanes):
    return (grid.side, grid.side, grid.half, rows, lanes)


def normed(values):
    center = values - jnp.mean(values, axis=-1, keepdims=True)
    spread = jnp.mean(center * center, axis=-1, keepdims=True)
    inverse = lax.rsqrt(spread + EPSILON)
    return center * inverse, inverse


def scaled(unit, gain, shift):
    return unit * (gain * ROOT_HALF) + shift * ROOT_HALF


def gelu(x):
    return (x * ROOT_HALF) * (1.0 + lax.erf(x))


def gelu_both(x):
    twice = 1.0 + lax.erf(x)
    return (x * ROOT_HALF) * twice, twice + (x * SLOPE) * jnp.exp2((x * LOG) * x)


def back_rows(twice_q, gain, unit, inverse):
    share = 1.0 / unit.shape[-1]
    half = gain * 0.5
    product = twice_q * unit
    weighted = twice_q * half
    first = jnp.sum(weighted, axis=-1, keepdims=True) * share
    second = jnp.sum(product * half, axis=-1, keepdims=True) * share
    return (weighted - first - unit * second) * inverse, product


def row_sum(values):
    return jnp.sum(values, axis=0, keepdims=True)


def dot_nn(left, right):
    return lax.dot_general(left, right, (((1,), (0,)), ((), ())), preferred_element_type=F32)


def dot_nt(left, right):
    return lax.dot_general(left, right, (((1,), (1,)), ((), ())), preferred_element_type=F32)


def dot_tn(left, right):
    return lax.dot_general(left, right, (((0,), (0,)), ((), ())), preferred_element_type=F32)


def group_of(count):
    return GROUP if count % GROUP == 0 else 1


def valid_rows(start_ref, length_ref, group, span):
    position = start_ref[0] + lax.broadcasted_iota(jnp.int32, (span, 1), 0)
    first = pl.program_id(0) * group
    return jnp.concatenate(
        [(position < length_ref[first + g]).astype(F32) for g in range(group)], axis=0
    )


def params(limit):
    return pltpu.CompilerParams(
        dimension_semantics=("arbitrary",), vmem_limit_bytes=limit * MIB
    )


def cost(flops, bytes_accessed, transcendentals=0):
    return pl.CostEstimate(
        flops=flops, bytes_accessed=bytes_accessed, transcendentals=transcendentals
    )


def whole(shape):
    return pl.BlockSpec(shape, lambda i, *_: (0,) * len(shape))


def rows_of(block):
    return pl.BlockSpec(block, lambda i, *_: (i,) + (0,) * (len(block) - 1))


def sds(shape, kind):
    return jax.ShapeDtypeStruct(shape, kind)


def pack_first_kernel(order, down, *refs):
    values, first = refs[:-1], refs[-1]
    hb, dl = down.shape
    first[0:hb] = down[...]
    sub = lax.broadcasted_iota(jnp.int32, (16, dl), 0)
    tail = jnp.zeros((16, dl), F32)
    for row, ref in enumerate(values):
        value = ref[...].astype(F32).reshape(1, -1)
        if value.shape[1] < dl:
            value = join([value, jnp.zeros((1, dl - value.shape[1]), F32)])
        tail = tail + jnp.where(sub == row, value, 0.0)
    first[hb : hb + 16] = tail.astype(BF)


def pack_first(order, down, values):
    hb, dl = down.shape
    return pl.pallas_call(
        functools.partial(pack_first_kernel, order),
        out_shape=sds((hb + 16, dl), BF),
        grid=(1,),
        in_specs=[whole(down.shape)] + [whole(value.shape) for value in values],
        out_specs=whole((hb + 16, dl)),
        compiler_params=params(60),
        cost_estimate=cost(0, 4 * hb * dl),
        name="pack_first",
    )(down, *values)


def pack_second_kernel(order, conv, up, second):
    hb, taps = order.hb, conv.shape[0]
    fold = up.shape[1] // hb
    blocks = [conv[k].astype(F32).T.astype(BF) for k in range(taps)]
    turned = up[...].astype(F32).T.astype(BF)
    blocks += [turned[f * hb : (f + 1) * hb] for f in range(fold)]
    parts = [block[:, : order.main] for block in blocks if order.main]
    if order.rest:
        parts += [block[:, order.main :] for block in blocks]
    second[...] = join(parts)


def pack_second(order, conv, up):
    hb = order.hb
    blocks = conv.shape[0] + up.shape[1] // hb
    return pl.pallas_call(
        functools.partial(pack_second_kernel, order),
        out_shape=sds((hb, blocks * order.hl), BF),
        grid=(1,),
        in_specs=[whole(conv.shape), whole(up.shape)],
        out_specs=whole((hb, blocks * order.hl)),
        compiler_params=params(60),
        cost_estimate=cost(0, 4 * hb * blocks * order.hl),
        name="pack_second",
    )(conv, up)


def unpack_rest_kernel(order, taps, *refs):
    terms, (conv, up) = refs[:-2], refs[-2:]
    hb = order.hb
    fold = up.shape[1] // hb
    total = add_up([term[...] for term in terms], F32)
    for j in range(taps + fold):
        block = rows_from_wire(order, [total], taps + fold, j).T
        if j < taps:
            conv[j] = block
        else:
            up[:, (j - taps) * hb : (j - taps + 1) * hb] = block


def unpack_rest(order, taps, fold, terms):
    return pl.pallas_call(
        functools.partial(unpack_rest_kernel, order, taps),
        out_shape=(
            sds((taps, order.hl, order.hb), F32),
            sds((order.hl, fold * order.hb), F32),
        ),
        compiler_params=pltpu.CompilerParams(vmem_limit_bytes=16 * MIB),
        cost_estimate=cost(0, 8 * (taps + fold) * order.hl * order.hb),
        name="unpack_rest",
    )(*terms)


def unpack_first_kernel(order, *refs):
    terms, (down, tail) = refs[:-2], refs[-2:]
    hb = order.hb
    total = add_up([term[...] for term in terms], F32)
    down[...] = total[0:hb]
    tail[...] = total[hb : hb + 16]


def unpack_first(order, terms):
    dl = terms[0].shape[1]
    return pl.pallas_call(
        functools.partial(unpack_first_kernel, order),
        out_shape=(sds((order.hb, dl), F32), sds((16, dl), F32)),
        compiler_params=pltpu.CompilerParams(vmem_limit_bytes=16 * MIB),
        cost_estimate=cost(0, 8 * dl * order.hb),
        name="unpack_first",
    )(*terms)


def stage_one_kernel(
    grid, order, place, start_ref, length_ref, tokens, *refs
):
    parts, refs = refs[: 4 * grid.side], refs[4 * grid.side :]
    hidden_one, narrow, conv_input, down_t, table, stage, sems = refs
    model = tokens.shape[2]
    hidden = narrow.shape[2]
    hb, dl = order.hb, model // grid.seq

    @pl.when(pl.program_id(0) == 0)
    def _():
        copies = stage_copies(place, grid.side, parts, stage, sems)
        for copy in copies:
            copy.wait()
        table[...] = jnp.zeros_like(table)
        for b in range(grid.batch):
            pieces = [staged(grid, place, stage, s, b) for s in range(grid.seq)]
            block = join([piece[0:hb] for piece in pieces])
            for offset, spot, length in order.runs(b * hb, hb):
                down_t[spot : spot + length] = block[offset : offset + length]
            tail = pieces[0][hb : hb + 16].astype(F32)
            wide = model // grid.batch
            table[0:WIDE_ROWS, b * wide : (b + 1) * wide] = tail[0:WIDE_ROWS, 0:wide]
            for offset, spot, length in order.runs(b * hb, hb):
                table[WIDE_ROWS:TABLE_ROWS, spot : spot + length] = tail[
                    WIDE_ROWS:TABLE_ROWS, offset : offset + length
                ]

    def vec(name, width):
        return table[ROW[name] : ROW[name] + 1, 0:width]

    group, span = tokens.shape[0], tokens.shape[1]
    unit, _ = normed(tokens[...].reshape(group * span, model).astype(F32))
    one = gelu(scaled(unit, vec("first_gain", model), vec("first_shift", model))).astype(BF)
    hidden_one[...] = one.reshape(group, span, model)
    values = dot_nt(one, down_t[...]) + vec("down_bias", hidden)
    narrow[...] = values.reshape(group, span, hidden)
    unit, _ = normed(values)
    active = gelu(scaled(unit, vec("middle_gain", hidden), vec("middle_shift", hidden)))
    valid = valid_rows(start_ref, length_ref, group, span)
    conv_input[...] = (active * valid).astype(BF).reshape(group, span, hidden)


def stage_one(grid, order, place, start, lengths, tokens, parts):
    count, span, model = tokens.shape
    hidden = order.hidden
    group = group_of(count)
    rows, lanes = parts[0].shape[-2:]
    return pl.pallas_call(
        functools.partial(stage_one_kernel, grid, order),
        out_shape=(
            sds((count, span, model), BF),
            sds((count, span, hidden), F32),
            sds((count, span, hidden), BF),
            sds((hidden, model), BF),
            sds((TABLE_ROWS, model), F32),
        ),
        grid_spec=pltpu.PrefetchScalarGridSpec(
            num_scalar_prefetch=3,
            grid=(count // group,),
            in_specs=[rows_of((group, span, model))]
            + [pl.BlockSpec(memory_space=pl.ANY)] * len(parts),
            out_specs=[
                rows_of((group, span, model)),
                rows_of((group, span, hidden)),
                rows_of((group, span, hidden)),
                whole((hidden, model)),
                whole((TABLE_ROWS, model)),
            ],
            scratch_shapes=[
                pltpu.VMEM((2, 2) + piece_shape(grid, rows, lanes), BF),
                pltpu.SemaphoreType.DMA((len(parts),)),
            ],
        ),
        compiler_params=params(54),
        cost_estimate=cost(
            2 * count * span * model * hidden, count * span * (4 * model + 6 * hidden)
        ),
        name="stage_one",
    )(place, start, lengths, tokens, *parts)


def fill_padded(padded, left, body, right):
    reach = left.shape[0]
    span = body.shape[0]
    padded[0:reach] = left
    padded[reach : reach + span] = body
    padded[reach + span : 2 * reach + span] = right


def tap_windows(padded, taps, span):
    group, _, hidden = padded.shape
    return [
        padded[:, k * DILATION : k * DILATION + span].reshape(group * span, hidden) for k in taps
    ]


def edge_windows(left, right, taps):
    count, reach, hidden = left.shape
    zeros = jnp.zeros((count, reach, hidden), BF)
    before = jnp.concatenate([left, zeros], axis=1)
    after_run = jnp.concatenate([zeros, right], axis=1)
    middle = taps // 2

    def window(rows, at):
        return rows[:, at : at + reach].reshape(count * reach, hidden)

    return (
        [window(before, k * DILATION) for k in range(middle)],
        [window(after_run, (k - middle) * DILATION) for k in range(middle + 1, taps)],
    )


def add_edges(part, edges):
    group, span, hidden = part.shape
    reach = edges.shape[1] // 2
    rows = [part[:, 0:reach] + edges[:, 0:reach]]
    if span > 2 * reach:
        rows.append(part[:, reach : span - reach])
    rows.append(part[:, span - reach : span] + edges[:, reach : 2 * reach])
    return jnp.concatenate(rows, axis=1).reshape(group * span, hidden)


def inner_kernel(
    grid, order, taps, place, cotangent, conv_input, *refs
):
    parts, refs = refs[: 4 * grid.side], refs[4 * grid.side :]
    part, error, conv_t, up_out, conv_f, up_t, padded, stage, sems, out_sems = refs
    group, span, model = cotangent.shape
    hidden = conv_input.shape[2]
    reach = (padded.shape[1] - span) // 2
    hb = order.hb
    fold = model // hidden

    def weight_copies():
        return [
            pltpu.make_async_copy(
                conv_f.at[:, k * hidden : (k + 1) * hidden], conv_t.at[k], out_sems.at[k]
            )
            for k in range(taps)
        ] + [pltpu.make_async_copy(up_t, up_out, out_sems.at[taps])]

    @pl.when(pl.program_id(0) == 0)
    def _():
        copies = stage_copies(place, grid.side, parts, stage, sems)
        padded[:, 0:reach] = jnp.zeros((group, reach, hidden), BF)
        padded[:, reach + span : 2 * reach + span] = jnp.zeros((group, reach, hidden), BF)
        for copy in copies:
            copy.wait()
        for b in range(grid.batch):
            wires = [staged(grid, place, stage, s, b) for s in range(grid.seq)]
            for k in range(taps):
                block = rows_from_wire(order, wires, taps + fold, k)
                for offset, spot, length in order.runs(b * hb, hb):
                    conv_f[spot : spot + length, k * hidden : (k + 1) * hidden] = block[
                        offset : offset + length
                    ]
            for f in range(fold):
                row = (b * fold + f) * hb
                up_t[row : row + hb] = rows_from_wire(order, wires, taps + fold, taps + f)
        for copy in weight_copies():
            copy.start()

    padded[:, reach : reach + span] = conv_input[...]
    windows = join(tap_windows(padded, range(taps), span))
    part[...] = dot_nt(windows, conv_f[...]).reshape(group, span, hidden)
    incoming = cotangent[...].reshape(group * span, model)
    error[...] = dot_nn(incoming, up_t[...]).reshape(group, span, hidden)

    @pl.when(pl.program_id(0) == pl.num_programs(0) - 1)
    def _():
        for copy in weight_copies():
            copy.wait()


def inner(grid, order, taps, reach, place, cotangent, conv_input, parts):
    count, span, model = cotangent.shape
    hidden = order.hidden
    group = group_of(count)
    rows, lanes = parts[0].shape[-2:]
    return pl.pallas_call(
        functools.partial(inner_kernel, grid, order, taps),
        out_shape=(
            sds((count, span, hidden), F32),
            sds((count, span, hidden), F32),
            sds((taps, hidden, hidden), BF),
            sds((model, hidden), BF),
        ),
        grid_spec=pltpu.PrefetchScalarGridSpec(
            num_scalar_prefetch=1,
            grid=(count // group,),
            in_specs=[rows_of((group, span, model)), rows_of((group, span, hidden))]
            + [pl.BlockSpec(memory_space=pl.ANY)] * len(parts),
            out_specs=[
                rows_of((group, span, hidden)),
                rows_of((group, span, hidden)),
                pl.BlockSpec(memory_space=pl.ANY),
                pl.BlockSpec(memory_space=pl.ANY),
            ],
            scratch_shapes=[
                pltpu.VMEM((hidden, taps * hidden), BF),
                pltpu.VMEM((model, hidden), BF),
                pltpu.VMEM((group, span + 2 * reach, hidden), BF),
                pltpu.VMEM((2, 2) + piece_shape(grid, rows, lanes), BF),
                pltpu.SemaphoreType.DMA((len(parts),)),
                pltpu.SemaphoreType.DMA((taps + 1,)),
            ],
        ),
        compiler_params=params(LIM2P),
        cost_estimate=cost(
            2 * count * span * hidden * (taps * hidden + model),
            count * span * (2 * model + 10 * hidden),
        ),
        name="inner",
    )(place, cotangent, conv_input, *parts)


def stage_two_kernel(
    grid, order, taps, place, tokens, cotangent, conv_input, left, right, part, error, table,
    conv_t, up_t,
    output, conv_out_grad, sums, part_a, part_b, part_c, part_d,
    padded, threes, edges, total, conv_total, pieces, out_sems,
):
    group, span, model = tokens.shape
    hidden = conv_input.shape[2]
    reach = left.shape[1]
    count = left.shape[0]
    size = group * span
    hb = order.hb
    fold = model // hidden
    step = pl.program_id(0)

    def vec(name, width):
        return table[ROW[name] : ROW[name] + 1, 0:width]

    def add(name, values, factor=1.0):
        width = values.shape[1]
        sums[ROW[name] : ROW[name] + 1, 0:width] += row_sum(values) * factor

    @pl.when(step == 0)
    def _():
        sums[...] = jnp.zeros_like(sums)
        total[...] = jnp.zeros_like(total)
        conv_total[...] = jnp.zeros_like(conv_total)
        before, behind = edge_windows(left[...], right[...], taps)
        for at, windows, first in ((0, before, 0), (reach, behind, taps // 2 + 1)):
            term = None
            for k, window in enumerate(windows):
                product = dot_nt(window, conv_t[first + k])
                term = product if term is None else term + product
            edges[:, at : at + reach] = term.reshape(count, reach, hidden)

    for g in range(group):
        at = step * group + g
        fill_padded(padded.at[g], left[at], conv_input[g], right[at])
    values = add_edges(part[...], edges[pl.ds(step * group, group)]) + vec("conv_bias", hidden)
    unit, inverse = normed(values)
    gain = vec("final_gain", hidden)
    three, slope = gelu_both(scaled(unit, gain, vec("final_shift", hidden)))
    threes[...] = three.astype(BF)
    incoming = cotangent[...].reshape(size, model)
    result = tokens[...].reshape(size, model).astype(F32) + dot_nt(threes[...], up_t[...])
    output[...] = (result + vec("up_bias", model)).astype(BF).reshape(group, span, model)
    twice = error[...].reshape(size, hidden) * slope
    grad, product = back_rows(twice, gain, unit, inverse)
    grad = grad.astype(BF)
    conv_out_grad[...] = grad.reshape(group, span, hidden)
    add("final_gain", product, 0.5)
    add("final_shift", twice, 0.5)
    add("conv_bias", grad.astype(F32))
    add("up_bias", incoming.astype(F32))
    total[...] += dot_tn(incoming, threes[...])
    windows = join(tap_windows(padded, range(taps), span))
    conv_total[...] += dot_nn(conv_out_grad[...].reshape(size, hidden).T, windows)

    @pl.when(step == pl.num_programs(0) - 1)
    def _():
        for b in range(grid.batch):
            for offset, spot, length in order.runs(b * hb, hb):
                rows = [
                    conv_total[spot : spot + length, k * hidden : (k + 1) * hidden].astype(BF)
                    for k in range(taps)
                ]
                for f in range(fold):
                    at = (b * fold + f) * hb + offset
                    rows.append(total[at : at + length].astype(BF))
                for s, piece in enumerate(wire_from_rows(order, rows)):
                    pieces[distance(grid, place, s, b) + (pl.ds(offset, length),)] = piece
        hand_out(pieces, (part_a, part_b, part_c, part_d), out_sems)


def stage_two(
    grid, order, taps, place, tokens, cotangent, conv_input, left, right, part, error, table,
    conv_t, up_t,
):
    count, span, model = tokens.shape
    hidden = conv_input.shape[2]
    reach = left.shape[1]
    group = group_of(count)
    fold = model // hidden
    pieces = piece_shape(grid, order.hb, (taps + fold) * order.hl)
    return pl.pallas_call(
        functools.partial(stage_two_kernel, grid, order, taps),
        out_shape=(
            sds((count, span, model), BF),
            sds((count, span, hidden), BF),
            sds((TABLE_ROWS, model), F32),
            *[sds(pieces, BF)] * 4,
        ),
        grid_spec=pltpu.PrefetchScalarGridSpec(
            num_scalar_prefetch=1,
            grid=(count // group,),
            in_specs=[
                rows_of((group, span, model)),
                rows_of((group, span, model)),
                rows_of((group, span, hidden)),
                whole((count, reach, hidden)),
                whole((count, reach, hidden)),
                rows_of((group, span, hidden)),
                rows_of((group, span, hidden)),
                whole(table.shape),
                whole(conv_t.shape),
                whole(up_t.shape),
            ],
            out_specs=[
                rows_of((group, span, model)),
                rows_of((group, span, hidden)),
                whole((TABLE_ROWS, model)),
                *[pl.BlockSpec(memory_space=pl.ANY)] * 4,
            ],
            scratch_shapes=[
                pltpu.VMEM((group, span + 2 * reach, hidden), BF),
                pltpu.VMEM((group * span, hidden), BF),
                pltpu.VMEM((count, 2 * reach, hidden), F32),
                pltpu.VMEM((model, hidden), F32),
                pltpu.VMEM((hidden, taps * hidden), F32),
                pltpu.VMEM((2, 2) + pieces, BF),
                pltpu.SemaphoreType.DMA((4,)),
            ],
        ),
        compiler_params=params(LIM2),
        cost_estimate=cost(
            2 * count * span * hidden * (taps * hidden + 2 * model),
            count * span * (6 * model + 12 * hidden),
        ),
        name="stage_two",
    )(
        place, tokens, cotangent, conv_input, left, right, part, error, table, conv_t, up_t,
    )


def inner_back_kernel(conv_out_grad, conv_t, part, padded):
    group, span, hidden = conv_out_grad.shape
    taps = conv_t.shape[0]
    reach = (padded.shape[1] - span) // 2

    @pl.when(pl.program_id(0) == 0)
    def _():
        padded[:, 0:reach] = jnp.zeros((group, reach, hidden), BF)
        padded[:, reach + span : 2 * reach + span] = jnp.zeros((group, reach, hidden), BF)

    padded[:, reach : reach + span] = conv_out_grad[...]
    windows = join(tap_windows(padded, reversed(range(taps)), span))
    part[...] = dot_nn(windows, conv_t[...].reshape(taps * hidden, hidden)).reshape(
        group, span, hidden
    )


def inner_back(conv_out_grad, conv_t, reach):
    count, span, hidden = conv_out_grad.shape
    taps = conv_t.shape[0]
    group = group_of(count)
    return pl.pallas_call(
        inner_back_kernel,
        out_shape=sds((count, span, hidden), F32),
        grid=(count // group,),
        in_specs=[rows_of((group, span, hidden)), whole(conv_t.shape)],
        out_specs=rows_of((group, span, hidden)),
        scratch_shapes=[pltpu.VMEM((group, span + 2 * reach, hidden), BF)],
        compiler_params=params(LIM3P),
        cost_estimate=cost(2 * count * span * hidden * taps * hidden, count * span * 6 * hidden),
        name="inner_back",
    )(conv_out_grad, conv_t)


def stage_three_kernel(
    start_ref, length_ref, part, narrow, left, right, table, sums_in, conv_t,
    narrow_grad, sums, edges,
):
    group, span, hidden = narrow.shape
    count, reach = left.shape[0], left.shape[1]
    taps = conv_t.shape[0]
    step = pl.program_id(0)

    def vec(name, width):
        return table[ROW[name] : ROW[name] + 1, 0:width]

    def add(name, values, factor=1.0):
        width = values.shape[1]
        sums[ROW[name] : ROW[name] + 1, 0:width] += row_sum(values) * factor

    @pl.when(step == 0)
    def _():
        sums[...] = sums_in[...]
        before, behind = edge_windows(left[...], right[...], taps)
        for at, windows, first in ((0, before, 0), (reach, behind, taps // 2 + 1)):
            term = None
            for k, window in enumerate(windows):
                product = dot_nn(window, conv_t[taps - 1 - first - k])
                term = product if term is None else term + product
            edges[:, at : at + reach] = term.reshape(count, reach, hidden)

    back = add_edges(part[...], edges[pl.ds(step * group, group)])
    back = back * valid_rows(start_ref, length_ref, group, span)
    unit, inverse = normed(narrow[...].reshape(group * span, hidden))
    gain = vec("middle_gain", hidden)
    _, slope = gelu_both(scaled(unit, gain, vec("middle_shift", hidden)))
    twice = back * slope
    low, product = back_rows(twice, gain, unit, inverse)
    low = low.astype(BF)
    narrow_grad[...] = low.reshape(group, span, hidden)
    add("middle_gain", product, 0.5)
    add("middle_shift", twice, 0.5)
    add("down_bias", low.astype(F32))


def stage_three(start, lengths, part, narrow, left, right, table, sums, conv_t):
    count, span, hidden = narrow.shape
    reach = left.shape[1]
    group = group_of(count)
    return pl.pallas_call(
        stage_three_kernel,
        out_shape=(sds((count, span, hidden), BF), sds(sums.shape, F32)),
        grid_spec=pltpu.PrefetchScalarGridSpec(
            num_scalar_prefetch=2,
            grid=(count // group,),
            in_specs=[
                rows_of((group, span, hidden)),
                rows_of((group, span, hidden)),
                whole((count, reach, hidden)),
                whole((count, reach, hidden)),
                whole(table.shape),
                whole(table.shape),
                whole(conv_t.shape),
            ],
            out_specs=[rows_of((group, span, hidden)), whole(sums.shape)],
            scratch_shapes=[pltpu.VMEM((count, 2 * reach, hidden), F32)],
        ),
        compiler_params=params(LIM3),
        cost_estimate=cost(2 * count * span * hidden * hidden, count * span * 10 * hidden),
        name="stage_three",
    )(start, lengths, part, narrow, left, right, table, sums, conv_t)


def stage_four_kernel(
    grid, order, last, begin, place, tokens, cotangent, hidden_one, narrow_grad, table, sums_in,
    down_t, *refs,
):
    if begin:
        grad_in, total_in = None, None
    else:
        grad_in, total_in, refs = refs[0], refs[1], refs[2:]
    tokens_grad, sums, total = refs[:3]
    model = tokens.shape[2]
    hidden = narrow_grad.shape[2]
    hb, dl = order.hb, model // grid.seq

    def vec(name, width):
        return table[ROW[name] : ROW[name] + 1, 0:width]

    def add(name, values, factor=1.0):
        width = values.shape[1]
        sums[ROW[name] : ROW[name] + 1, 0:width] += row_sum(values) * factor

    @pl.when(pl.program_id(0) == 0)
    def _():
        sums[...] = sums_in[...]
        total[...] = jnp.zeros_like(total) if begin else total_in[...]

    group, span = tokens.shape[0], tokens.shape[1]
    size = group * span
    low = narrow_grad[...].reshape(size, hidden)
    total[...] += dot_tn(low, hidden_one[...].reshape(size, model))
    deep = dot_nn(low, down_t[...])
    unit, inverse = normed(tokens[...].reshape(size, model).astype(F32))
    gain = vec("first_gain", model)
    _, slope = gelu_both(scaled(unit, gain, vec("first_shift", model)))
    twice = deep * slope
    grad, product = back_rows(twice, gain, unit, inverse)
    add("first_gain", product, 0.5)
    add("first_shift", twice, 0.5)
    grad = grad + cotangent[...].reshape(size, model).astype(F32)
    tokens_grad[...] = grad.astype(BF).reshape(group, span, model)

    if last:
        part_a, part_b, part_c, part_d, pieces, out_sems = refs[3:]

        @pl.when(pl.program_id(0) == pl.num_programs(0) - 1)
        def _():
            wide = model // grid.batch
            sub = lax.broadcasted_iota(jnp.int32, (TABLE_ROWS, dl), 0)
            for b in range(grid.batch):
                upper = sums[:, b * wide : (b + 1) * wide]
                lower = join(
                    [
                        sums[:, spot : spot + length]
                        for _, spot, length in order.runs(b * hb, hb)
                    ]
                )
                if wide < dl:
                    upper = join([upper, jnp.zeros((TABLE_ROWS, dl - wide), F32)])
                lower = join([lower, jnp.zeros((TABLE_ROWS, dl - hb), F32)])
                tail = jnp.where(sub < WIDE_ROWS, upper, lower)
                tail = tail.astype(BF)
                for s in range(grid.seq):
                    to = distance(grid, place, s, b)
                    for offset, spot, length in order.runs(b * hb, hb):
                        pieces[to + (pl.ds(offset, length),)] = total[
                            spot : spot + length, s * dl : (s + 1) * dl
                        ].astype(BF)
                    pieces[to + (pl.ds(hb, 16),)] = tail
            hand_out(pieces, (part_a, part_b, part_c, part_d), out_sems)


def stage_four(
    grid, order, first, part, begin, last, place, tokens, cotangent, hidden_one, narrow_grad,
    table, sums, down_t, grad_in, total_in,
):
    count, span, model = tokens.shape
    hidden = narrow_grad.shape[2]
    group = group_of(part)
    pieces = piece_shape(grid, order.hb + 16, model // grid.seq)

    def part_of(block):
        return pl.BlockSpec(block, lambda i, *_: (first // group + i,) + (0,) * (len(block) - 1))

    in_specs = [
        part_of((group, span, model)),
        part_of((group, span, model)),
        part_of((group, span, model)),
        part_of((group, span, hidden)),
        whole(table.shape),
        whole(table.shape),
        whole(down_t.shape),
    ]
    inputs = [tokens, cotangent, hidden_one, narrow_grad, table, sums, down_t]
    aliases = {}
    if not begin:
        in_specs += [pl.BlockSpec(memory_space=pl.ANY), whole((hidden, model))]
        inputs += [grad_in, total_in]
        aliases = {8: 0}
    out_shape = [
        sds((count, span, model), BF),
        sds(table.shape, F32),
        sds((hidden, model), F32),
    ]
    out_specs = [part_of((group, span, model)), whole(table.shape), whole((hidden, model))]
    scratch = []
    if last:
        out_shape += [sds(pieces, BF)] * 4
        out_specs += [pl.BlockSpec(memory_space=pl.ANY)] * 4
        scratch = [pltpu.VMEM((2, 2) + pieces, BF), pltpu.SemaphoreType.DMA((4,))]
    return pl.pallas_call(
        functools.partial(stage_four_kernel, grid, order, last, begin),
        out_shape=tuple(out_shape),
        grid_spec=pltpu.PrefetchScalarGridSpec(
            num_scalar_prefetch=1,
            grid=(part // group,),
            in_specs=in_specs,
            out_specs=out_specs,
            scratch_shapes=scratch,
        ),
        input_output_aliases=aliases,
        compiler_params=params(LIM4),
        cost_estimate=cost(
            4 * part * span * hidden * model, part * span * (8 * model + 2 * hidden)
        ),
        name="stage_four",
    )(place, *inputs)


def halos(cells, reach):
    count = lax.axis_size("seq")
    left = lax.ppermute(
        cells[:, cells.shape[1] - reach :], "seq", [(i, i + 1) for i in range(count - 1)]
    )
    right = lax.ppermute(cells[:, :reach], "seq", [(i + 1, i) for i in range(count - 1)])
    return left, right


def after(value, *others):
    return lax.optimization_barrier((value,) + others)[0]


def body(
    grid,
    tokens,
    lengths,
    first_gain,
    first_shift,
    down_weight,
    down_bias,
    middle_gain,
    middle_shift,
    conv_weight,
    conv_bias,
    final_gain,
    final_shift,
    up_weight,
    up_bias,
    cotangent,
):
    shape = tokens.shape
    span, model = shape[2], shape[3]
    count = shape[0] * shape[1]
    taps = conv_weight.shape[0]
    hidden = down_weight.shape[1] * grid.batch
    order = Order(grid, hidden)
    hb, hl, dl = order.hb, order.hl, down_weight.shape[0]
    fold = model // hidden
    reach = (taps - 1) // 2 * DILATION

    tokens = tokens.reshape(count, span, model)
    cotangent = cotangent.reshape(count, span, model)
    lengths = lengths.reshape(count)
    place = jnp.stack(grid.here()).astype(jnp.int32)
    start = (lax.axis_index("seq") * span).astype(jnp.int32).reshape(1)

    vectors = {
        "first_gain": first_gain,
        "first_shift": first_shift,
        "up_bias": up_bias,
        "down_bias": down_bias,
        "middle_gain": middle_gain,
        "middle_shift": middle_shift,
        "conv_bias": conv_bias,
        "final_gain": final_gain,
        "final_shift": final_shift,
    }
    first_piece = pack_first(order, down_weight.T, [vectors[name] for name in WIDE + NARROW])
    second_piece = pack_second(order, after(conv_weight, first_piece), up_weight)

    def meet(*groups):
        flat = lax.optimization_barrier(tuple(value for group in groups for value in group))
        found, at = [], 0
        for group in groups:
            found.append(flat[at : at + len(group)])
            at += len(group)
        return found

    first = grid.gather_deep(first_piece)
    neighbour, second_piece = lax.optimization_barrier((first[1], second_piece))
    first[1] = neighbour
    second = grid.halves(grid.gather_deep(second_piece))
    one, two = grid.gather_near(*grid.halves(first))
    far_one, far_two = grid.gather_far(one, two)
    first = [one, *far_one, two, *far_two]
    first, second = meet(first, second)
    first = [*first, *grid.gather_core(first)]
    near = grid.gather_near(*second)
    near, first = meet(near, first)
    near_other = grid.gather_core(near)
    far_one, far_two = grid.gather_far(*near)
    hidden_one, narrow, conv_input, down_t, table = stage_one(
        grid, order, place, start, lengths, tokens, first
    )
    far_one, far_two, near_other, (conv_input,) = meet(
        far_one, far_two, near_other, (conv_input,)
    )
    left, right = halos(conv_input, reach)
    far_one_other, far_two_other = grid.gather_core(far_one), grid.gather_core(far_two)
    second = [near[0], *far_one, near[1], *far_two]
    second += [near_other[0], *far_one_other, near_other[1], *far_two_other]
    part, error, conv_t, up_t = inner(
        grid, order, taps, reach, place, cotangent, conv_input, second
    )
    block_output, conv_out_grad, sums, *rest = stage_two(
        grid, order, taps, place, tokens, cotangent, conv_input, left, right, part, error, table,
        conv_t, up_t,
    )
    half = count // 2

    left, right = halos(conv_out_grad, reach)
    rest = grid.reduce_core(*rest)
    part = inner_back(conv_out_grad, conv_t, reach)
    rest, (sums, left, right, part) = meet(rest, (sums, left, right, part))

    rest = grid.reduce_far(*rest)
    narrow_grad, sums = stage_three(
        start, lengths, part, narrow, left, right, table, sums, conv_t
    )
    tokens_grad, sums, total = stage_four(
        grid, order, 0, half, True, False, place, tokens, cotangent, hidden_one, narrow_grad,
        table, sums, down_t, None, None,
    )
    rest, (sums,) = meet(rest, (sums,))

    rest = grid.reduce_near(*rest)
    tokens_grad, sums, total, *down = stage_four(
        grid, order, half, half, False, True, place, tokens, cotangent, hidden_one, narrow_grad,
        table, sums, down_t, tokens_grad, total,
    )
    rest, down = meet(rest, down)

    down = grid.reduce_core(*down)
    down, rest = meet(down, rest)
    down = grid.reduce_far(*down)
    rest = grid.reduce_deep(*rest)
    down = grid.reduce_near(*down)
    rest, down = meet(rest, down)
    down = grid.reduce_deep(*down)
    conv_grad, up_grad = unpack_rest(order, taps, fold, rest)
    down_grad, tail = unpack_first(order, down)
    grads = {name: tail[ROW[name], : vectors[name].shape[0]] for name in vectors}
    return (
        block_output.reshape(shape),
        tokens_grad.reshape(shape),
        grads["first_gain"],
        grads["first_shift"],
        down_grad.T,
        grads["down_bias"],
        grads["middle_gain"],
        grads["middle_shift"],
        conv_grad,
        grads["conv_bias"],
        grads["final_gain"],
        grads["final_shift"],
        up_grad,
        grads["up_bias"],
    )


def solution(mesh):
    grid = Grid(mesh.shape["seq"], mesh.shape["batch"])
    return jax.shard_map(
        functools.partial(body, grid),
        mesh=mesh,
        in_specs=(
            P(None, "batch", "seq", None),
            P(None, "batch"),
            P("batch"),
            P("batch"),
            P("seq", "batch"),
            P("batch"),
            P("batch"),
            P("batch"),
            P(None, "seq", "batch"),
            P("batch"),
            P("batch"),
            P("batch"),
            P("seq", "batch"),
            P("batch"),
            P(None, "batch", "seq", None),
        ),
        out_specs=(
            P(None, "batch", "seq", None),
            P(None, "batch", "seq", None),
            P("batch"),
            P("batch"),
            P("seq", "batch"),
            P("batch"),
            P("batch"),
            P("batch"),
            P(None, "seq", "batch"),
            P("batch"),
            P("batch"),
            P("batch"),
            P("seq", "batch"),
            P("batch"),
        ),
        check_vma=False,
    )
```

```python
import functools
import math

import jax
import jax.numpy as jnp
from jax import lax
from jax.experimental import pallas as pl
from jax.experimental.pallas import tpu as pltpu
from jax.sharding import PartitionSpec as P

DILATION = 16
EPSILON = 1e-05
BF = jnp.bfloat16
F32 = jnp.float32
ROOT_HALF = math.sqrt(0.5)
SLOPE = 2.0 / math.sqrt(math.pi)
LOG = -math.log2(math.e)
MIB = 1 << 20
GROUP = 2
LIM2P = 60
LIM2 = 60
LIM3P = 56
LIM3 = 40
LIM4 = 48

WIDE = ("first_gain", "first_shift", "up_bias")
NARROW = ("down_bias", "middle_gain", "middle_shift", "conv_bias", "final_gain", "final_shift")
WIDE_ROWS = 3
ROW = {name: row for row, name in enumerate(WIDE + NARROW)}
TABLE_ROWS = 16


def add_up(terms, kind):
    total = terms[0].astype(F32)
    for term in terms[1:]:
        total = total + term.astype(F32)
    return total.astype(kind)


class Grid:
    def __init__(self, seq, batch):
        self.seq, self.batch = seq, batch
        self.side = math.isqrt(seq)
        assert self.side * self.side == seq
        self.depth = batch // 2
        self.half = self.depth // 2

    def here(self):
        s, b = lax.axis_index("seq"), lax.axis_index("batch")
        return s // self.side, s % self.side, b // 2, b % 2

    def send(self, value, move):
        pairs = []
        for s in range(self.seq):
            for b in range(self.batch):
                h, l, z, c = move(s // self.side, s % self.side, b // 2, b % 2)
                pairs.append((s * self.batch + b, (h * self.side + l) * self.batch + z * 2 + c))
        return lax.ppermute(value, ("seq", "batch"), pairs)

    def high(self, value, k):
        return self.send(value, lambda h, l, z, c: ((h + k) % self.side, l, z, c))

    def low(self, value, k):
        return self.send(value, lambda h, l, z, c: (h, (l + k) % self.side, z, c))

    def deep(self, value, k):
        return self.send(value, lambda h, l, z, c: (h, l, (z + k) % self.depth, c))

    def core(self, value):
        return self.send(value, lambda h, l, z, c: (h, l, z, 1 - c))

    def gather_deep(self, piece):
        return [piece] + [self.deep(piece, k) for k in range(1, self.depth)]

    def halves(self, column):
        return jnp.stack(column[: self.half]), jnp.stack(column[self.half :])

    def gather_near(self, one, two):
        one = jnp.stack([one] + [self.low(one, k) for k in range(1, self.side)])
        two = jnp.stack([two] + [self.high(two, k) for k in range(1, self.side)])
        return one, two

    def gather_far(self, one, two):
        return (
            [self.high(one, k) for k in range(1, self.side)],
            [self.low(two, k) for k in range(1, self.side)],
        )

    def gather_core(self, values):
        return [self.core(value) for value in values]

    def reduce_core(self, keep_one, keep_two, give_one, give_two):
        return (
            add_up([keep_one, self.core(give_one)], BF),
            add_up([keep_two, self.core(give_two)], BF),
        )

    def reduce_far(self, one, two):
        one = add_up([one[0]] + [self.high(one[k], -k) for k in range(1, self.side)], BF)
        two = add_up([two[0]] + [self.low(two[k], -k) for k in range(1, self.side)], BF)
        return one, two

    def reduce_near(self, one, two):
        one = add_up([one[0]] + [self.low(one[k], -k) for k in range(1, self.side)], BF)
        two = add_up([two[0]] + [self.high(two[k], -k) for k in range(1, self.side)], BF)
        return one, two

    def reduce_deep(self, one, two):
        column = [one[k] for k in range(self.half)] + [two[k] for k in range(self.half)]
        return (column[0],) + tuple(self.deep(column[k], -k) for k in range(1, self.depth))


def near_distance(grid, place, s):
    side = grid.side
    return (
        lax.rem(place[0] - s // side + side, side),
        lax.rem(place[1] - s % side + side, side),
    )


def deep_distance(grid, place, b):
    return lax.rem(place[2] - b // 2 + grid.depth, grid.depth)


def spot_of(grid, place, s, b):
    rh, rl = near_distance(grid, place, s)
    rz = deep_distance(grid, place, b)
    second = rz >= grid.half
    return (
        jnp.where(second, 1, 0),
        jnp.where(second, rl, rh),
        jnp.where(second, rh, rl),
        jnp.where(second, rz - grid.half, rz),
    )


def distance(grid, place, s, b):
    return (jnp.where(place[3] == b % 2, 0, 1),) + spot_of(grid, place, s, b)


class Order:
    def __init__(self, grid, hidden):
        self.grid, self.hidden = grid, hidden
        self.hl, self.hb = hidden // grid.seq, hidden // grid.batch
        self.main = self.hl // 128 * 128
        self.rest = self.hl - self.main

    def runs(self, first, count):
        found = []
        at = first
        while at < first + count:
            block, r = at // self.hl, at % self.hl
            if r < self.main:
                length = min(self.main - r, first + count - at)
                place = block * self.main + r
            else:
                length = min(self.hl - r, first + count - at)
                place = self.grid.seq * self.main + block * self.rest + r - self.main
            if found and found[-1][1] + found[-1][2] == place:
                found[-1] = (found[-1][0], found[-1][1], found[-1][2] + length)
            else:
                found.append((at - first, place, length))
            at += length
        return found


def join(parts):
    return parts[0] if len(parts) == 1 else jnp.concatenate(parts, axis=1)


def wire_from_rows(order, row_blocks):
    main, rest, seq = order.main, order.rest, order.grid.seq
    pieces = []
    for s in range(seq):
        parts = [block[:, s * main : (s + 1) * main] for block in row_blocks if main]
        if rest:
            at = seq * main + s * rest
            parts += [block[:, at : at + rest] for block in row_blocks]
        pieces.append(join(parts))
    return pieces


def rows_from_wire(order, pieces, count, j):
    main, rest = order.main, order.rest
    parts = [piece[:, j * main : (j + 1) * main] for piece in pieces if main]
    if rest:
        at = count * main + j * rest
        parts += [piece[:, at : at + rest] for piece in pieces]
    return join(parts)


def stage_copies(place, side, parts, stage, sems):
    copies = []
    for index, part in enumerate(parts):
        mine = index < 2 * side
        core = place[3] if mine else 1 - place[3]
        half, far = index // side % 2, index % side
        copies.append(pltpu.make_async_copy(part, stage.at[core, half, far], sems.at[index]))
    for copy in copies:
        copy.start()
    return copies


def staged(grid, place, stage, s, b):
    return stage[(b % 2,) + spot_of(grid, place, s, b)]


def hand_out(pieces, parts, sems):
    copies = [
        pltpu.make_async_copy(pieces.at[index // 2, index % 2], part, sems.at[index])
        for index, part in enumerate(parts)
    ]
    for copy in copies:
        copy.start()
    for copy in copies:
        copy.wait()


def piece_shape(grid, rows, lanes):
    return (grid.side, grid.side, grid.half, rows, lanes)


def normed(values):
    center = values - jnp.mean(values, axis=-1, keepdims=True)
    spread = jnp.mean(center * center, axis=-1, keepdims=True)
    inverse = lax.rsqrt(spread + EPSILON)
    return center * inverse, inverse


def scaled(unit, gain, shift):
    return unit * (gain * ROOT_HALF) + shift * ROOT_HALF


def gelu(x):
    return (x * ROOT_HALF) * (1.0 + lax.erf(x))


def gelu_both(x):
    twice = 1.0 + lax.erf(x)
    return (x * ROOT_HALF) * twice, twice + (x * SLOPE) * jnp.exp2((x * LOG) * x)


def back_rows(twice_q, gain, unit, inverse):
    share = 1.0 / unit.shape[-1]
    half = gain * 0.5
    product = twice_q * unit
    weighted = twice_q * half
    first = jnp.sum(weighted, axis=-1, keepdims=True) * share
    second = jnp.sum(product * half, axis=-1, keepdims=True) * share
    return (weighted - first - unit * second) * inverse, product


def row_sum(values):
    return jnp.sum(values, axis=0, keepdims=True)


def dot_nn(left, right):
    return lax.dot_general(left, right, (((1,), (0,)), ((), ())), preferred_element_type=F32)


def dot_nt(left, right):
    return lax.dot_general(left, right, (((1,), (1,)), ((), ())), preferred_element_type=F32)


def dot_tn(left, right):
    return lax.dot_general(left, right, (((0,), (0,)), ((), ())), preferred_element_type=F32)


def group_of(count):
    return GROUP if count % GROUP == 0 else 1


def valid_rows(start_ref, length_ref, group, span):
    position = start_ref[0] + lax.broadcasted_iota(jnp.int32, (span, 1), 0)
    first = pl.program_id(0) * group
    return jnp.concatenate(
        [(position < length_ref[first + g]).astype(F32) for g in range(group)], axis=0
    )


def params(limit):
    return pltpu.CompilerParams(
        dimension_semantics=("arbitrary",), vmem_limit_bytes=limit * MIB
    )


def cost(flops, bytes_accessed, transcendentals=0):
    return pl.CostEstimate(
        flops=flops, bytes_accessed=bytes_accessed, transcendentals=transcendentals
    )


def whole(shape):
    return pl.BlockSpec(shape, lambda i, *_: (0,) * len(shape))


def rows_of(block):
    return pl.BlockSpec(block, lambda i, *_: (i,) + (0,) * (len(block) - 1))


def sds(shape, kind):
    return jax.ShapeDtypeStruct(shape, kind)


def pack_first_kernel(order, down, *refs):
    values, first = refs[:-1], refs[-1]
    hb, dl = down.shape
    first[0:hb] = down[...]
    sub = lax.broadcasted_iota(jnp.int32, (16, dl), 0)
    tail = jnp.zeros((16, dl), F32)
    for row, ref in enumerate(values):
        value = ref[...].astype(F32).reshape(1, -1)
        if value.shape[1] < dl:
            value = join([value, jnp.zeros((1, dl - value.shape[1]), F32)])
        tail = tail + jnp.where(sub == row, value, 0.0)
    first[hb : hb + 16] = tail.astype(BF)


def pack_first(order, down, values):
    hb, dl = down.shape
    return pl.pallas_call(
        functools.partial(pack_first_kernel, order),
        out_shape=sds((hb + 16, dl), BF),
        grid=(1,),
        in_specs=[whole(down.shape)] + [whole(value.shape) for value in values],
        out_specs=whole((hb + 16, dl)),
        compiler_params=params(60),
        cost_estimate=cost(0, 4 * hb * dl),
        name="pack_first",
    )(down, *values)


def pack_second_kernel(order, conv, up, second):
    hb, taps = order.hb, conv.shape[0]
    fold = up.shape[1] // hb
    blocks = [conv[k].astype(F32).T.astype(BF) for k in range(taps)]
    turned = up[...].astype(F32).T.astype(BF)
    blocks += [turned[f * hb : (f + 1) * hb] for f in range(fold)]
    parts = [block[:, : order.main] for block in blocks if order.main]
    if order.rest:
        parts += [block[:, order.main :] for block in blocks]
    second[...] = join(parts)


def pack_second(order, conv, up):
    hb = order.hb
    blocks = conv.shape[0] + up.shape[1] // hb
    return pl.pallas_call(
        functools.partial(pack_second_kernel, order),
        out_shape=sds((hb, blocks * order.hl), BF),
        grid=(1,),
        in_specs=[whole(conv.shape), whole(up.shape)],
        out_specs=whole((hb, blocks * order.hl)),
        compiler_params=params(60),
        cost_estimate=cost(0, 4 * hb * blocks * order.hl),
        name="pack_second",
    )(conv, up)


def unpack_rest_kernel(order, taps, *refs):
    terms, (conv, up) = refs[:-2], refs[-2:]
    hb = order.hb
    fold = up.shape[1] // hb
    total = add_up([term[...] for term in terms], F32)
    for j in range(taps + fold):
        block = rows_from_wire(order, [total], taps + fold, j).T
        if j < taps:
            conv[j] = block
        else:
            up[:, (j - taps) * hb : (j - taps + 1) * hb] = block


def unpack_rest(order, taps, fold, terms):
    return pl.pallas_call(
        functools.partial(unpack_rest_kernel, order, taps),
        out_shape=(
            sds((taps, order.hl, order.hb), F32),
            sds((order.hl, fold * order.hb), F32),
        ),
        compiler_params=pltpu.CompilerParams(vmem_limit_bytes=16 * MIB),
        cost_estimate=cost(0, 8 * (taps + fold) * order.hl * order.hb),
        name="unpack_rest",
    )(*terms)


def unpack_first_kernel(order, *refs):
    terms, (down, tail) = refs[:-2], refs[-2:]
    hb = order.hb
    total = add_up([term[...] for term in terms], F32)
    down[...] = total[0:hb]
    tail[...] = total[hb : hb + 16]


def unpack_first(order, terms):
    dl = terms[0].shape[1]
    return pl.pallas_call(
        functools.partial(unpack_first_kernel, order),
        out_shape=(sds((order.hb, dl), F32), sds((16, dl), F32)),
        compiler_params=pltpu.CompilerParams(vmem_limit_bytes=16 * MIB),
        cost_estimate=cost(0, 8 * dl * order.hb),
        name="unpack_first",
    )(*terms)


def stage_one_kernel(
    grid, order, place, start_ref, length_ref, tokens, *refs
):
    parts, refs = refs[: 4 * grid.side], refs[4 * grid.side :]
    hidden_one, narrow, conv_input, down_t, table, stage, sems = refs
    model = tokens.shape[2]
    hidden = narrow.shape[2]
    hb, dl = order.hb, model // grid.seq

    @pl.when(pl.program_id(0) == 0)
    def _():
        copies = stage_copies(place, grid.side, parts, stage, sems)
        for copy in copies:
            copy.wait()
        table[...] = jnp.zeros_like(table)
        for b in range(grid.batch):
            pieces = [staged(grid, place, stage, s, b) for s in range(grid.seq)]
            block = join([piece[0:hb] for piece in pieces])
            for offset, spot, length in order.runs(b * hb, hb):
                down_t[spot : spot + length] = block[offset : offset + length]
            tail = pieces[0][hb : hb + 16].astype(F32)
            wide = model // grid.batch
            table[0:WIDE_ROWS, b * wide : (b + 1) * wide] = tail[0:WIDE_ROWS, 0:wide]
            for offset, spot, length in order.runs(b * hb, hb):
                table[WIDE_ROWS:TABLE_ROWS, spot : spot + length] = tail[
                    WIDE_ROWS:TABLE_ROWS, offset : offset + length
                ]

    def vec(name, width):
        return table[ROW[name] : ROW[name] + 1, 0:width]

    group, span = tokens.shape[0], tokens.shape[1]
    unit, _ = normed(tokens[...].reshape(group * span, model).astype(F32))
    one = gelu(scaled(unit, vec("first_gain", model), vec("first_shift", model))).astype(BF)
    hidden_one[...] = one.reshape(group, span, model)
    values = dot_nt(one, down_t[...]) + vec("down_bias", hidden)
    narrow[...] = values.reshape(group, span, hidden)
    unit, _ = normed(values)
    active = gelu(scaled(unit, vec("middle_gain", hidden), vec("middle_shift", hidden)))
    valid = valid_rows(start_ref, length_ref, group, span)
    conv_input[...] = (active * valid).astype(BF).reshape(group, span, hidden)


def stage_one(grid, order, place, start, lengths, tokens, parts):
    count, span, model = tokens.shape
    hidden = order.hidden
    group = group_of(count)
    rows, lanes = parts[0].shape[-2:]
    return pl.pallas_call(
        functools.partial(stage_one_kernel, grid, order),
        out_shape=(
            sds((count, span, model), BF),
            sds((count, span, hidden), F32),
            sds((count, span, hidden), BF),
            sds((hidden, model), BF),
            sds((TABLE_ROWS, model), F32),
        ),
        grid_spec=pltpu.PrefetchScalarGridSpec(
            num_scalar_prefetch=3,
            grid=(count // group,),
            in_specs=[rows_of((group, span, model))]
            + [pl.BlockSpec(memory_space=pl.ANY)] * len(parts),
            out_specs=[
                rows_of((group, span, model)),
                rows_of((group, span, hidden)),
                rows_of((group, span, hidden)),
                whole((hidden, model)),
                whole((TABLE_ROWS, model)),
            ],
            scratch_shapes=[
                pltpu.VMEM((2, 2) + piece_shape(grid, rows, lanes), BF),
                pltpu.SemaphoreType.DMA((len(parts),)),
            ],
        ),
        compiler_params=params(54),
        cost_estimate=cost(
            2 * count * span * model * hidden, count * span * (4 * model + 6 * hidden)
        ),
        name="stage_one",
    )(place, start, lengths, tokens, *parts)


def fill_padded(padded, left, body, right):
    reach = left.shape[0]
    span = body.shape[0]
    padded[0:reach] = left
    padded[reach : reach + span] = body
    padded[reach + span : 2 * reach + span] = right


def tap_windows(padded, taps, span):
    group, _, hidden = padded.shape
    return [
        padded[:, k * DILATION : k * DILATION + span].reshape(group * span, hidden) for k in taps
    ]


def edge_windows(left, right, taps):
    count, reach, hidden = left.shape
    zeros = jnp.zeros((count, reach, hidden), BF)
    before = jnp.concatenate([left, zeros], axis=1)
    after_run = jnp.concatenate([zeros, right], axis=1)
    middle = taps // 2

    def window(rows, at):
        return rows[:, at : at + reach].reshape(count * reach, hidden)

    return (
        [window(before, k * DILATION) for k in range(middle)],
        [window(after_run, (k - middle) * DILATION) for k in range(middle + 1, taps)],
    )


def add_edges(part, edges):
    group, span, hidden = part.shape
    reach = edges.shape[1] // 2
    rows = [part[:, 0:reach] + edges[:, 0:reach]]
    if span > 2 * reach:
        rows.append(part[:, reach : span - reach])
    rows.append(part[:, span - reach : span] + edges[:, reach : 2 * reach])
    return jnp.concatenate(rows, axis=1).reshape(group * span, hidden)


def inner_kernel(
    grid, order, taps, place, cotangent, conv_input, *refs
):
    parts, refs = refs[: 4 * grid.side], refs[4 * grid.side :]
    part, error, conv_t, up_out, conv_f, up_t, padded, stage, sems, out_sems = refs
    group, span, model = cotangent.shape
    hidden = conv_input.shape[2]
    reach = (padded.shape[1] - span) // 2
    hb = order.hb
    fold = model // hidden

    def weight_copies():
        return [
            pltpu.make_async_copy(
                conv_f.at[:, k * hidden : (k + 1) * hidden], conv_t.at[k], out_sems.at[k]
            )
            for k in range(taps)
        ] + [pltpu.make_async_copy(up_t, up_out, out_sems.at[taps])]

    @pl.when(pl.program_id(0) == 0)
    def _():
        copies = stage_copies(place, grid.side, parts, stage, sems)
        padded[:, 0:reach] = jnp.zeros((group, reach, hidden), BF)
        padded[:, reach + span : 2 * reach + span] = jnp.zeros((group, reach, hidden), BF)
        for copy in copies:
            copy.wait()
        for b in range(grid.batch):
            wires = [staged(grid, place, stage, s, b) for s in range(grid.seq)]
            for k in range(taps):
                block = rows_from_wire(order, wires, taps + fold, k)
                for offset, spot, length in order.runs(b * hb, hb):
                    conv_f[spot : spot + length, k * hidden : (k + 1) * hidden] = block[
                        offset : offset + length
                    ]
            for f in range(fold):
                row = (b * fold + f) * hb
                up_t[row : row + hb] = rows_from_wire(order, wires, taps + fold, taps + f)
        for copy in weight_copies():
            copy.start()

    padded[:, reach : reach + span] = conv_input[...]
    windows = join(tap_windows(padded, range(taps), span))
    part[...] = dot_nt(windows, conv_f[...]).reshape(group, span, hidden)
    incoming = cotangent[...].reshape(group * span, model)
    error[...] = dot_nn(incoming, up_t[...]).reshape(group, span, hidden)

    @pl.when(pl.program_id(0) == pl.num_programs(0) - 1)
    def _():
        for copy in weight_copies():
            copy.wait()


def inner(grid, order, taps, reach, place, cotangent, conv_input, parts):
    count, span, model = cotangent.shape
    hidden = order.hidden
    group = group_of(count)
    rows, lanes = parts[0].shape[-2:]
    return pl.pallas_call(
        functools.partial(inner_kernel, grid, order, taps),
        out_shape=(
            sds((count, span, hidden), F32),
            sds((count, span, hidden), F32),
            sds((taps, hidden, hidden), BF),
            sds((model, hidden), BF),
        ),
        grid_spec=pltpu.PrefetchScalarGridSpec(
            num_scalar_prefetch=1,
            grid=(count // group,),
            in_specs=[rows_of((group, span, model)), rows_of((group, span, hidden))]
            + [pl.BlockSpec(memory_space=pl.ANY)] * len(parts),
            out_specs=[
                rows_of((group, span, hidden)),
                rows_of((group, span, hidden)),
                pl.BlockSpec(memory_space=pl.ANY),
                pl.BlockSpec(memory_space=pl.ANY),
            ],
            scratch_shapes=[
                pltpu.VMEM((hidden, taps * hidden), BF),
                pltpu.VMEM((model, hidden), BF),
                pltpu.VMEM((group, span + 2 * reach, hidden), BF),
                pltpu.VMEM((2, 2) + piece_shape(grid, rows, lanes), BF),
                pltpu.SemaphoreType.DMA((len(parts),)),
                pltpu.SemaphoreType.DMA((taps + 1,)),
            ],
        ),
        compiler_params=params(LIM2P),
        cost_estimate=cost(
            2 * count * span * hidden * (taps * hidden + model),
            count * span * (2 * model + 10 * hidden),
        ),
        name="inner",
    )(place, cotangent, conv_input, *parts)


def stage_two_kernel(
    grid, order, taps, place, tokens, cotangent, conv_input, left, right, part, error, table,
    conv_t, up_t,
    output, conv_out_grad, sums, part_a, part_b, part_c, part_d,
    padded, threes, edges, total, conv_total, pieces, out_sems,
):
    group, span, model = tokens.shape
    hidden = conv_input.shape[2]
    reach = left.shape[1]
    count = left.shape[0]
    size = group * span
    hb = order.hb
    fold = model // hidden
    step = pl.program_id(0)

    def vec(name, width):
        return table[ROW[name] : ROW[name] + 1, 0:width]

    def add(name, values, factor=1.0):
        width = values.shape[1]
        sums[ROW[name] : ROW[name] + 1, 0:width] += row_sum(values) * factor

    @pl.when(step == 0)
    def _():
        sums[...] = jnp.zeros_like(sums)
        total[...] = jnp.zeros_like(total)
        conv_total[...] = jnp.zeros_like(conv_total)
        before, behind = edge_windows(left[...], right[...], taps)
        for at, windows, first in ((0, before, 0), (reach, behind, taps // 2 + 1)):
            term = None
            for k, window in enumerate(windows):
                product = dot_nt(window, conv_t[first + k])
                term = product if term is None else term + product
            edges[:, at : at + reach] = term.reshape(count, reach, hidden)

    for g in range(group):
        at = step * group + g
        fill_padded(padded.at[g], left[at], conv_input[g], right[at])
    values = add_edges(part[...], edges[pl.ds(step * group, group)]) + vec("conv_bias", hidden)
    unit, inverse = normed(values)
    gain = vec("final_gain", hidden)
    three, slope = gelu_both(scaled(unit, gain, vec("final_shift", hidden)))
    threes[...] = three.astype(BF)
    incoming = cotangent[...].reshape(size, model)
    result = tokens[...].reshape(size, model).astype(F32) + dot_nt(threes[...], up_t[...])
    output[...] = (result + vec("up_bias", model)).astype(BF).reshape(group, span, model)
    twice = error[...].reshape(size, hidden) * slope
    grad, product = back_rows(twice, gain, unit, inverse)
    grad = grad.astype(BF)
    conv_out_grad[...] = grad.reshape(group, span, hidden)
    add("final_gain", product, 0.5)
    add("final_shift", twice, 0.5)
    add("conv_bias", grad.astype(F32))
    add("up_bias", incoming.astype(F32))
    total[...] += dot_tn(incoming, threes[...])
    windows = join(tap_windows(padded, range(taps), span))
    conv_total[...] += dot_nn(conv_out_grad[...].reshape(size, hidden).T, windows)

    @pl.when(step == pl.num_programs(0) - 1)
    def _():
        for b in range(grid.batch):
            for offset, spot, length in order.runs(b * hb, hb):
                rows = [
                    conv_total[spot : spot + length, k * hidden : (k + 1) * hidden].astype(BF)
                    for k in range(taps)
                ]
                for f in range(fold):
                    at = (b * fold + f) * hb + offset
                    rows.append(total[at : at + length].astype(BF))
                for s, piece in enumerate(wire_from_rows(order, rows)):
                    pieces[distance(grid, place, s, b) + (pl.ds(offset, length),)] = piece
        hand_out(pieces, (part_a, part_b, part_c, part_d), out_sems)


def stage_two(
    grid, order, taps, place, tokens, cotangent, conv_input, left, right, part, error, table,
    conv_t, up_t,
):
    count, span, model = tokens.shape
    hidden = conv_input.shape[2]
    reach = left.shape[1]
    group = group_of(count)
    fold = model // hidden
    pieces = piece_shape(grid, order.hb, (taps + fold) * order.hl)
    return pl.pallas_call(
        functools.partial(stage_two_kernel, grid, order, taps),
        out_shape=(
            sds((count, span, model), BF),
            sds((count, span, hidden), BF),
            sds((TABLE_ROWS, model), F32),
            *[sds(pieces, BF)] * 4,
        ),
        grid_spec=pltpu.PrefetchScalarGridSpec(
            num_scalar_prefetch=1,
            grid=(count // group,),
            in_specs=[
                rows_of((group, span, model)),
                rows_of((group, span, model)),
                rows_of((group, span, hidden)),
                whole((count, reach, hidden)),
                whole((count, reach, hidden)),
                rows_of((group, span, hidden)),
                rows_of((group, span, hidden)),
                whole(table.shape),
                whole(conv_t.shape),
                whole(up_t.shape),
            ],
            out_specs=[
                rows_of((group, span, model)),
                rows_of((group, span, hidden)),
                whole((TABLE_ROWS, model)),
                *[pl.BlockSpec(memory_space=pl.ANY)] * 4,
            ],
            scratch_shapes=[
                pltpu.VMEM((group, span + 2 * reach, hidden), BF),
                pltpu.VMEM((group * span, hidden), BF),
                pltpu.VMEM((count, 2 * reach, hidden), F32),
                pltpu.VMEM((model, hidden), F32),
                pltpu.VMEM((hidden, taps * hidden), F32),
                pltpu.VMEM((2, 2) + pieces, BF),
                pltpu.SemaphoreType.DMA((4,)),
            ],
        ),
        compiler_params=params(LIM2),
        cost_estimate=cost(
            2 * count * span * hidden * (taps * hidden + 2 * model),
            count * span * (6 * model + 12 * hidden),
        ),
        name="stage_two",
    )(
        place, tokens, cotangent, conv_input, left, right, part, error, table, conv_t, up_t,
    )


def inner_back_kernel(conv_out_grad, conv_t, part, padded):
    group, span, hidden = conv_out_grad.shape
    taps = conv_t.shape[0]
    reach = (padded.shape[1] - span) // 2

    @pl.when(pl.program_id(0) == 0)
    def _():
        padded[:, 0:reach] = jnp.zeros((group, reach, hidden), BF)
        padded[:, reach + span : 2 * reach + span] = jnp.zeros((group, reach, hidden), BF)

    padded[:, reach : reach + span] = conv_out_grad[...]
    windows = join(tap_windows(padded, reversed(range(taps)), span))
    part[...] = dot_nn(windows, conv_t[...].reshape(taps * hidden, hidden)).reshape(
        group, span, hidden
    )


def inner_back(conv_out_grad, conv_t, reach):
    count, span, hidden = conv_out_grad.shape
    taps = conv_t.shape[0]
    group = group_of(count)
    return pl.pallas_call(
        inner_back_kernel,
        out_shape=sds((count, span, hidden), F32),
        grid=(count // group,),
        in_specs=[rows_of((group, span, hidden)), whole(conv_t.shape)],
        out_specs=rows_of((group, span, hidden)),
        scratch_shapes=[pltpu.VMEM((group, span + 2 * reach, hidden), BF)],
        compiler_params=params(LIM3P),
        cost_estimate=cost(2 * count * span * hidden * taps * hidden, count * span * 6 * hidden),
        name="inner_back",
    )(conv_out_grad, conv_t)


def stage_three_kernel(
    start_ref, length_ref, part, narrow, left, right, table, sums_in, conv_t,
    narrow_grad, sums, edges,
):
    group, span, hidden = narrow.shape
    count, reach = left.shape[0], left.shape[1]
    taps = conv_t.shape[0]
    step = pl.program_id(0)

    def vec(name, width):
        return table[ROW[name] : ROW[name] + 1, 0:width]

    def add(name, values, factor=1.0):
        width = values.shape[1]
        sums[ROW[name] : ROW[name] + 1, 0:width] += row_sum(values) * factor

    @pl.when(step == 0)
    def _():
        sums[...] = sums_in[...]
        before, behind = edge_windows(left[...], right[...], taps)
        for at, windows, first in ((0, before, 0), (reach, behind, taps // 2 + 1)):
            term = None
            for k, window in enumerate(windows):
                product = dot_nn(window, conv_t[taps - 1 - first - k])
                term = product if term is None else term + product
            edges[:, at : at + reach] = term.reshape(count, reach, hidden)

    back = add_edges(part[...], edges[pl.ds(step * group, group)])
    back = back * valid_rows(start_ref, length_ref, group, span)
    unit, inverse = normed(narrow[...].reshape(group * span, hidden))
    gain = vec("middle_gain", hidden)
    _, slope = gelu_both(scaled(unit, gain, vec("middle_shift", hidden)))
    twice = back * slope
    low, product = back_rows(twice, gain, unit, inverse)
    low = low.astype(BF)
    narrow_grad[...] = low.reshape(group, span, hidden)
    add("middle_gain", product, 0.5)
    add("middle_shift", twice, 0.5)
    add("down_bias", low.astype(F32))


def stage_three(start, lengths, part, narrow, left, right, table, sums, conv_t):
    count, span, hidden = narrow.shape
    reach = left.shape[1]
    group = group_of(count)
    return pl.pallas_call(
        stage_three_kernel,
        out_shape=(sds((count, span, hidden), BF), sds(sums.shape, F32)),
        grid_spec=pltpu.PrefetchScalarGridSpec(
            num_scalar_prefetch=2,
            grid=(count // group,),
            in_specs=[
                rows_of((group, span, hidden)),
                rows_of((group, span, hidden)),
                whole((count, reach, hidden)),
                whole((count, reach, hidden)),
                whole(table.shape),
                whole(table.shape),
                whole(conv_t.shape),
            ],
            out_specs=[rows_of((group, span, hidden)), whole(sums.shape)],
            scratch_shapes=[pltpu.VMEM((count, 2 * reach, hidden), F32)],
        ),
        compiler_params=params(LIM3),
        cost_estimate=cost(2 * count * span * hidden * hidden, count * span * 10 * hidden),
        name="stage_three",
    )(start, lengths, part, narrow, left, right, table, sums, conv_t)


def stage_four_kernel(
    grid, order, begin, last, place, tokens, cotangent, narrow_grad, table, sums_in, down_t, *refs
):
    if last:
        hidden_one, narrow_all, refs = refs[0], refs[1], refs[2:]
    if not begin:
        refs = refs[1:]
    tokens_grad, sums, refs = refs[0], refs[1], refs[2:]
    span, model = tokens.shape[1], tokens.shape[2]
    hidden = narrow_grad.shape[2]
    hb, dl = order.hb, model // grid.seq
    step = pl.program_id(0)

    def vec(name, width):
        return table[ROW[name] : ROW[name] + 1, 0:width]

    def add(name, values, factor=1.0):
        width = values.shape[1]
        sums[ROW[name] : ROW[name] + 1, 0:width] += row_sum(values) * factor

    @pl.when(step == 0)
    def _():
        sums[...] = sums_in[...]
        if last:
            refs[4][...] = jnp.zeros_like(refs[4])

    if last:
        *parts, total, pieces, out_sems = refs
        size = narrow_all.shape[0] * span
        total[...] += dot_tn(
            narrow_all[...].reshape(size, hidden), hidden_one[...].reshape(size, model)
        )
    deep = dot_nn(narrow_grad[0], down_t[...])
    unit, inverse = normed(tokens[0].astype(F32))
    gain = vec("first_gain", model)
    _, slope = gelu_both(scaled(unit, gain, vec("first_shift", model)))
    twice = deep * slope
    grad, product = back_rows(twice, gain, unit, inverse)
    add("first_gain", product, 0.5)
    add("first_shift", twice, 0.5)
    tokens_grad[0] = (grad + cotangent[0].astype(F32)).astype(BF)

    if last:

        @pl.when(step == pl.num_programs(0) - 1)
        def _():
            wide = model // grid.batch
            sub = lax.broadcasted_iota(jnp.int32, (TABLE_ROWS, dl), 0)
            for b in range(grid.batch):
                upper = sums[:, b * wide : (b + 1) * wide]
                runs = order.runs(b * hb, hb)
                lower = join([sums[:, spot : spot + length] for _, spot, length in runs])
                if wide < dl:
                    upper = join([upper, jnp.zeros((TABLE_ROWS, dl - wide), F32)])
                lower = join([lower, jnp.zeros((TABLE_ROWS, dl - hb), F32)])
                tail = jnp.where(sub < WIDE_ROWS, upper, lower).astype(BF)
                for s in range(grid.seq):
                    to = distance(grid, place, s, b)
                    for offset, spot, length in runs:
                        pieces[to + (pl.ds(offset, length),)] = total[
                            spot : spot + length, s * dl : (s + 1) * dl
                        ].astype(BF)
                    pieces[to + (pl.ds(hb, 16),)] = tail
            hand_out(pieces, parts, out_sems)


def stage_four(
    grid, order, first, part, begin, last, place, tokens, cotangent, hidden_one, narrow_grad,
    table, sums, down_t, grad_in,
):
    count, span, model = tokens.shape
    hidden = narrow_grad.shape[2]
    pieces = piece_shape(grid, order.hb + 16, model // grid.seq)

    def part_of(block):
        return pl.BlockSpec(block, lambda i, *_: (first + i,) + (0,) * (len(block) - 1))

    in_specs = [
        part_of((1, span, model)),
        part_of((1, span, model)),
        part_of((1, span, hidden)),
        whole(table.shape),
        whole(table.shape),
        whole(down_t.shape),
    ]
    inputs = [tokens, cotangent, narrow_grad, table, sums, down_t]
    out_shape = [sds((count, span, model), BF), sds(table.shape, F32)]
    out_specs = [part_of((1, span, model)), whole(table.shape)]
    scratch = []
    if last:
        share = count // part
        in_specs += [rows_of((share, span, model)), rows_of((share, span, hidden))]
        inputs += [hidden_one, narrow_grad]
        out_shape += [sds(pieces, BF)] * 4
        out_specs += [pl.BlockSpec(memory_space=pl.ANY)] * 4
        scratch = [
            pltpu.VMEM((hidden, model), F32),
            pltpu.VMEM((2, 2) + pieces, BF),
            pltpu.SemaphoreType.DMA((4,)),
        ]
    aliases = {}
    if not begin:
        in_specs.append(pl.BlockSpec(memory_space=pl.ANY))
        inputs.append(grad_in)
        aliases = {len(inputs): 0}
    return pl.pallas_call(
        functools.partial(stage_four_kernel, grid, order, begin, last),
        out_shape=tuple(out_shape),
        grid_spec=pltpu.PrefetchScalarGridSpec(
            num_scalar_prefetch=1,
            grid=(part,),
            in_specs=in_specs,
            out_specs=out_specs,
            scratch_shapes=scratch,
        ),
        input_output_aliases=aliases,
        compiler_params=params(LIM4),
        cost_estimate=cost(
            4 * part * span * hidden * model, part * span * (8 * model + 2 * hidden)
        ),
        name="stage_four",
    )(place, *inputs)


def halos(cells, reach):
    count = lax.axis_size("seq")
    left = lax.ppermute(
        cells[:, cells.shape[1] - reach :], "seq", [(i, i + 1) for i in range(count - 1)]
    )
    right = lax.ppermute(cells[:, :reach], "seq", [(i + 1, i) for i in range(count - 1)])
    return left, right


def after(value, *others):
    return lax.optimization_barrier((value,) + others)[0]


def body(
    grid,
    tokens,
    lengths,
    first_gain,
    first_shift,
    down_weight,
    down_bias,
    middle_gain,
    middle_shift,
    conv_weight,
    conv_bias,
    final_gain,
    final_shift,
    up_weight,
    up_bias,
    cotangent,
):
    shape = tokens.shape
    span, model = shape[2], shape[3]
    count = shape[0] * shape[1]
    taps = conv_weight.shape[0]
    hidden = down_weight.shape[1] * grid.batch
    order = Order(grid, hidden)
    hb, hl, dl = order.hb, order.hl, down_weight.shape[0]
    fold = model // hidden
    reach = (taps - 1) // 2 * DILATION

    tokens = tokens.reshape(count, span, model)
    cotangent = cotangent.reshape(count, span, model)
    lengths = lengths.reshape(count)
    place = jnp.stack(grid.here()).astype(jnp.int32)
    start = (lax.axis_index("seq") * span).astype(jnp.int32).reshape(1)

    vectors = {
        "first_gain": first_gain,
        "first_shift": first_shift,
        "up_bias": up_bias,
        "down_bias": down_bias,
        "middle_gain": middle_gain,
        "middle_shift": middle_shift,
        "conv_bias": conv_bias,
        "final_gain": final_gain,
        "final_shift": final_shift,
    }
    first_piece = pack_first(order, down_weight.T, [vectors[name] for name in WIDE + NARROW])
    second_piece = pack_second(order, after(conv_weight, first_piece), up_weight)

    def meet(*groups):
        flat = lax.optimization_barrier(tuple(value for group in groups for value in group))
        found, at = [], 0
        for group in groups:
            found.append(flat[at : at + len(group)])
            at += len(group)
        return found

    first = grid.gather_deep(first_piece)
    neighbour, second_piece = lax.optimization_barrier((first[1], second_piece))
    first[1] = neighbour
    second = grid.halves(grid.gather_deep(second_piece))
    one, two = grid.gather_near(*grid.halves(first))
    far_one, far_two = grid.gather_far(one, two)
    first = [one, *far_one, two, *far_two]
    first, second = meet(first, second)
    first = [*first, *grid.gather_core(first)]
    near = grid.gather_near(*second)
    near, first = meet(near, first)
    near_other = grid.gather_core(near)
    far_one, far_two = grid.gather_far(*near)
    hidden_one, narrow, conv_input, down_t, table = stage_one(
        grid, order, place, start, lengths, tokens, first
    )
    far_one, far_two, near_other, (conv_input,) = meet(
        far_one, far_two, near_other, (conv_input,)
    )
    left, right = halos(conv_input, reach)
    far_one_other, far_two_other = grid.gather_core(far_one), grid.gather_core(far_two)
    second = [near[0], *far_one, near[1], *far_two]
    second += [near_other[0], *far_one_other, near_other[1], *far_two_other]
    part, error, conv_t, up_t = inner(
        grid, order, taps, reach, place, cotangent, conv_input, second
    )
    block_output, conv_out_grad, sums, *rest = stage_two(
        grid, order, taps, place, tokens, cotangent, conv_input, left, right, part, error, table,
        conv_t, up_t,
    )

    left, right = halos(conv_out_grad, reach)
    rest = grid.reduce_core(*rest)
    part = inner_back(conv_out_grad, conv_t, reach)
    rest, (sums, left, right, part) = meet(rest, (sums, left, right, part))

    rest = grid.reduce_far(*rest)
    narrow_grad, sums = stage_three(
        start, lengths, part, narrow, left, right, table, sums, conv_t
    )
    half = count // 2
    tokens_grad, sums = stage_four(
        grid, order, 0, half, True, False, place, tokens, cotangent, hidden_one, narrow_grad,
        table, sums, down_t, None,
    )
    rest, (sums,) = meet(rest, (sums,))

    rest = grid.reduce_near(*rest)
    tokens_grad, sums, *down = stage_four(
        grid, order, half, half, False, True, place, tokens, cotangent, hidden_one, narrow_grad,
        table, sums, down_t, tokens_grad,
    )
    rest, down = meet(rest, down)

    down = grid.reduce_core(*down)
    down, rest = meet(down, rest)
    down = grid.reduce_far(*down)
    rest = grid.reduce_deep(*rest)
    down = grid.reduce_near(*down)
    down = grid.reduce_deep(*down)
    conv_grad, up_grad = unpack_rest(order, taps, fold, rest)
    down_grad, tail = unpack_first(order, down)
    grads = {name: tail[ROW[name], : vectors[name].shape[0]] for name in vectors}
    return (
        block_output.reshape(shape),
        tokens_grad.reshape(shape),
        grads["first_gain"],
        grads["first_shift"],
        down_grad.T,
        grads["down_bias"],
        grads["middle_gain"],
        grads["middle_shift"],
        conv_grad,
        grads["conv_bias"],
        grads["final_gain"],
        grads["final_shift"],
        up_grad,
        grads["up_bias"],
    )


def solution(mesh):
    grid = Grid(mesh.shape["seq"], mesh.shape["batch"])
    return jax.shard_map(
        functools.partial(body, grid),
        mesh=mesh,
        in_specs=(
            P(None, "batch", "seq", None),
            P(None, "batch"),
            P("batch"),
            P("batch"),
            P("seq", "batch"),
            P("batch"),
            P("batch"),
            P("batch"),
            P(None, "seq", "batch"),
            P("batch"),
            P("batch"),
            P("batch"),
            P("seq", "batch"),
            P("batch"),
            P(None, "batch", "seq", None),
        ),
        out_specs=(
            P(None, "batch", "seq", None),
            P(None, "batch", "seq", None),
            P("batch"),
            P("batch"),
            P("seq", "batch"),
            P("batch"),
            P("batch"),
            P("batch"),
            P(None, "seq", "batch"),
            P("batch"),
            P("batch"),
            P("batch"),
            P("seq", "batch"),
            P("batch"),
        ),
        check_vma=False,
    )
```

```python
import functools
import math

import jax
import jax.numpy as jnp
from jax import lax
from jax.experimental import pallas as pl
from jax.experimental.pallas import tpu as pltpu
from jax.sharding import PartitionSpec as P

DILATION = 16
EPSILON = 1e-05
BF = jnp.bfloat16
F32 = jnp.float32
ROOT_HALF = math.sqrt(0.5)
SLOPE = 2.0 / math.sqrt(math.pi)
LOG = -math.log2(math.e)
MIB = 1 << 20
GROUP = 2
LIM2P = 60
LIM2 = 60
LIM3P = 56
LIM3 = 40
LIM4 = 48

WIDE = ("first_gain", "first_shift", "up_bias")
NARROW = ("down_bias", "middle_gain", "middle_shift", "conv_bias", "final_gain", "final_shift")
WIDE_ROWS = 3
ROW = {name: row for row, name in enumerate(WIDE + NARROW)}
TABLE_ROWS = 16


def add_up(terms, kind):
    total = terms[0].astype(F32)
    for term in terms[1:]:
        total = total + term.astype(F32)
    return total.astype(kind)


class Grid:
    def __init__(self, seq, batch):
        self.seq, self.batch = seq, batch
        self.side = math.isqrt(seq)
        assert self.side * self.side == seq
        self.depth = batch // 2
        self.half = self.depth // 2

    def here(self):
        s, b = lax.axis_index("seq"), lax.axis_index("batch")
        return s // self.side, s % self.side, b // 2, b % 2

    def send(self, value, move):
        pairs = []
        for s in range(self.seq):
            for b in range(self.batch):
                h, l, z, c = move(s // self.side, s % self.side, b // 2, b % 2)
                pairs.append((s * self.batch + b, (h * self.side + l) * self.batch + z * 2 + c))
        return lax.ppermute(value, ("seq", "batch"), pairs)

    def high(self, value, k):
        return self.send(value, lambda h, l, z, c: ((h + k) % self.side, l, z, c))

    def low(self, value, k):
        return self.send(value, lambda h, l, z, c: (h, (l + k) % self.side, z, c))

    def deep(self, value, k):
        return self.send(value, lambda h, l, z, c: (h, l, (z + k) % self.depth, c))

    def core(self, value):
        return self.send(value, lambda h, l, z, c: (h, l, z, 1 - c))

    def gather_deep(self, piece):
        return [piece] + [self.deep(piece, k) for k in range(1, self.depth)]

    def halves(self, column):
        return jnp.stack(column[: self.half]), jnp.stack(column[self.half :])

    def gather_near(self, one, two):
        one = jnp.stack([one] + [self.low(one, k) for k in range(1, self.side)])
        two = jnp.stack([two] + [self.high(two, k) for k in range(1, self.side)])
        return one, two

    def gather_far(self, one, two):
        return (
            [self.high(one, k) for k in range(1, self.side)],
            [self.low(two, k) for k in range(1, self.side)],
        )

    def gather_core(self, values):
        return [self.core(value) for value in values]

    def reduce_core(self, keep_one, keep_two, give_one, give_two):
        return (
            add_up([keep_one, self.core(give_one)], BF),
            add_up([keep_two, self.core(give_two)], BF),
        )

    def reduce_far(self, one, two):
        one = add_up([one[0]] + [self.high(one[k], -k) for k in range(1, self.side)], BF)
        two = add_up([two[0]] + [self.low(two[k], -k) for k in range(1, self.side)], BF)
        return one, two

    def reduce_near(self, one, two):
        one = add_up([one[0]] + [self.low(one[k], -k) for k in range(1, self.side)], BF)
        two = add_up([two[0]] + [self.high(two[k], -k) for k in range(1, self.side)], BF)
        return one, two

    def reduce_deep(self, one, two):
        column = [one[k] for k in range(self.half)] + [two[k] for k in range(self.half)]
        return (column[0],) + tuple(self.deep(column[k], -k) for k in range(1, self.depth))


def near_distance(grid, place, s):
    side = grid.side
    return (
        lax.rem(place[0] - s // side + side, side),
        lax.rem(place[1] - s % side + side, side),
    )


def deep_distance(grid, place, b):
    return lax.rem(place[2] - b // 2 + grid.depth, grid.depth)


def spot_of(grid, place, s, b):
    rh, rl = near_distance(grid, place, s)
    rz = deep_distance(grid, place, b)
    second = rz >= grid.half
    return (
        jnp.where(second, 1, 0),
        jnp.where(second, rl, rh),
        jnp.where(second, rh, rl),
        jnp.where(second, rz - grid.half, rz),
    )


def distance(grid, place, s, b):
    return (jnp.where(place[3] == b % 2, 0, 1),) + spot_of(grid, place, s, b)


class Order:
    def __init__(self, grid, hidden):
        self.grid, self.hidden = grid, hidden
        self.hl, self.hb = hidden // grid.seq, hidden // grid.batch
        self.main = self.hl // 128 * 128
        self.rest = self.hl - self.main

    def runs(self, first, count):
        found = []
        at = first
        while at < first + count:
            block, r = at // self.hl, at % self.hl
            if r < self.main:
                length = min(self.main - r, first + count - at)
                place = block * self.main + r
            else:
                length = min(self.hl - r, first + count - at)
                place = self.grid.seq * self.main + block * self.rest + r - self.main
            if found and found[-1][1] + found[-1][2] == place:
                found[-1] = (found[-1][0], found[-1][1], found[-1][2] + length)
            else:
                found.append((at - first, place, length))
            at += length
        return found


def join(parts):
    return parts[0] if len(parts) == 1 else jnp.concatenate(parts, axis=1)


def wire_from_rows(order, row_blocks):
    main, rest, seq = order.main, order.rest, order.grid.seq
    pieces = []
    for s in range(seq):
        parts = [block[:, s * main : (s + 1) * main] for block in row_blocks if main]
        if rest:
            at = seq * main + s * rest
            parts += [block[:, at : at + rest] for block in row_blocks]
        pieces.append(join(parts))
    return pieces


def rows_from_wire(order, pieces, count, j):
    main, rest = order.main, order.rest
    parts = [piece[:, j * main : (j + 1) * main] for piece in pieces if main]
    if rest:
        at = count * main + j * rest
        parts += [piece[:, at : at + rest] for piece in pieces]
    return join(parts)


def stage_copies(place, side, parts, stage, sems):
    copies = []
    for index, part in enumerate(parts):
        mine = index < 2 * side
        core = place[3] if mine else 1 - place[3]
        half, far = index // side % 2, index % side
        copies.append(pltpu.make_async_copy(part, stage.at[core, half, far], sems.at[index]))
    for copy in copies:
        copy.start()
    return copies


def staged(grid, place, stage, s, b):
    return stage[(b % 2,) + spot_of(grid, place, s, b)]


def hand_out(pieces, parts, sems):
    copies = [
        pltpu.make_async_copy(pieces.at[index // 2, index % 2], part, sems.at[index])
        for index, part in enumerate(parts)
    ]
    for copy in copies:
        copy.start()
    for copy in copies:
        copy.wait()


def piece_shape(grid, rows, lanes):
    return (grid.side, grid.side, grid.half, rows, lanes)


def normed(values):
    center = values - jnp.mean(values, axis=-1, keepdims=True)
    spread = jnp.mean(center * center, axis=-1, keepdims=True)
    inverse = lax.rsqrt(spread + EPSILON)
    return center * inverse, inverse


def scaled(unit, gain, shift):
    return unit * (gain * ROOT_HALF) + shift * ROOT_HALF


def gelu(x):
    return (x * ROOT_HALF) * (1.0 + lax.erf(x))


def gelu_both(x):
    twice = 1.0 + lax.erf(x)
    return (x * ROOT_HALF) * twice, twice + (x * SLOPE) * jnp.exp2((x * LOG) * x)


def back_rows(twice_q, gain, unit, inverse):
    share = 1.0 / unit.shape[-1]
    half = gain * 0.5
    product = twice_q * unit
    weighted = twice_q * half
    first = jnp.sum(weighted, axis=-1, keepdims=True) * share
    second = jnp.sum(product * half, axis=-1, keepdims=True) * share
    return (weighted - first - unit * second) * inverse, product


def row_sum(values):
    return jnp.sum(values, axis=0, keepdims=True)


def dot_nn(left, right):
    return lax.dot_general(left, right, (((1,), (0,)), ((), ())), preferred_element_type=F32)


def dot_nt(left, right):
    return lax.dot_general(left, right, (((1,), (1,)), ((), ())), preferred_element_type=F32)


def dot_tn(left, right):
    return lax.dot_general(left, right, (((0,), (0,)), ((), ())), preferred_element_type=F32)


def group_of(count):
    return GROUP if count % GROUP == 0 else 1


def valid_rows(start_ref, length_ref, group, span):
    position = start_ref[0] + lax.broadcasted_iota(jnp.int32, (span, 1), 0)
    first = pl.program_id(0) * group
    return jnp.concatenate(
        [(position < length_ref[first + g]).astype(F32) for g in range(group)], axis=0
    )


def params(limit):
    return pltpu.CompilerParams(
        dimension_semantics=("arbitrary",), vmem_limit_bytes=limit * MIB
    )


def cost(flops, bytes_accessed, transcendentals=0):
    return pl.CostEstimate(
        flops=flops, bytes_accessed=bytes_accessed, transcendentals=transcendentals
    )


def whole(shape):
    return pl.BlockSpec(shape, lambda i, *_: (0,) * len(shape))


def rows_of(block):
    return pl.BlockSpec(block, lambda i, *_: (i,) + (0,) * (len(block) - 1))


def sds(shape, kind):
    return jax.ShapeDtypeStruct(shape, kind)


def pack_first_kernel(order, down, *refs):
    values, first = refs[:-1], refs[-1]
    hb, dl = down.shape
    first[0:hb] = down[...]
    sub = lax.broadcasted_iota(jnp.int32, (16, dl), 0)
    tail = jnp.zeros((16, dl), F32)
    for row, ref in enumerate(values):
        value = ref[...].astype(F32).reshape(1, -1)
        if value.shape[1] < dl:
            value = join([value, jnp.zeros((1, dl - value.shape[1]), F32)])
        tail = tail + jnp.where(sub == row, value, 0.0)
    first[hb : hb + 16] = tail.astype(BF)


def pack_first(order, down, values):
    hb, dl = down.shape
    return pl.pallas_call(
        functools.partial(pack_first_kernel, order),
        out_shape=sds((hb + 16, dl), BF),
        grid=(1,),
        in_specs=[whole(down.shape)] + [whole(value.shape) for value in values],
        out_specs=whole((hb + 16, dl)),
        compiler_params=params(60),
        cost_estimate=cost(0, 4 * hb * dl),
        name="pack_first",
    )(down, *values)


def pack_second_kernel(order, conv, up, second):
    hb, taps = order.hb, conv.shape[0]
    fold = up.shape[1] // hb
    blocks = [conv[k].astype(F32).T.astype(BF) for k in range(taps)]
    turned = up[...].astype(F32).T.astype(BF)
    blocks += [turned[f * hb : (f + 1) * hb] for f in range(fold)]
    parts = [block[:, : order.main] for block in blocks if order.main]
    if order.rest:
        parts += [block[:, order.main :] for block in blocks]
    second[...] = join(parts)


def pack_second(order, conv, up):
    hb = order.hb
    blocks = conv.shape[0] + up.shape[1] // hb
    return pl.pallas_call(
        functools.partial(pack_second_kernel, order),
        out_shape=sds((hb, blocks * order.hl), BF),
        grid=(1,),
        in_specs=[whole(conv.shape), whole(up.shape)],
        out_specs=whole((hb, blocks * order.hl)),
        compiler_params=params(60),
        cost_estimate=cost(0, 4 * hb * blocks * order.hl),
        name="pack_second",
    )(conv, up)


def unpack_rest_kernel(order, taps, *refs):
    terms, (conv, up) = refs[:-2], refs[-2:]
    hb = order.hb
    fold = up.shape[1] // hb
    total = add_up([term[...] for term in terms], F32)
    for j in range(taps + fold):
        block = rows_from_wire(order, [total], taps + fold, j).T
        if j < taps:
            conv[j] = block
        else:
            up[:, (j - taps) * hb : (j - taps + 1) * hb] = block


def unpack_rest(order, taps, fold, terms):
    return pl.pallas_call(
        functools.partial(unpack_rest_kernel, order, taps),
        out_shape=(
            sds((taps, order.hl, order.hb), F32),
            sds((order.hl, fold * order.hb), F32),
        ),
        compiler_params=pltpu.CompilerParams(vmem_limit_bytes=16 * MIB),
        cost_estimate=cost(0, 8 * (taps + fold) * order.hl * order.hb),
        name="unpack_rest",
    )(*terms)


def unpack_first_kernel(order, count, *refs):
    terms, down, vectors = refs[:count], refs[count], refs[count + 1 :]
    hb = order.hb
    total = add_up([term[...] for term in terms], F32)
    down[...] = total[0:hb]
    for row, vector in enumerate(vectors):
        width = vector.shape[0]
        vector[...] = total[hb + row : hb + row + 1, 0:width].reshape(width)


def unpack_first(order, terms, widths):
    dl = terms[0].shape[1]
    return pl.pallas_call(
        functools.partial(unpack_first_kernel, order, len(terms)),
        out_shape=(sds((order.hb, dl), F32), *[sds((width,), F32) for width in widths]),
        compiler_params=pltpu.CompilerParams(vmem_limit_bytes=16 * MIB),
        cost_estimate=cost(0, 8 * dl * order.hb),
        name="unpack_first",
    )(*terms)


def stage_one_kernel(
    grid, order, place, start_ref, length_ref, tokens, *refs
):
    parts, refs = refs[: 4 * grid.side], refs[4 * grid.side :]
    hidden_one, narrow, conv_input, head, foot, down_t, table, stage, sems = refs
    model = tokens.shape[2]
    hidden = narrow.shape[2]
    hb, dl = order.hb, model // grid.seq

    @pl.when(pl.program_id(0) == 0)
    def _():
        copies = stage_copies(place, grid.side, parts, stage, sems)
        for copy in copies:
            copy.wait()
        table[...] = jnp.zeros_like(table)
        for b in range(grid.batch):
            pieces = [staged(grid, place, stage, s, b) for s in range(grid.seq)]
            block = join([piece[0:hb] for piece in pieces])
            for offset, spot, length in order.runs(b * hb, hb):
                down_t[spot : spot + length] = block[offset : offset + length]
            tail = pieces[0][hb : hb + 16].astype(F32)
            wide = model // grid.batch
            table[0:WIDE_ROWS, b * wide : (b + 1) * wide] = tail[0:WIDE_ROWS, 0:wide]
            for offset, spot, length in order.runs(b * hb, hb):
                table[WIDE_ROWS:TABLE_ROWS, spot : spot + length] = tail[
                    WIDE_ROWS:TABLE_ROWS, offset : offset + length
                ]

    def vec(name, width):
        return table[ROW[name] : ROW[name] + 1, 0:width]

    group, span = tokens.shape[0], tokens.shape[1]
    unit, _ = normed(tokens[...].reshape(group * span, model).astype(F32))
    one = gelu(scaled(unit, vec("first_gain", model), vec("first_shift", model))).astype(BF)
    hidden_one[...] = one.reshape(group, span, model)
    values = dot_nt(one, down_t[...]) + vec("down_bias", hidden)
    narrow[...] = values.reshape(group, span, hidden)
    unit, _ = normed(values)
    active = gelu(scaled(unit, vec("middle_gain", hidden), vec("middle_shift", hidden)))
    valid = valid_rows(start_ref, length_ref, group, span)
    conv_input[...] = (active * valid).astype(BF).reshape(group, span, hidden)
    reach = head.shape[1]
    head[...] = conv_input[:, 0:reach]
    foot[...] = conv_input[:, span - reach : span]


def stage_one(grid, order, reach, place, start, lengths, tokens, parts):
    count, span, model = tokens.shape
    hidden = order.hidden
    group = group_of(count)
    rows, lanes = parts[0].shape[-2:]
    return pl.pallas_call(
        functools.partial(stage_one_kernel, grid, order),
        out_shape=(
            sds((count, span, model), BF),
            sds((count, span, hidden), F32),
            sds((count, span, hidden), BF),
            sds((count, reach, hidden), BF),
            sds((count, reach, hidden), BF),
            sds((hidden, model), BF),
            sds((TABLE_ROWS, model), F32),
        ),
        grid_spec=pltpu.PrefetchScalarGridSpec(
            num_scalar_prefetch=3,
            grid=(count // group,),
            in_specs=[rows_of((group, span, model))]
            + [pl.BlockSpec(memory_space=pl.ANY)] * len(parts),
            out_specs=[
                rows_of((group, span, model)),
                rows_of((group, span, hidden)),
                rows_of((group, span, hidden)),
                rows_of((group, reach, hidden)),
                rows_of((group, reach, hidden)),
                whole((hidden, model)),
                whole((TABLE_ROWS, model)),
            ],
            scratch_shapes=[
                pltpu.VMEM((2, 2) + piece_shape(grid, rows, lanes), BF),
                pltpu.SemaphoreType.DMA((len(parts),)),
            ],
        ),
        compiler_params=params(54),
        cost_estimate=cost(
            2 * count * span * model * hidden, count * span * (4 * model + 6 * hidden)
        ),
        name="stage_one",
    )(place, start, lengths, tokens, *parts)


def fill_padded(padded, left, body, right):
    reach = left.shape[0]
    span = body.shape[0]
    padded[0:reach] = left
    padded[reach : reach + span] = body
    padded[reach + span : 2 * reach + span] = right


def tap_windows(padded, taps, span):
    group, _, hidden = padded.shape
    return [
        padded[:, k * DILATION : k * DILATION + span].reshape(group * span, hidden) for k in taps
    ]


def edge_windows(left, right, taps):
    count, reach, hidden = left.shape
    zeros = jnp.zeros((count, reach, hidden), BF)
    before = jnp.concatenate([left, zeros], axis=1)
    after_run = jnp.concatenate([zeros, right], axis=1)
    middle = taps // 2

    def window(rows, at):
        return rows[:, at : at + reach].reshape(count * reach, hidden)

    return (
        [window(before, k * DILATION) for k in range(middle)],
        [window(after_run, (k - middle) * DILATION) for k in range(middle + 1, taps)],
    )


def add_edges(part, edges):
    group, span, hidden = part.shape
    reach = edges.shape[1] // 2
    rows = [part[:, 0:reach] + edges[:, 0:reach]]
    if span > 2 * reach:
        rows.append(part[:, reach : span - reach])
    rows.append(part[:, span - reach : span] + edges[:, reach : 2 * reach])
    return jnp.concatenate(rows, axis=1).reshape(group * span, hidden)


def inner_kernel(
    grid, order, taps, place, cotangent, conv_input, *refs
):
    parts, refs = refs[: 4 * grid.side], refs[4 * grid.side :]
    part, error, conv_t, up_out, conv_f, up_t, padded, stage, sems, out_sems = refs
    group, span, model = cotangent.shape
    hidden = conv_input.shape[2]
    reach = (padded.shape[1] - span) // 2
    hb = order.hb
    fold = model // hidden

    def weight_copies():
        return [
            pltpu.make_async_copy(
                conv_f.at[:, k * hidden : (k + 1) * hidden], conv_t.at[k], out_sems.at[k]
            )
            for k in range(taps)
        ] + [pltpu.make_async_copy(up_t, up_out, out_sems.at[taps])]

    @pl.when(pl.program_id(0) == 0)
    def _():
        copies = stage_copies(place, grid.side, parts, stage, sems)
        padded[:, 0:reach] = jnp.zeros((group, reach, hidden), BF)
        padded[:, reach + span : 2 * reach + span] = jnp.zeros((group, reach, hidden), BF)
        for copy in copies:
            copy.wait()
        for b in range(grid.batch):
            wires = [staged(grid, place, stage, s, b) for s in range(grid.seq)]
            for k in range(taps):
                block = rows_from_wire(order, wires, taps + fold, k)
                for offset, spot, length in order.runs(b * hb, hb):
                    conv_f[spot : spot + length, k * hidden : (k + 1) * hidden] = block[
                        offset : offset + length
                    ]
            for f in range(fold):
                row = (b * fold + f) * hb
                up_t[row : row + hb] = rows_from_wire(order, wires, taps + fold, taps + f)
        for copy in weight_copies():
            copy.start()

    padded[:, reach : reach + span] = conv_input[...]
    windows = join(tap_windows(padded, range(taps), span))
    part[...] = dot_nt(windows, conv_f[...]).reshape(group, span, hidden)
    incoming = cotangent[...].reshape(group * span, model)
    error[...] = dot_nn(incoming, up_t[...]).reshape(group, span, hidden)

    @pl.when(pl.program_id(0) == pl.num_programs(0) - 1)
    def _():
        for copy in weight_copies():
            copy.wait()


def inner(grid, order, taps, reach, place, cotangent, conv_input, parts):
    count, span, model = cotangent.shape
    hidden = order.hidden
    group = group_of(count)
    rows, lanes = parts[0].shape[-2:]
    return pl.pallas_call(
        functools.partial(inner_kernel, grid, order, taps),
        out_shape=(
            sds((count, span, hidden), F32),
            sds((count, span, hidden), F32),
            sds((taps, hidden, hidden), BF),
            sds((model, hidden), BF),
        ),
        grid_spec=pltpu.PrefetchScalarGridSpec(
            num_scalar_prefetch=1,
            grid=(count // group,),
            in_specs=[rows_of((group, span, model)), rows_of((group, span, hidden))]
            + [pl.BlockSpec(memory_space=pl.ANY)] * len(parts),
            out_specs=[
                rows_of((group, span, hidden)),
                rows_of((group, span, hidden)),
                pl.BlockSpec(memory_space=pl.ANY),
                pl.BlockSpec(memory_space=pl.ANY),
            ],
            scratch_shapes=[
                pltpu.VMEM((hidden, taps * hidden), BF),
                pltpu.VMEM((model, hidden), BF),
                pltpu.VMEM((group, span + 2 * reach, hidden), BF),
                pltpu.VMEM((2, 2) + piece_shape(grid, rows, lanes), BF),
                pltpu.SemaphoreType.DMA((len(parts),)),
                pltpu.SemaphoreType.DMA((taps + 1,)),
            ],
        ),
        compiler_params=params(LIM2P),
        cost_estimate=cost(
            2 * count * span * hidden * (taps * hidden + model),
            count * span * (2 * model + 10 * hidden),
        ),
        name="inner",
    )(place, cotangent, conv_input, *parts)


def stage_two_kernel(
    grid, order, taps, place, tokens, cotangent, conv_input, left, right, part, error, table,
    conv_t, up_t,
    output, conv_out_grad, head, foot, sums, part_a, part_b, part_c, part_d,
    padded, threes, edges, total, conv_total, pieces, out_sems,
):
    group, span, model = tokens.shape
    hidden = conv_input.shape[2]
    reach = left.shape[1]
    count = left.shape[0]
    size = group * span
    hb = order.hb
    fold = model // hidden
    step = pl.program_id(0)

    def vec(name, width):
        return table[ROW[name] : ROW[name] + 1, 0:width]

    def add(name, values, factor=1.0):
        width = values.shape[1]
        sums[ROW[name] : ROW[name] + 1, 0:width] += row_sum(values) * factor

    @pl.when(step == 0)
    def _():
        sums[...] = jnp.zeros_like(sums)
        total[...] = jnp.zeros_like(total)
        conv_total[...] = jnp.zeros_like(conv_total)
        before, behind = edge_windows(left[...], right[...], taps)
        for at, windows, first in ((0, before, 0), (reach, behind, taps // 2 + 1)):
            term = None
            for k, window in enumerate(windows):
                product = dot_nt(window, conv_t[first + k])
                term = product if term is None else term + product
            edges[:, at : at + reach] = term.reshape(count, reach, hidden)

    for g in range(group):
        at = step * group + g
        fill_padded(padded.at[g], left[at], conv_input[g], right[at])
    values = add_edges(part[...], edges[pl.ds(step * group, group)]) + vec("conv_bias", hidden)
    unit, inverse = normed(values)
    gain = vec("final_gain", hidden)
    three, slope = gelu_both(scaled(unit, gain, vec("final_shift", hidden)))
    threes[...] = three.astype(BF)
    incoming = cotangent[...].reshape(size, model)
    result = tokens[...].reshape(size, model).astype(F32) + dot_nt(threes[...], up_t[...])
    output[...] = (result + vec("up_bias", model)).astype(BF).reshape(group, span, model)
    twice = error[...].reshape(size, hidden) * slope
    grad, product = back_rows(twice, gain, unit, inverse)
    grad = grad.astype(BF)
    conv_out_grad[...] = grad.reshape(group, span, hidden)
    head[...] = conv_out_grad[:, 0:reach]
    foot[...] = conv_out_grad[:, span - reach : span]
    add("final_gain", product, 0.5)
    add("final_shift", twice, 0.5)
    add("conv_bias", grad.astype(F32))
    add("up_bias", incoming.astype(F32))
    total[...] += dot_tn(incoming, threes[...])
    windows = join(tap_windows(padded, range(taps), span))
    conv_total[...] += dot_nn(conv_out_grad[...].reshape(size, hidden).T, windows)

    @pl.when(step == pl.num_programs(0) - 1)
    def _():
        for b in range(grid.batch):
            for offset, spot, length in order.runs(b * hb, hb):
                rows = [
                    conv_total[spot : spot + length, k * hidden : (k + 1) * hidden].astype(BF)
                    for k in range(taps)
                ]
                for f in range(fold):
                    at = (b * fold + f) * hb + offset
                    rows.append(total[at : at + length].astype(BF))
                for s, piece in enumerate(wire_from_rows(order, rows)):
                    pieces[distance(grid, place, s, b) + (pl.ds(offset, length),)] = piece
        hand_out(pieces, (part_a, part_b, part_c, part_d), out_sems)


def stage_two(
    grid, order, taps, place, tokens, cotangent, conv_input, left, right, part, error, table,
    conv_t, up_t,
):
    count, span, model = tokens.shape
    hidden = conv_input.shape[2]
    reach = left.shape[1]
    group = group_of(count)
    fold = model // hidden
    pieces = piece_shape(grid, order.hb, (taps + fold) * order.hl)
    return pl.pallas_call(
        functools.partial(stage_two_kernel, grid, order, taps),
        out_shape=(
            sds((count, span, model), BF),
            sds((count, span, hidden), BF),
            sds((count, reach, hidden), BF),
            sds((count, reach, hidden), BF),
            sds((TABLE_ROWS, model), F32),
            *[sds(pieces, BF)] * 4,
        ),
        grid_spec=pltpu.PrefetchScalarGridSpec(
            num_scalar_prefetch=1,
            grid=(count // group,),
            in_specs=[
                rows_of((group, span, model)),
                rows_of((group, span, model)),
                rows_of((group, span, hidden)),
                whole((count, reach, hidden)),
                whole((count, reach, hidden)),
                rows_of((group, span, hidden)),
                rows_of((group, span, hidden)),
                whole(table.shape),
                whole(conv_t.shape),
                whole(up_t.shape),
            ],
            out_specs=[
                rows_of((group, span, model)),
                rows_of((group, span, hidden)),
                rows_of((group, reach, hidden)),
                rows_of((group, reach, hidden)),
                whole((TABLE_ROWS, model)),
                *[pl.BlockSpec(memory_space=pl.ANY)] * 4,
            ],
            scratch_shapes=[
                pltpu.VMEM((group, span + 2 * reach, hidden), BF),
                pltpu.VMEM((group * span, hidden), BF),
                pltpu.VMEM((count, 2 * reach, hidden), F32),
                pltpu.VMEM((model, hidden), F32),
                pltpu.VMEM((hidden, taps * hidden), F32),
                pltpu.VMEM((2, 2) + pieces, BF),
                pltpu.SemaphoreType.DMA((4,)),
            ],
        ),
        compiler_params=params(LIM2),
        cost_estimate=cost(
            2 * count * span * hidden * (taps * hidden + 2 * model),
            count * span * (6 * model + 12 * hidden),
        ),
        name="stage_two",
    )(
        place, tokens, cotangent, conv_input, left, right, part, error, table, conv_t, up_t,
    )


def inner_back_kernel(conv_out_grad, conv_t, part, padded):
    group, span, hidden = conv_out_grad.shape
    taps = conv_t.shape[0]
    reach = (padded.shape[1] - span) // 2

    @pl.when(pl.program_id(0) == 0)
    def _():
        padded[:, 0:reach] = jnp.zeros((group, reach, hidden), BF)
        padded[:, reach + span : 2 * reach + span] = jnp.zeros((group, reach, hidden), BF)

    padded[:, reach : reach + span] = conv_out_grad[...]
    windows = join(tap_windows(padded, reversed(range(taps)), span))
    part[...] = dot_nn(windows, conv_t[...].reshape(taps * hidden, hidden)).reshape(
        group, span, hidden
    )


def inner_back(conv_out_grad, conv_t, reach):
    count, span, hidden = conv_out_grad.shape
    taps = conv_t.shape[0]
    group = group_of(count)
    return pl.pallas_call(
        inner_back_kernel,
        out_shape=sds((count, span, hidden), F32),
        grid=(count // group,),
        in_specs=[rows_of((group, span, hidden)), whole(conv_t.shape)],
        out_specs=rows_of((group, span, hidden)),
        scratch_shapes=[pltpu.VMEM((group, span + 2 * reach, hidden), BF)],
        compiler_params=params(LIM3P),
        cost_estimate=cost(2 * count * span * hidden * taps * hidden, count * span * 6 * hidden),
        name="inner_back",
    )(conv_out_grad, conv_t)


def stage_three_kernel(
    start_ref, length_ref, part, narrow, left, right, table, sums_in, conv_t,
    narrow_grad, sums, edges,
):
    group, span, hidden = narrow.shape
    count, reach = left.shape[0], left.shape[1]
    taps = conv_t.shape[0]
    step = pl.program_id(0)

    def vec(name, width):
        return table[ROW[name] : ROW[name] + 1, 0:width]

    def add(name, values, factor=1.0):
        width = values.shape[1]
        sums[ROW[name] : ROW[name] + 1, 0:width] += row_sum(values) * factor

    @pl.when(step == 0)
    def _():
        sums[...] = sums_in[...]
        before, behind = edge_windows(left[...], right[...], taps)
        for at, windows, first in ((0, before, 0), (reach, behind, taps // 2 + 1)):
            term = None
            for k, window in enumerate(windows):
                product = dot_nn(window, conv_t[taps - 1 - first - k])
                term = product if term is None else term + product
            edges[:, at : at + reach] = term.reshape(count, reach, hidden)

    back = add_edges(part[...], edges[pl.ds(step * group, group)])
    back = back * valid_rows(start_ref, length_ref, group, span)
    unit, inverse = normed(narrow[...].reshape(group * span, hidden))
    gain = vec("middle_gain", hidden)
    _, slope = gelu_both(scaled(unit, gain, vec("middle_shift", hidden)))
    twice = back * slope
    low, product = back_rows(twice, gain, unit, inverse)
    low = low.astype(BF)
    narrow_grad[...] = low.reshape(group, span, hidden)
    add("middle_gain", product, 0.5)
    add("middle_shift", twice, 0.5)
    add("down_bias", low.astype(F32))


def stage_three(start, lengths, part, narrow, left, right, table, sums, conv_t):
    count, span, hidden = narrow.shape
    reach = left.shape[1]
    group = group_of(count)
    return pl.pallas_call(
        stage_three_kernel,
        out_shape=(sds((count, span, hidden), BF), sds(sums.shape, F32)),
        grid_spec=pltpu.PrefetchScalarGridSpec(
            num_scalar_prefetch=2,
            grid=(count // group,),
            in_specs=[
                rows_of((group, span, hidden)),
                rows_of((group, span, hidden)),
                whole((count, reach, hidden)),
                whole((count, reach, hidden)),
                whole(table.shape),
                whole(table.shape),
                whole(conv_t.shape),
            ],
            out_specs=[rows_of((group, span, hidden)), whole(sums.shape)],
            scratch_shapes=[pltpu.VMEM((count, 2 * reach, hidden), F32)],
        ),
        compiler_params=params(LIM3),
        cost_estimate=cost(2 * count * span * hidden * hidden, count * span * 10 * hidden),
        name="stage_three",
    )(start, lengths, part, narrow, left, right, table, sums, conv_t)


def stage_four_kernel(
    grid, order, begin, last, place, tokens, cotangent, narrow_grad, table, sums_in, down_t, *refs
):
    if last:
        hidden_one, narrow_all, refs = refs[0], refs[1], refs[2:]
    if not begin:
        refs = refs[1:]
    tokens_grad, sums, refs = refs[0], refs[1], refs[2:]
    span, model = tokens.shape[1], tokens.shape[2]
    hidden = narrow_grad.shape[2]
    hb, dl = order.hb, model // grid.seq
    step = pl.program_id(0)

    def vec(name, width):
        return table[ROW[name] : ROW[name] + 1, 0:width]

    def add(name, values, factor=1.0):
        width = values.shape[1]
        sums[ROW[name] : ROW[name] + 1, 0:width] += row_sum(values) * factor

    @pl.when(step == 0)
    def _():
        sums[...] = sums_in[...]
        if last:
            refs[4][...] = jnp.zeros_like(refs[4])

    if last:
        *parts, total, pieces, out_sems = refs
        size = narrow_all.shape[0] * span
        total[...] += dot_tn(
            narrow_all[...].reshape(size, hidden), hidden_one[...].reshape(size, model)
        )
    deep = dot_nn(narrow_grad[0], down_t[...])
    unit, inverse = normed(tokens[0].astype(F32))
    gain = vec("first_gain", model)
    _, slope = gelu_both(scaled(unit, gain, vec("first_shift", model)))
    twice = deep * slope
    grad, product = back_rows(twice, gain, unit, inverse)
    add("first_gain", product, 0.5)
    add("first_shift", twice, 0.5)
    tokens_grad[0] = (grad + cotangent[0].astype(F32)).astype(BF)

    if last:

        @pl.when(step == pl.num_programs(0) - 1)
        def _():
            wide = model // grid.batch
            sub = lax.broadcasted_iota(jnp.int32, (TABLE_ROWS, dl), 0)
            for b in range(grid.batch):
                upper = sums[:, b * wide : (b + 1) * wide]
                runs = order.runs(b * hb, hb)
                lower = join([sums[:, spot : spot + length] for _, spot, length in runs])
                if wide < dl:
                    upper = join([upper, jnp.zeros((TABLE_ROWS, dl - wide), F32)])
                lower = join([lower, jnp.zeros((TABLE_ROWS, dl - hb), F32)])
                tail = jnp.where(sub < WIDE_ROWS, upper, lower).astype(BF)
                for s in range(grid.seq):
                    to = distance(grid, place, s, b)
                    for offset, spot, length in runs:
                        pieces[to + (pl.ds(offset, length),)] = total[
                            spot : spot + length, s * dl : (s + 1) * dl
                        ].astype(BF)
                    pieces[to + (pl.ds(hb, 16),)] = tail
            hand_out(pieces, parts, out_sems)


def stage_four(
    grid, order, first, part, begin, last, place, tokens, cotangent, hidden_one, narrow_grad,
    table, sums, down_t, grad_in,
):
    count, span, model = tokens.shape
    hidden = narrow_grad.shape[2]
    pieces = piece_shape(grid, order.hb + 16, model // grid.seq)

    def part_of(block):
        return pl.BlockSpec(block, lambda i, *_: (first + i,) + (0,) * (len(block) - 1))

    in_specs = [
        part_of((1, span, model)),
        part_of((1, span, model)),
        part_of((1, span, hidden)),
        whole(table.shape),
        whole(table.shape),
        whole(down_t.shape),
    ]
    inputs = [tokens, cotangent, narrow_grad, table, sums, down_t]
    out_shape = [sds((count, span, model), BF), sds(table.shape, F32)]
    out_specs = [part_of((1, span, model)), whole(table.shape)]
    scratch = []
    if last:
        share = count // part
        in_specs += [rows_of((share, span, model)), rows_of((share, span, hidden))]
        inputs += [hidden_one, narrow_grad]
        out_shape += [sds(pieces, BF)] * 4
        out_specs += [pl.BlockSpec(memory_space=pl.ANY)] * 4
        scratch = [
            pltpu.VMEM((hidden, model), F32),
            pltpu.VMEM((2, 2) + pieces, BF),
            pltpu.SemaphoreType.DMA((4,)),
        ]
    aliases = {}
    if not begin:
        in_specs.append(pl.BlockSpec(memory_space=pl.ANY))
        inputs.append(grad_in)
        aliases = {len(inputs): 0}
    return pl.pallas_call(
        functools.partial(stage_four_kernel, grid, order, begin, last),
        out_shape=tuple(out_shape),
        grid_spec=pltpu.PrefetchScalarGridSpec(
            num_scalar_prefetch=1,
            grid=(part,),
            in_specs=in_specs,
            out_specs=out_specs,
            scratch_shapes=scratch,
        ),
        input_output_aliases=aliases,
        compiler_params=params(LIM4),
        cost_estimate=cost(
            4 * part * span * hidden * model, part * span * (8 * model + 2 * hidden)
        ),
        name="stage_four",
    )(place, *inputs)


def halos(head, foot):
    count = lax.axis_size("seq")
    left = lax.ppermute(foot, "seq", [(i, i + 1) for i in range(count - 1)])
    right = lax.ppermute(head, "seq", [(i + 1, i) for i in range(count - 1)])
    return left, right


def after(value, *others):
    return lax.optimization_barrier((value,) + others)[0]


def body(
    grid,
    tokens,
    lengths,
    first_gain,
    first_shift,
    down_weight,
    down_bias,
    middle_gain,
    middle_shift,
    conv_weight,
    conv_bias,
    final_gain,
    final_shift,
    up_weight,
    up_bias,
    cotangent,
):
    shape = tokens.shape
    span, model = shape[2], shape[3]
    count = shape[0] * shape[1]
    taps = conv_weight.shape[0]
    hidden = down_weight.shape[1] * grid.batch
    order = Order(grid, hidden)
    hb, hl, dl = order.hb, order.hl, down_weight.shape[0]
    fold = model // hidden
    reach = (taps - 1) // 2 * DILATION

    tokens = tokens.reshape(count, span, model)
    cotangent = cotangent.reshape(count, span, model)
    lengths = lengths.reshape(count)
    place = jnp.stack(grid.here()).astype(jnp.int32)
    start = (lax.axis_index("seq") * span).astype(jnp.int32).reshape(1)

    vectors = {
        "first_gain": first_gain,
        "first_shift": first_shift,
        "up_bias": up_bias,
        "down_bias": down_bias,
        "middle_gain": middle_gain,
        "middle_shift": middle_shift,
        "conv_bias": conv_bias,
        "final_gain": final_gain,
        "final_shift": final_shift,
    }
    first_piece = pack_first(order, down_weight.T, [vectors[name] for name in WIDE + NARROW])
    second_piece = pack_second(order, after(conv_weight, first_piece), up_weight)

    def meet(*groups):
        flat = lax.optimization_barrier(tuple(value for group in groups for value in group))
        found, at = [], 0
        for group in groups:
            found.append(flat[at : at + len(group)])
            at += len(group)
        return found

    first = grid.gather_deep(first_piece)
    (first[1], second_piece), (place, start, lengths) = meet(
        (first[1], second_piece), (place, start, lengths)
    )
    second = grid.halves(grid.gather_deep(second_piece))
    one, two = grid.gather_near(*grid.halves(first))
    far_one, far_two = grid.gather_far(one, two)
    first = [one, *far_one, two, *far_two]
    first, second = meet(first, second)
    first = [*first, *grid.gather_core(first)]
    near = grid.gather_near(*second)
    near, first = meet(near, first)
    near_other = grid.gather_core(near)
    far_one, far_two = grid.gather_far(*near)
    hidden_one, narrow, conv_input, head, foot, down_t, table = stage_one(
        grid, order, reach, place, start, lengths, tokens, first
    )
    far_one, far_two, near_other, (head, foot) = meet(
        far_one, far_two, near_other, (head, foot)
    )
    left, right = halos(head, foot)
    far_one_other, far_two_other = grid.gather_core(far_one), grid.gather_core(far_two)
    second = [near[0], *far_one, near[1], *far_two]
    second += [near_other[0], *far_one_other, near_other[1], *far_two_other]
    part, error, conv_t, up_t = inner(
        grid, order, taps, reach, place, cotangent, conv_input, second
    )
    block_output, conv_out_grad, head, foot, sums, *rest = stage_two(
        grid, order, taps, place, tokens, cotangent, conv_input, left, right, part, error, table,
        conv_t, up_t,
    )

    left, right = halos(head, foot)
    rest = grid.reduce_core(*rest)
    part = inner_back(conv_out_grad, conv_t, reach)
    rest, (sums, left, right, part) = meet(rest, (sums, left, right, part))

    rest = grid.reduce_far(*rest)
    narrow_grad, sums = stage_three(
        start, lengths, part, narrow, left, right, table, sums, conv_t
    )
    half = count // 2
    tokens_grad, sums = stage_four(
        grid, order, 0, half, True, False, place, tokens, cotangent, hidden_one, narrow_grad,
        table, sums, down_t, None,
    )
    rest, (sums,) = meet(rest, (sums,))

    rest = grid.reduce_near(*rest)
    tokens_grad, sums, *down = stage_four(
        grid, order, half, half, False, True, place, tokens, cotangent, hidden_one, narrow_grad,
        table, sums, down_t, tokens_grad,
    )
    rest, down = meet(rest, down)

    down = grid.reduce_core(*down)
    down, rest = meet(down, rest)
    down = grid.reduce_far(*down)
    rest = grid.reduce_deep(*rest)
    down = grid.reduce_near(*down)
    down = grid.reduce_deep(*down)
    conv_grad, up_grad = unpack_rest(order, taps, fold, rest)
    names = WIDE + NARROW
    down_grad, *found = unpack_first(order, down, [vectors[name].shape[0] for name in names])
    grads = dict(zip(names, found))
    return (
        block_output.reshape(shape),
        tokens_grad.reshape(shape),
        grads["first_gain"],
        grads["first_shift"],
        down_grad.T,
        grads["down_bias"],
        grads["middle_gain"],
        grads["middle_shift"],
        conv_grad,
        grads["conv_bias"],
        grads["final_gain"],
        grads["final_shift"],
        up_grad,
        grads["up_bias"],
    )


def solution(mesh):
    grid = Grid(mesh.shape["seq"], mesh.shape["batch"])
    return jax.shard_map(
        functools.partial(body, grid),
        mesh=mesh,
        in_specs=(
            P(None, "batch", "seq", None),
            P(None, "batch"),
            P("batch"),
            P("batch"),
            P("seq", "batch"),
            P("batch"),
            P("batch"),
            P("batch"),
            P(None, "seq", "batch"),
            P("batch"),
            P("batch"),
            P("batch"),
            P("seq", "batch"),
            P("batch"),
            P(None, "batch", "seq", None),
        ),
        out_specs=(
            P(None, "batch", "seq", None),
            P(None, "batch", "seq", None),
            P("batch"),
            P("batch"),
            P("seq", "batch"),
            P("batch"),
            P("batch"),
            P("batch"),
            P(None, "seq", "batch"),
            P("batch"),
            P("batch"),
            P("batch"),
            P("seq", "batch"),
            P("batch"),
        ),
        check_vma=False,
    )
```

```python
import functools
import math

import jax
import jax.numpy as jnp
from jax import lax
from jax.experimental import pallas as pl
from jax.experimental.pallas import tpu as pltpu
from jax.sharding import PartitionSpec as P

DILATION = 16
EPSILON = 1e-05
BF = jnp.bfloat16
F32 = jnp.float32
ROOT_HALF = math.sqrt(0.5)
SLOPE = 2.0 / math.sqrt(math.pi)
LOG = -math.log2(math.e)
MIB = 1 << 20
GROUP = 2
LIM2P = 60
LIM2 = 60
LIM3P = 56
LIM3 = 40
LIM4 = 48

WIDE = ("first_gain", "first_shift", "up_bias")
NARROW = ("down_bias", "middle_gain", "middle_shift", "conv_bias", "final_gain", "final_shift")
WIDE_ROWS = 3
ROW = {name: row for row, name in enumerate(WIDE + NARROW)}
TABLE_ROWS = 16


def add_up(terms, kind):
    total = terms[0].astype(F32)
    for term in terms[1:]:
        total = total + term.astype(F32)
    return total.astype(kind)


class Grid:
    def __init__(self, seq, batch):
        self.seq, self.batch = seq, batch
        self.side = math.isqrt(seq)
        assert self.side * self.side == seq
        self.depth = batch // 2
        self.half = self.depth // 2

    def here(self):
        s, b = lax.axis_index("seq"), lax.axis_index("batch")
        return s // self.side, s % self.side, b // 2, b % 2

    def send(self, value, move):
        pairs = []
        for s in range(self.seq):
            for b in range(self.batch):
                h, l, z, c = move(s // self.side, s % self.side, b // 2, b % 2)
                pairs.append((s * self.batch + b, (h * self.side + l) * self.batch + z * 2 + c))
        return lax.ppermute(value, ("seq", "batch"), pairs)

    def high(self, value, k):
        return self.send(value, lambda h, l, z, c: ((h + k) % self.side, l, z, c))

    def low(self, value, k):
        return self.send(value, lambda h, l, z, c: (h, (l + k) % self.side, z, c))

    def deep(self, value, k):
        return self.send(value, lambda h, l, z, c: (h, l, (z + k) % self.depth, c))

    def core(self, value):
        return self.send(value, lambda h, l, z, c: (h, l, z, 1 - c))

    def gather_deep(self, piece):
        return [piece] + [self.deep(piece, k) for k in range(1, self.depth)]

    def halves(self, column):
        return jnp.stack(column[: self.half]), jnp.stack(column[self.half :])

    def gather_near(self, one, two):
        one = jnp.stack([one] + [self.low(one, k) for k in range(1, self.side)])
        two = jnp.stack([two] + [self.high(two, k) for k in range(1, self.side)])
        return one, two

    def gather_far(self, one, two):
        return (
            [self.high(one, k) for k in range(1, self.side)],
            [self.low(two, k) for k in range(1, self.side)],
        )

    def gather_core(self, values):
        return [self.core(value) for value in values]

    def reduce_core(self, keep_one, keep_two, give_one, give_two):
        return (
            add_up([keep_one, self.core(give_one)], BF),
            add_up([keep_two, self.core(give_two)], BF),
        )

    def reduce_far(self, one, two):
        one = add_up([one[0]] + [self.high(one[k], -k) for k in range(1, self.side)], BF)
        two = add_up([two[0]] + [self.low(two[k], -k) for k in range(1, self.side)], BF)
        return one, two

    def reduce_near(self, one, two):
        one = add_up([one[0]] + [self.low(one[k], -k) for k in range(1, self.side)], BF)
        two = add_up([two[0]] + [self.high(two[k], -k) for k in range(1, self.side)], BF)
        return one, two

    def reduce_deep(self, one, two):
        column = [one[k] for k in range(self.half)] + [two[k] for k in range(self.half)]
        return (column[0],) + tuple(self.deep(column[k], -k) for k in range(1, self.depth))


def near_distance(grid, place, s):
    side = grid.side
    return (
        lax.rem(place[0] - s // side + side, side),
        lax.rem(place[1] - s % side + side, side),
    )


def deep_distance(grid, place, b):
    return lax.rem(place[2] - b // 2 + grid.depth, grid.depth)


def spot_of(grid, place, s, b):
    rh, rl = near_distance(grid, place, s)
    rz = deep_distance(grid, place, b)
    second = rz >= grid.half
    return (
        jnp.where(second, 1, 0),
        jnp.where(second, rl, rh),
        jnp.where(second, rh, rl),
        jnp.where(second, rz - grid.half, rz),
    )


def distance(grid, place, s, b):
    return (jnp.where(place[3] == b % 2, 0, 1),) + spot_of(grid, place, s, b)


class Order:
    def __init__(self, grid, hidden):
        self.grid, self.hidden = grid, hidden
        self.hl, self.hb = hidden // grid.seq, hidden // grid.batch
        self.main = self.hl // 128 * 128
        self.rest = self.hl - self.main

    def runs(self, first, count):
        found = []
        at = first
        while at < first + count:
            block, r = at // self.hl, at % self.hl
            if r < self.main:
                length = min(self.main - r, first + count - at)
                place = block * self.main + r
            else:
                length = min(self.hl - r, first + count - at)
                place = self.grid.seq * self.main + block * self.rest + r - self.main
            if found and found[-1][1] + found[-1][2] == place:
                found[-1] = (found[-1][0], found[-1][1], found[-1][2] + length)
            else:
                found.append((at - first, place, length))
            at += length
        return found


def join(parts):
    return parts[0] if len(parts) == 1 else jnp.concatenate(parts, axis=1)


def wire_from_rows(order, row_blocks):
    main, rest, seq = order.main, order.rest, order.grid.seq
    pieces = []
    for s in range(seq):
        parts = [block[:, s * main : (s + 1) * main] for block in row_blocks if main]
        if rest:
            at = seq * main + s * rest
            parts += [block[:, at : at + rest] for block in row_blocks]
        pieces.append(join(parts))
    return pieces


def rows_from_wire(order, pieces, count, j):
    main, rest = order.main, order.rest
    parts = [piece[:, j * main : (j + 1) * main] for piece in pieces if main]
    if rest:
        at = count * main + j * rest
        parts += [piece[:, at : at + rest] for piece in pieces]
    return join(parts)


def stage_copies(place, side, parts, stage, sems):
    copies = []
    for index, part in enumerate(parts):
        mine = index < 2 * side
        core = place[3] if mine else 1 - place[3]
        half, far = index // side % 2, index % side
        copies.append(pltpu.make_async_copy(part, stage.at[core, half, far], sems.at[index]))
    for copy in copies:
        copy.start()
    return copies


def staged(grid, place, stage, s, b):
    return stage[(b % 2,) + spot_of(grid, place, s, b)]


def hand_out(place, parity, pieces, parts, sems):
    def copies(core):
        return [
            pltpu.make_async_copy(
                pieces.at[core, half], parts[2 * core + half], sems.at[2 * core + half]
            )
            for half in range(2)
        ]

    @pl.when(place[3] == parity)
    def _():
        for copy in copies(0):
            copy.start()

    @pl.when(place[3] != parity)
    def _():
        for copy in copies(1):
            copy.start()

    if parity == 1:
        for core in range(2):
            for copy in copies(core):
                copy.wait()


def piece_shape(grid, rows, lanes):
    return (grid.side, grid.side, grid.half, rows, lanes)


def normed(values):
    center = values - jnp.mean(values, axis=-1, keepdims=True)
    spread = jnp.mean(center * center, axis=-1, keepdims=True)
    inverse = lax.rsqrt(spread + EPSILON)
    return center * inverse, inverse


def scaled(unit, gain, shift):
    return unit * (gain * ROOT_HALF) + shift * ROOT_HALF


def gelu(x):
    return (x * ROOT_HALF) * (1.0 + lax.erf(x))


def gelu_both(x):
    twice = 1.0 + lax.erf(x)
    return (x * ROOT_HALF) * twice, twice + (x * SLOPE) * jnp.exp2((x * LOG) * x)


def back_rows(twice_q, gain, unit, inverse):
    share = 1.0 / unit.shape[-1]
    half = gain * 0.5
    product = twice_q * unit
    weighted = twice_q * half
    first = jnp.sum(weighted, axis=-1, keepdims=True) * share
    second = jnp.sum(product * half, axis=-1, keepdims=True) * share
    return (weighted - first - unit * second) * inverse, product


def row_sum(values):
    return jnp.sum(values, axis=0, keepdims=True)


def dot_nn(left, right):
    return lax.dot_general(left, right, (((1,), (0,)), ((), ())), preferred_element_type=F32)


def dot_nt(left, right):
    return lax.dot_general(left, right, (((1,), (1,)), ((), ())), preferred_element_type=F32)


def dot_tn(left, right):
    return lax.dot_general(left, right, (((0,), (0,)), ((), ())), preferred_element_type=F32)


def group_of(count):
    return GROUP if count % GROUP == 0 else 1


def valid_rows(start_ref, length_ref, group, span):
    position = start_ref[0] + lax.broadcasted_iota(jnp.int32, (span, 1), 0)
    first = pl.program_id(0) * group
    return jnp.concatenate(
        [(position < length_ref[first + g]).astype(F32) for g in range(group)], axis=0
    )


def params(limit):
    return pltpu.CompilerParams(
        dimension_semantics=("arbitrary",), vmem_limit_bytes=limit * MIB
    )


def cost(flops, bytes_accessed, transcendentals=0):
    return pl.CostEstimate(
        flops=flops, bytes_accessed=bytes_accessed, transcendentals=transcendentals
    )


def whole(shape):
    return pl.BlockSpec(shape, lambda i, *_: (0,) * len(shape))


def rows_of(block):
    return pl.BlockSpec(block, lambda i, *_: (i,) + (0,) * (len(block) - 1))


def sds(shape, kind):
    return jax.ShapeDtypeStruct(shape, kind)


def pack_first_kernel(order, down, *refs):
    values, first = refs[:-1], refs[-1]
    hb, dl = down.shape
    first[0:hb] = down[...]
    sub = lax.broadcasted_iota(jnp.int32, (16, dl), 0)
    tail = jnp.zeros((16, dl), F32)
    for row, ref in enumerate(values):
        value = ref[...].astype(F32).reshape(1, -1)
        if value.shape[1] < dl:
            value = join([value, jnp.zeros((1, dl - value.shape[1]), F32)])
        tail = tail + jnp.where(sub == row, value, 0.0)
    first[hb : hb + 16] = tail.astype(BF)


def pack_first(order, down, values):
    hb, dl = down.shape
    return pl.pallas_call(
        functools.partial(pack_first_kernel, order),
        out_shape=sds((hb + 16, dl), BF),
        grid=(1,),
        in_specs=[whole(down.shape)] + [whole(value.shape) for value in values],
        out_specs=whole((hb + 16, dl)),
        compiler_params=params(60),
        cost_estimate=cost(0, 4 * hb * dl),
        name="pack_first",
    )(down, *values)


def pack_second_kernel(order, conv, up, second):
    hb, taps = order.hb, conv.shape[0]
    fold = up.shape[1] // hb
    blocks = [conv[k].astype(F32).T.astype(BF) for k in range(taps)]
    turned = up[...].astype(F32).T.astype(BF)
    blocks += [turned[f * hb : (f + 1) * hb] for f in range(fold)]
    parts = [block[:, : order.main] for block in blocks if order.main]
    if order.rest:
        parts += [block[:, order.main :] for block in blocks]
    second[...] = join(parts)


def pack_second(order, conv, up):
    hb = order.hb
    blocks = conv.shape[0] + up.shape[1] // hb
    return pl.pallas_call(
        functools.partial(pack_second_kernel, order),
        out_shape=sds((hb, blocks * order.hl), BF),
        grid=(1,),
        in_specs=[whole(conv.shape), whole(up.shape)],
        out_specs=whole((hb, blocks * order.hl)),
        compiler_params=params(60),
        cost_estimate=cost(0, 4 * hb * blocks * order.hl),
        name="pack_second",
    )(conv, up)


def unpack_rest_kernel(order, taps, *refs):
    terms, (conv, up) = refs[:-2], refs[-2:]
    hb = order.hb
    fold = up.shape[1] // hb
    total = add_up([term[...] for term in terms], F32)
    for j in range(taps + fold):
        block = rows_from_wire(order, [total], taps + fold, j).T
        if j < taps:
            conv[j] = block
        else:
            up[:, (j - taps) * hb : (j - taps + 1) * hb] = block


def unpack_rest(order, taps, fold, terms):
    return pl.pallas_call(
        functools.partial(unpack_rest_kernel, order, taps),
        out_shape=(
            sds((taps, order.hl, order.hb), F32),
            sds((order.hl, fold * order.hb), F32),
        ),
        compiler_params=pltpu.CompilerParams(vmem_limit_bytes=16 * MIB),
        cost_estimate=cost(0, 8 * (taps + fold) * order.hl * order.hb),
        name="unpack_rest",
    )(*terms)


def unpack_first_kernel(order, count, *refs):
    terms, down, vectors = refs[:count], refs[count], refs[count + 1 :]
    hb = order.hb
    total = add_up([term[...] for term in terms], F32)
    down[...] = total[0:hb]
    for row, vector in enumerate(vectors):
        width = vector.shape[0]
        vector[...] = total[hb + row : hb + row + 1, 0:width].reshape(width)


def unpack_first(order, terms, widths):
    dl = terms[0].shape[1]
    return pl.pallas_call(
        functools.partial(unpack_first_kernel, order, len(terms)),
        out_shape=(sds((order.hb, dl), F32), *[sds((width,), F32) for width in widths]),
        compiler_params=pltpu.CompilerParams(vmem_limit_bytes=16 * MIB),
        cost_estimate=cost(0, 8 * dl * order.hb),
        name="unpack_first",
    )(*terms)


def stage_one_kernel(
    grid, order, place, start_ref, length_ref, tokens, *refs
):
    parts, refs = refs[: 4 * grid.side], refs[4 * grid.side :]
    hidden_one, narrow, conv_input, head, foot, down_t, table, stage, sems = refs
    model = tokens.shape[2]
    hidden = narrow.shape[2]
    hb, dl = order.hb, model // grid.seq

    @pl.when(pl.program_id(0) == 0)
    def _():
        copies = stage_copies(place, grid.side, parts, stage, sems)
        for copy in copies:
            copy.wait()
        table[...] = jnp.zeros_like(table)
        for b in range(grid.batch):
            pieces = [staged(grid, place, stage, s, b) for s in range(grid.seq)]
            block = join([piece[0:hb] for piece in pieces])
            for offset, spot, length in order.runs(b * hb, hb):
                down_t[spot : spot + length] = block[offset : offset + length]
            tail = pieces[0][hb : hb + 16].astype(F32)
            wide = model // grid.batch
            table[0:WIDE_ROWS, b * wide : (b + 1) * wide] = tail[0:WIDE_ROWS, 0:wide]
            for offset, spot, length in order.runs(b * hb, hb):
                table[WIDE_ROWS:TABLE_ROWS, spot : spot + length] = tail[
                    WIDE_ROWS:TABLE_ROWS, offset : offset + length
                ]

    def vec(name, width):
        return table[ROW[name] : ROW[name] + 1, 0:width]

    group, span = tokens.shape[0], tokens.shape[1]
    unit, _ = normed(tokens[...].reshape(group * span, model).astype(F32))
    one = gelu(scaled(unit, vec("first_gain", model), vec("first_shift", model))).astype(BF)
    hidden_one[...] = one.reshape(group, span, model)
    values = dot_nt(one, down_t[...]) + vec("down_bias", hidden)
    narrow[...] = values.reshape(group, span, hidden)
    unit, _ = normed(values)
    active = gelu(scaled(unit, vec("middle_gain", hidden), vec("middle_shift", hidden)))
    valid = valid_rows(start_ref, length_ref, group, span)
    conv_input[...] = (active * valid).astype(BF).reshape(group, span, hidden)
    reach = head.shape[1]
    head[...] = conv_input[:, 0:reach]
    foot[...] = conv_input[:, span - reach : span]


def stage_one(grid, order, reach, place, start, lengths, tokens, parts):
    count, span, model = tokens.shape
    hidden = order.hidden
    group = group_of(count)
    rows, lanes = parts[0].shape[-2:]
    return pl.pallas_call(
        functools.partial(stage_one_kernel, grid, order),
        out_shape=(
            sds((count, span, model), BF),
            sds((count, span, hidden), F32),
            sds((count, span, hidden), BF),
            sds((count, reach, hidden), BF),
            sds((count, reach, hidden), BF),
            sds((hidden, model), BF),
            sds((TABLE_ROWS, model), F32),
        ),
        grid_spec=pltpu.PrefetchScalarGridSpec(
            num_scalar_prefetch=3,
            grid=(count // group,),
            in_specs=[rows_of((group, span, model))]
            + [pl.BlockSpec(memory_space=pl.ANY)] * len(parts),
            out_specs=[
                rows_of((group, span, model)),
                rows_of((group, span, hidden)),
                rows_of((group, span, hidden)),
                rows_of((group, reach, hidden)),
                rows_of((group, reach, hidden)),
                whole((hidden, model)),
                whole((TABLE_ROWS, model)),
            ],
            scratch_shapes=[
                pltpu.VMEM((2, 2) + piece_shape(grid, rows, lanes), BF),
                pltpu.SemaphoreType.DMA((len(parts),)),
            ],
        ),
        compiler_params=params(54),
        cost_estimate=cost(
            2 * count * span * model * hidden, count * span * (4 * model + 6 * hidden)
        ),
        name="stage_one",
    )(place, start, lengths, tokens, *parts)


def fill_padded(padded, left, body, right):
    reach = left.shape[0]
    span = body.shape[0]
    padded[0:reach] = left
    padded[reach : reach + span] = body
    padded[reach + span : 2 * reach + span] = right


def tap_windows(padded, taps, span):
    group, _, hidden = padded.shape
    return [
        padded[:, k * DILATION : k * DILATION + span].reshape(group * span, hidden) for k in taps
    ]


def edge_windows(left, right, taps):
    count, reach, hidden = left.shape
    zeros = jnp.zeros((count, reach, hidden), BF)
    before = jnp.concatenate([left, zeros], axis=1)
    after_run = jnp.concatenate([zeros, right], axis=1)
    middle = taps // 2

    def window(rows, at):
        return rows[:, at : at + reach].reshape(count * reach, hidden)

    return (
        [window(before, k * DILATION) for k in range(middle)],
        [window(after_run, (k - middle) * DILATION) for k in range(middle + 1, taps)],
    )


def add_edges(part, edges):
    group, span, hidden = part.shape
    reach = edges.shape[1] // 2
    rows = [part[:, 0:reach] + edges[:, 0:reach]]
    if span > 2 * reach:
        rows.append(part[:, reach : span - reach])
    rows.append(part[:, span - reach : span] + edges[:, reach : 2 * reach])
    return jnp.concatenate(rows, axis=1).reshape(group * span, hidden)


def inner_kernel(
    grid, order, taps, place, cotangent, conv_input, *refs
):
    parts, refs = refs[: 4 * grid.side], refs[4 * grid.side :]
    part, error, conv_t, up_out, conv_f, up_t, padded, stage, sems, out_sems = refs
    group, span, model = cotangent.shape
    hidden = conv_input.shape[2]
    reach = (padded.shape[1] - span) // 2
    hb = order.hb
    fold = model // hidden

    def weight_copies():
        return [
            pltpu.make_async_copy(
                conv_f.at[:, k * hidden : (k + 1) * hidden], conv_t.at[k], out_sems.at[k]
            )
            for k in range(taps)
        ] + [pltpu.make_async_copy(up_t, up_out, out_sems.at[taps])]

    @pl.when(pl.program_id(0) == 0)
    def _():
        copies = stage_copies(place, grid.side, parts, stage, sems)
        padded[:, 0:reach] = jnp.zeros((group, reach, hidden), BF)
        padded[:, reach + span : 2 * reach + span] = jnp.zeros((group, reach, hidden), BF)
        for copy in copies:
            copy.wait()
        for b in range(grid.batch):
            wires = [staged(grid, place, stage, s, b) for s in range(grid.seq)]
            for k in range(taps):
                block = rows_from_wire(order, wires, taps + fold, k)
                for offset, spot, length in order.runs(b * hb, hb):
                    conv_f[spot : spot + length, k * hidden : (k + 1) * hidden] = block[
                        offset : offset + length
                    ]
            for f in range(fold):
                row = (b * fold + f) * hb
                up_t[row : row + hb] = rows_from_wire(order, wires, taps + fold, taps + f)
        for copy in weight_copies():
            copy.start()

    padded[:, reach : reach + span] = conv_input[...]
    windows = join(tap_windows(padded, range(taps), span))
    part[...] = dot_nt(windows, conv_f[...]).reshape(group, span, hidden)
    incoming = cotangent[...].reshape(group * span, model)
    error[...] = dot_nn(incoming, up_t[...]).reshape(group, span, hidden)

    @pl.when(pl.program_id(0) == pl.num_programs(0) - 1)
    def _():
        for copy in weight_copies():
            copy.wait()


def inner(grid, order, taps, reach, place, cotangent, conv_input, parts):
    count, span, model = cotangent.shape
    hidden = order.hidden
    group = group_of(count)
    rows, lanes = parts[0].shape[-2:]
    return pl.pallas_call(
        functools.partial(inner_kernel, grid, order, taps),
        out_shape=(
            sds((count, span, hidden), F32),
            sds((count, span, hidden), F32),
            sds((taps, hidden, hidden), BF),
            sds((model, hidden), BF),
        ),
        grid_spec=pltpu.PrefetchScalarGridSpec(
            num_scalar_prefetch=1,
            grid=(count // group,),
            in_specs=[rows_of((group, span, model)), rows_of((group, span, hidden))]
            + [pl.BlockSpec(memory_space=pl.ANY)] * len(parts),
            out_specs=[
                rows_of((group, span, hidden)),
                rows_of((group, span, hidden)),
                pl.BlockSpec(memory_space=pl.ANY),
                pl.BlockSpec(memory_space=pl.ANY),
            ],
            scratch_shapes=[
                pltpu.VMEM((hidden, taps * hidden), BF),
                pltpu.VMEM((model, hidden), BF),
                pltpu.VMEM((group, span + 2 * reach, hidden), BF),
                pltpu.VMEM((2, 2) + piece_shape(grid, rows, lanes), BF),
                pltpu.SemaphoreType.DMA((len(parts),)),
                pltpu.SemaphoreType.DMA((taps + 1,)),
            ],
        ),
        compiler_params=params(LIM2P),
        cost_estimate=cost(
            2 * count * span * hidden * (taps * hidden + model),
            count * span * (2 * model + 10 * hidden),
        ),
        name="inner",
    )(place, cotangent, conv_input, *parts)


def stage_two_kernel(
    grid, order, taps, place, tokens, cotangent, conv_input, left, right, part, error, table,
    conv_t, up_t,
    output, conv_out_grad, head, foot, sums, part_a, part_b, part_c, part_d,
    padded, threes, edges, total, conv_total, pieces, out_sems,
):
    group, span, model = tokens.shape
    hidden = conv_input.shape[2]
    reach = left.shape[1]
    count = left.shape[0]
    size = group * span
    hb = order.hb
    fold = model // hidden
    step = pl.program_id(0)

    def vec(name, width):
        return table[ROW[name] : ROW[name] + 1, 0:width]

    def add(name, values, factor=1.0):
        width = values.shape[1]
        sums[ROW[name] : ROW[name] + 1, 0:width] += row_sum(values) * factor

    @pl.when(step == 0)
    def _():
        sums[...] = jnp.zeros_like(sums)
        total[...] = jnp.zeros_like(total)
        conv_total[...] = jnp.zeros_like(conv_total)
        before, behind = edge_windows(left[...], right[...], taps)
        for at, windows, first in ((0, before, 0), (reach, behind, taps // 2 + 1)):
            term = None
            for k, window in enumerate(windows):
                product = dot_nt(window, conv_t[first + k])
                term = product if term is None else term + product
            edges[:, at : at + reach] = term.reshape(count, reach, hidden)

    for g in range(group):
        at = step * group + g
        fill_padded(padded.at[g], left[at], conv_input[g], right[at])
    values = add_edges(part[...], edges[pl.ds(step * group, group)]) + vec("conv_bias", hidden)
    unit, inverse = normed(values)
    gain = vec("final_gain", hidden)
    three, slope = gelu_both(scaled(unit, gain, vec("final_shift", hidden)))
    threes[...] = three.astype(BF)
    incoming = cotangent[...].reshape(size, model)
    result = tokens[...].reshape(size, model).astype(F32) + dot_nt(threes[...], up_t[...])
    output[...] = (result + vec("up_bias", model)).astype(BF).reshape(group, span, model)
    twice = error[...].reshape(size, hidden) * slope
    grad, product = back_rows(twice, gain, unit, inverse)
    grad = grad.astype(BF)
    conv_out_grad[...] = grad.reshape(group, span, hidden)
    head[...] = conv_out_grad[:, 0:reach]
    foot[...] = conv_out_grad[:, span - reach : span]
    add("final_gain", product, 0.5)
    add("final_shift", twice, 0.5)
    add("conv_bias", grad.astype(F32))
    add("up_bias", incoming.astype(F32))
    total[...] += dot_tn(incoming, threes[...])
    windows = join(tap_windows(padded, range(taps), span))
    conv_total[...] += dot_nn(conv_out_grad[...].reshape(size, hidden).T, windows)

    @pl.when(step == pl.num_programs(0) - 1)
    def _():
        for b in [*range(0, grid.batch, 2), *range(1, grid.batch, 2)]:
            for offset, spot, length in order.runs(b * hb, hb):
                rows = [
                    conv_total[spot : spot + length, k * hidden : (k + 1) * hidden].astype(BF)
                    for k in range(taps)
                ]
                for f in range(fold):
                    at = (b * fold + f) * hb + offset
                    rows.append(total[at : at + length].astype(BF))
                for s, piece in enumerate(wire_from_rows(order, rows)):
                    pieces[distance(grid, place, s, b) + (pl.ds(offset, length),)] = piece
            if b >= grid.batch - 2:
                hand_out(place, b % 2, pieces, (part_a, part_b, part_c, part_d), out_sems)


def stage_two(
    grid, order, taps, place, tokens, cotangent, conv_input, left, right, part, error, table,
    conv_t, up_t,
):
    count, span, model = tokens.shape
    hidden = conv_input.shape[2]
    reach = left.shape[1]
    group = group_of(count)
    fold = model // hidden
    pieces = piece_shape(grid, order.hb, (taps + fold) * order.hl)
    return pl.pallas_call(
        functools.partial(stage_two_kernel, grid, order, taps),
        out_shape=(
            sds((count, span, model), BF),
            sds((count, span, hidden), BF),
            sds((count, reach, hidden), BF),
            sds((count, reach, hidden), BF),
            sds((TABLE_ROWS, model), F32),
            *[sds(pieces, BF)] * 4,
        ),
        grid_spec=pltpu.PrefetchScalarGridSpec(
            num_scalar_prefetch=1,
            grid=(count // group,),
            in_specs=[
                rows_of((group, span, model)),
                rows_of((group, span, model)),
                rows_of((group, span, hidden)),
                whole((count, reach, hidden)),
                whole((count, reach, hidden)),
                rows_of((group, span, hidden)),
                rows_of((group, span, hidden)),
                whole(table.shape),
                whole(conv_t.shape),
                whole(up_t.shape),
            ],
            out_specs=[
                rows_of((group, span, model)),
                rows_of((group, span, hidden)),
                rows_of((group, reach, hidden)),
                rows_of((group, reach, hidden)),
                whole((TABLE_ROWS, model)),
                *[pl.BlockSpec(memory_space=pl.ANY)] * 4,
            ],
            scratch_shapes=[
                pltpu.VMEM((group, span + 2 * reach, hidden), BF),
                pltpu.VMEM((group * span, hidden), BF),
                pltpu.VMEM((count, 2 * reach, hidden), F32),
                pltpu.VMEM((model, hidden), F32),
                pltpu.VMEM((hidden, taps * hidden), F32),
                pltpu.VMEM((2, 2) + pieces, BF),
                pltpu.SemaphoreType.DMA((4,)),
            ],
        ),
        compiler_params=params(LIM2),
        cost_estimate=cost(
            2 * count * span * hidden * (taps * hidden + 2 * model),
            count * span * (6 * model + 12 * hidden),
        ),
        name="stage_two",
    )(
        place, tokens, cotangent, conv_input, left, right, part, error, table, conv_t, up_t,
    )


def inner_back_kernel(conv_out_grad, conv_t, part, padded):
    group, span, hidden = conv_out_grad.shape
    taps = conv_t.shape[0]
    reach = (padded.shape[1] - span) // 2

    @pl.when(pl.program_id(0) == 0)
    def _():
        padded[:, 0:reach] = jnp.zeros((group, reach, hidden), BF)
        padded[:, reach + span : 2 * reach + span] = jnp.zeros((group, reach, hidden), BF)

    padded[:, reach : reach + span] = conv_out_grad[...]
    windows = join(tap_windows(padded, reversed(range(taps)), span))
    part[...] = dot_nn(windows, conv_t[...].reshape(taps * hidden, hidden)).reshape(
        group, span, hidden
    )


def inner_back(conv_out_grad, conv_t, reach):
    count, span, hidden = conv_out_grad.shape
    taps = conv_t.shape[0]
    group = group_of(count)
    return pl.pallas_call(
        inner_back_kernel,
        out_shape=sds((count, span, hidden), F32),
        grid=(count // group,),
        in_specs=[rows_of((group, span, hidden)), whole(conv_t.shape)],
        out_specs=rows_of((group, span, hidden)),
        scratch_shapes=[pltpu.VMEM((group, span + 2 * reach, hidden), BF)],
        compiler_params=params(LIM3P),
        cost_estimate=cost(2 * count * span * hidden * taps * hidden, count * span * 6 * hidden),
        name="inner_back",
    )(conv_out_grad, conv_t)


def stage_three_kernel(
    start_ref, length_ref, part, narrow, left, right, table, sums_in, conv_t,
    narrow_grad, sums, edges,
):
    group, span, hidden = narrow.shape
    count, reach = left.shape[0], left.shape[1]
    taps = conv_t.shape[0]
    step = pl.program_id(0)

    def vec(name, width):
        return table[ROW[name] : ROW[name] + 1, 0:width]

    def add(name, values, factor=1.0):
        width = values.shape[1]
        sums[ROW[name] : ROW[name] + 1, 0:width] += row_sum(values) * factor

    @pl.when(step == 0)
    def _():
        sums[...] = sums_in[...]
        before, behind = edge_windows(left[...], right[...], taps)
        for at, windows, first in ((0, before, 0), (reach, behind, taps // 2 + 1)):
            term = None
            for k, window in enumerate(windows):
                product = dot_nn(window, conv_t[taps - 1 - first - k])
                term = product if term is None else term + product
            edges[:, at : at + reach] = term.reshape(count, reach, hidden)

    back = add_edges(part[...], edges[pl.ds(step * group, group)])
    back = back * valid_rows(start_ref, length_ref, group, span)
    unit, inverse = normed(narrow[...].reshape(group * span, hidden))
    gain = vec("middle_gain", hidden)
    _, slope = gelu_both(scaled(unit, gain, vec("middle_shift", hidden)))
    twice = back * slope
    low, product = back_rows(twice, gain, unit, inverse)
    low = low.astype(BF)
    narrow_grad[...] = low.reshape(group, span, hidden)
    add("middle_gain", product, 0.5)
    add("middle_shift", twice, 0.5)
    add("down_bias", low.astype(F32))


def stage_three(start, lengths, part, narrow, left, right, table, sums, conv_t):
    count, span, hidden = narrow.shape
    reach = left.shape[1]
    group = group_of(count)
    return pl.pallas_call(
        stage_three_kernel,
        out_shape=(sds((count, span, hidden), BF), sds(sums.shape, F32)),
        grid_spec=pltpu.PrefetchScalarGridSpec(
            num_scalar_prefetch=2,
            grid=(count // group,),
            in_specs=[
                rows_of((group, span, hidden)),
                rows_of((group, span, hidden)),
                whole((count, reach, hidden)),
                whole((count, reach, hidden)),
                whole(table.shape),
                whole(table.shape),
                whole(conv_t.shape),
            ],
            out_specs=[rows_of((group, span, hidden)), whole(sums.shape)],
            scratch_shapes=[pltpu.VMEM((count, 2 * reach, hidden), F32)],
        ),
        compiler_params=params(LIM3),
        cost_estimate=cost(2 * count * span * hidden * hidden, count * span * 10 * hidden),
        name="stage_three",
    )(start, lengths, part, narrow, left, right, table, sums, conv_t)


def stage_four_kernel(
    grid, order, begin, last, place, tokens, cotangent, narrow_grad, table, sums_in, down_t, *refs
):
    if last:
        hidden_one, narrow_all, refs = refs[0], refs[1], refs[2:]
    if not begin:
        refs = refs[1:]
    tokens_grad, sums, refs = refs[0], refs[1], refs[2:]
    span, model = tokens.shape[1], tokens.shape[2]
    hidden = narrow_grad.shape[2]
    hb, dl = order.hb, model // grid.seq
    step = pl.program_id(0)

    def vec(name, width):
        return table[ROW[name] : ROW[name] + 1, 0:width]

    def add(name, values, factor=1.0):
        width = values.shape[1]
        sums[ROW[name] : ROW[name] + 1, 0:width] += row_sum(values) * factor

    @pl.when(step == 0)
    def _():
        sums[...] = sums_in[...]
        if last:
            refs[4][...] = jnp.zeros_like(refs[4])

    if last:
        *parts, total, pieces, out_sems = refs
        size = narrow_all.shape[0] * span
        total[...] += dot_tn(
            narrow_all[...].reshape(size, hidden), hidden_one[...].reshape(size, model)
        )
    deep = dot_nn(narrow_grad[0], down_t[...])
    unit, inverse = normed(tokens[0].astype(F32))
    gain = vec("first_gain", model)
    _, slope = gelu_both(scaled(unit, gain, vec("first_shift", model)))
    twice = deep * slope
    grad, product = back_rows(twice, gain, unit, inverse)
    add("first_gain", product, 0.5)
    add("first_shift", twice, 0.5)
    tokens_grad[0] = (grad + cotangent[0].astype(F32)).astype(BF)

    if last:

        @pl.when(step == pl.num_programs(0) - 1)
        def _():
            wide = model // grid.batch
            sub = lax.broadcasted_iota(jnp.int32, (TABLE_ROWS, dl), 0)
            for b in [*range(0, grid.batch, 2), *range(1, grid.batch, 2)]:
                upper = sums[:, b * wide : (b + 1) * wide]
                runs = order.runs(b * hb, hb)
                lower = join([sums[:, spot : spot + length] for _, spot, length in runs])
                if wide < dl:
                    upper = join([upper, jnp.zeros((TABLE_ROWS, dl - wide), F32)])
                lower = join([lower, jnp.zeros((TABLE_ROWS, dl - hb), F32)])
                tail = jnp.where(sub < WIDE_ROWS, upper, lower).astype(BF)
                for s in range(grid.seq):
                    to = distance(grid, place, s, b)
                    for offset, spot, length in runs:
                        pieces[to + (pl.ds(offset, length),)] = total[
                            spot : spot + length, s * dl : (s + 1) * dl
                        ].astype(BF)
                    pieces[to + (pl.ds(hb, 16),)] = tail
                if b >= grid.batch - 2:
                    hand_out(place, b % 2, pieces, parts, out_sems)


def stage_four(
    grid, order, first, part, begin, last, place, tokens, cotangent, hidden_one, narrow_grad,
    table, sums, down_t, grad_in,
):
    count, span, model = tokens.shape
    hidden = narrow_grad.shape[2]
    pieces = piece_shape(grid, order.hb + 16, model // grid.seq)

    def part_of(block):
        return pl.BlockSpec(block, lambda i, *_: (first + i,) + (0,) * (len(block) - 1))

    in_specs = [
        part_of((1, span, model)),
        part_of((1, span, model)),
        part_of((1, span, hidden)),
        whole(table.shape),
        whole(table.shape),
        whole(down_t.shape),
    ]
    inputs = [tokens, cotangent, narrow_grad, table, sums, down_t]
    out_shape = [sds((count, span, model), BF), sds(table.shape, F32)]
    out_specs = [part_of((1, span, model)), whole(table.shape)]
    scratch = []
    if last:
        share = count // part
        in_specs += [rows_of((share, span, model)), rows_of((share, span, hidden))]
        inputs += [hidden_one, narrow_grad]
        out_shape += [sds(pieces, BF)] * 4
        out_specs += [pl.BlockSpec(memory_space=pl.ANY)] * 4
        scratch = [
            pltpu.VMEM((hidden, model), F32),
            pltpu.VMEM((2, 2) + pieces, BF),
            pltpu.SemaphoreType.DMA((4,)),
        ]
    aliases = {}
    if not begin:
        in_specs.append(pl.BlockSpec(memory_space=pl.ANY))
        inputs.append(grad_in)
        aliases = {len(inputs): 0}
    return pl.pallas_call(
        functools.partial(stage_four_kernel, grid, order, begin, last),
        out_shape=tuple(out_shape),
        grid_spec=pltpu.PrefetchScalarGridSpec(
            num_scalar_prefetch=1,
            grid=(part,),
            in_specs=in_specs,
            out_specs=out_specs,
            scratch_shapes=scratch,
        ),
        input_output_aliases=aliases,
        compiler_params=params(LIM4),
        cost_estimate=cost(
            4 * part * span * hidden * model, part * span * (8 * model + 2 * hidden)
        ),
        name="stage_four",
    )(place, *inputs)


def halos(head, foot):
    count = lax.axis_size("seq")
    left = lax.ppermute(foot, "seq", [(i, i + 1) for i in range(count - 1)])
    right = lax.ppermute(head, "seq", [(i + 1, i) for i in range(count - 1)])
    return left, right


def after(value, *others):
    return lax.optimization_barrier((value,) + others)[0]


def body(
    grid,
    tokens,
    lengths,
    first_gain,
    first_shift,
    down_weight,
    down_bias,
    middle_gain,
    middle_shift,
    conv_weight,
    conv_bias,
    final_gain,
    final_shift,
    up_weight,
    up_bias,
    cotangent,
):
    shape = tokens.shape
    span, model = shape[2], shape[3]
    count = shape[0] * shape[1]
    taps = conv_weight.shape[0]
    hidden = down_weight.shape[1] * grid.batch
    order = Order(grid, hidden)
    hb, hl, dl = order.hb, order.hl, down_weight.shape[0]
    fold = model // hidden
    reach = (taps - 1) // 2 * DILATION

    tokens = tokens.reshape(count, span, model)
    cotangent = cotangent.reshape(count, span, model)
    lengths = lengths.reshape(count)
    place = jnp.stack(grid.here()).astype(jnp.int32)
    start = (lax.axis_index("seq") * span).astype(jnp.int32).reshape(1)

    vectors = {
        "first_gain": first_gain,
        "first_shift": first_shift,
        "up_bias": up_bias,
        "down_bias": down_bias,
        "middle_gain": middle_gain,
        "middle_shift": middle_shift,
        "conv_bias": conv_bias,
        "final_gain": final_gain,
        "final_shift": final_shift,
    }
    first_piece = pack_first(order, down_weight.T, [vectors[name] for name in WIDE + NARROW])
    second_piece = pack_second(order, after(conv_weight, first_piece), up_weight)

    def meet(*groups):
        flat = lax.optimization_barrier(tuple(value for group in groups for value in group))
        found, at = [], 0
        for group in groups:
            found.append(flat[at : at + len(group)])
            at += len(group)
        return found

    first = grid.gather_deep(first_piece)
    (first[1], second_piece), (place, start, lengths) = meet(
        (first[1], second_piece), (place, start, lengths)
    )
    second = grid.halves(grid.gather_deep(second_piece))
    one, two = grid.gather_near(*grid.halves(first))
    far_one, far_two = grid.gather_far(one, two)
    first = [one, *far_one, two, *far_two]
    first, second = meet(first, second)
    first = [*first, *grid.gather_core(first)]
    near = grid.gather_near(*second)
    near, first = meet(near, first)
    near_other = grid.gather_core(near)
    far_one, far_two = grid.gather_far(*near)
    hidden_one, narrow, conv_input, head, foot, down_t, table = stage_one(
        grid, order, reach, place, start, lengths, tokens, first
    )
    far_one, far_two, near_other, (head, foot) = meet(
        far_one, far_two, near_other, (head, foot)
    )
    left, right = halos(head, foot)
    far_one_other, far_two_other = grid.gather_core(far_one), grid.gather_core(far_two)
    second = [near[0], *far_one, near[1], *far_two]
    second += [near_other[0], *far_one_other, near_other[1], *far_two_other]
    part, error, conv_t, up_t = inner(
        grid, order, taps, reach, place, cotangent, conv_input, second
    )
    block_output, conv_out_grad, head, foot, sums, *rest = stage_two(
        grid, order, taps, place, tokens, cotangent, conv_input, left, right, part, error, table,
        conv_t, up_t,
    )

    left, right = halos(head, foot)
    rest = grid.reduce_core(*rest)
    part = inner_back(conv_out_grad, conv_t, reach)
    rest, (sums, left, right, part) = meet(rest, (sums, left, right, part))

    rest = grid.reduce_far(*rest)
    narrow_grad, sums = stage_three(
        start, lengths, part, narrow, left, right, table, sums, conv_t
    )
    half = count // 2
    tokens_grad, sums = stage_four(
        grid, order, 0, half, True, False, place, tokens, cotangent, hidden_one, narrow_grad,
        table, sums, down_t, None,
    )
    rest, (sums,) = meet(rest, (sums,))

    rest = grid.reduce_near(*rest)
    tokens_grad, sums, *down = stage_four(
        grid, order, half, half, False, True, place, tokens, cotangent, hidden_one, narrow_grad,
        table, sums, down_t, tokens_grad,
    )
    rest, down = meet(rest, down)

    down = grid.reduce_core(*down)
    down, rest = meet(down, rest)
    down = grid.reduce_far(*down)
    rest = grid.reduce_deep(*rest)
    down = grid.reduce_near(*down)
    down = grid.reduce_deep(*down)
    conv_grad, up_grad = unpack_rest(order, taps, fold, rest)
    names = WIDE + NARROW
    down_grad, *found = unpack_first(order, down, [vectors[name].shape[0] for name in names])
    grads = dict(zip(names, found))
    return (
        block_output.reshape(shape),
        tokens_grad.reshape(shape),
        grads["first_gain"],
        grads["first_shift"],
        down_grad.T,
        grads["down_bias"],
        grads["middle_gain"],
        grads["middle_shift"],
        conv_grad,
        grads["conv_bias"],
        grads["final_gain"],
        grads["final_shift"],
        up_grad,
        grads["up_bias"],
    )


def solution(mesh):
    grid = Grid(mesh.shape["seq"], mesh.shape["batch"])
    return jax.shard_map(
        functools.partial(body, grid),
        mesh=mesh,
        in_specs=(
            P(None, "batch", "seq", None),
            P(None, "batch"),
            P("batch"),
            P("batch"),
            P("seq", "batch"),
            P("batch"),
            P("batch"),
            P("batch"),
            P(None, "seq", "batch"),
            P("batch"),
            P("batch"),
            P("batch"),
            P("seq", "batch"),
            P("batch"),
            P(None, "batch", "seq", None),
        ),
        out_specs=(
            P(None, "batch", "seq", None),
            P(None, "batch", "seq", None),
            P("batch"),
            P("batch"),
            P("seq", "batch"),
            P("batch"),
            P("batch"),
            P("batch"),
            P(None, "seq", "batch"),
            P("batch"),
            P("batch"),
            P("batch"),
            P("seq", "batch"),
            P("batch"),
        ),
        check_vma=False,
    )
```
